256 devices in a mesh: blk: 32 (over z, y_hi, core), cset: 8 (over y_lo, x).
Axes of the slice: x: 4, y: 4 (y_hi: 2, y_lo: 2; y = y_hi * 2 + y_lo), z: 8, core: 2. Of those that a mesh axis runs over, the one named last changes fastest.
Arguments:
- active_table: bfloat16 [65536, 256], P(('blk', 'cset')), may hold values from 0.019897461 to 0.19921875
- passive_table: bfloat16 [65536, 256], P(('blk', 'cset')), may hold values from 0 to 0.15
- adjacency: bfloat16 [32, 8, 9, 8, 128, 128], P('blk', 'cset'), may hold values from 0 to 1, as said below
- tile_dst: int32 [32, 8, 9, 8], P('blk', 'cset'), may hold values from 0 to 1
- tile_src: int32 [32, 8, 9, 8], P('blk', 'cset'), may hold values from 0 to 15
- tile_count: int32 [32, 8, 9], P('blk', 'cset'), may hold values from 1 to 8, as said below
- split_active: int32 [20, 924], replicated, may hold values from 0 to 219, as said below
- split_passive: int32 [20, 924], replicated, may hold values from 0 to 219, as said below
Outputs:
- joined_table: bfloat16 [65536, 1024], P('blk', 'cset')
The draws below stay inside these ranges and needn't reach their ends.
Inputs may be any that keep to these rules, and one draw needn't show every extreme that they name: For each six-color set s, the 20 pairs (split_active[j, s], split_passive[j, s]) name its 20 divisions into an ordered pair of three-color sets, each once, as columns of the two child tables; a child table's columns hold its 220 color sets in some fixed order, and columns 220 and above are never named. `split_passive`: see split_active; each table is a column order of its own. `tile_count`: the own partition's slot r = 4 is full on every device. `adjacency`: edge weights are 0 or 1.
All inputs are finite; a program needn't handle non-finite values.
Results may differ from the reference program's by a relative error of at most 0.0026.
Values may be sent and summed in bfloat16 or wider, within the bound.
No kernel may reach another device: no remote copies, remote signals or barrier semaphores. Data moves between devices by JAX's collectives and lax.ppermute only.
A program may use at most 64 MiB of HBM per device.

```python
import math
import jax
import jax.numpy as jnp
import numpy as np
from jax import lax

K = 12
CHILD = 220
OUT = 924
CPAD = 256
OUTPAD = 1024
TILE = 128
TPP = 8
RDEV = 256
REACH_HALF = 4
REACH = 9
PR = 2048
V = 65536
N_BLK = 32
N_CSET = 8


def count_members(candidate):
    total = 0
    for position in range(K):
        total = total + (candidate >> position & 1)
    return total


def subset_tables():

    def subsets_of(members):
        return [candidate for candidate in range(1 << K) if count_members(candidate) == members]
    smaller = subsets_of(3)
    ranking = {}
    for position, candidate in enumerate(smaller):
        ranking[candidate] = position
    leading = []
    trailing = []
    for parent in subsets_of(6):
        inside = [candidate for candidate in smaller if candidate & parent == candidate]
        leading.append([ranking[candidate] for candidate in inside])
        trailing.append([ranking[parent ^ candidate] for candidate in inside])
    return (np.array(leading, dtype=np.int32).T, np.array(trailing, dtype=np.int32).T)


def row_counts(key, low, high, factor_low, factor_high):
    key_scale, key_factor, key_keep = jax.random.split(key, 3)
    exponent = jax.random.uniform(key_scale, (V, 1), jnp.float32, math.log(low), math.log(high))
    factor = jax.random.uniform(key_factor, (V, CPAD), jnp.float32, factor_low, factor_high)
    keep = jax.random.bernoulli(key_keep, 0.5, (V, CPAD)).astype(jnp.float32)
    return jnp.exp(exponent) * factor * keep


def draw_passive_table(key, part):
    key = jax.random.fold_in(key, 5)
    values = row_counts(key, 0.0001, 0.1, 0.5, 1.5)
    return values.astype(jnp.bfloat16)


def draw_adjacency(key, part):
    key = jax.random.fold_in(key, 1)
    key_density, key_edges = jax.random.split(key)
    shape = (N_BLK, N_CSET, REACH, TPP, TILE, TILE)
    level = jax.random.uniform(key_density, (N_BLK, N_CSET, REACH, TPP, 1, 1), jnp.float32, math.log(0.01), math.log(0.3))
    density = jnp.exp(level)
    edges = jax.random.bernoulli(key_edges, density, shape)
    return edges.astype(jnp.float32).astype(jnp.bfloat16)


def draw_tile_count(key, part):
    key = jax.random.fold_in(key, 2)
    counts = jax.random.randint(key, (N_BLK, N_CSET, REACH), 1, TPP + 1, dtype=jnp.int32)
    return counts.at[:, :, REACH_HALF].set(TPP)


def draw_split_active(key, part):
    key = jax.random.fold_in(key, 3)
    leading, trailing = subset_tables()
    order = jax.random.permutation(key, CHILD).astype(jnp.int32)
    return order[jnp.asarray(leading)]


def draw_split_passive(key, part):
    key = jax.random.fold_in(key, 4)
    leading, trailing = subset_tables()
    order = jax.random.permutation(key, CHILD).astype(jnp.int32)
    return order[jnp.asarray(trailing)]


def touch_ends(result, own_key, least, high):
    spot = [jax.random.randint(jax.random.fold_in(own_key, axis), (), 0, length) for axis, length in enumerate(result.shape)]
    main_axis = result.shape.index(max(result.shape))
    next_to = spot[:main_axis] + [(spot[main_axis] + 1) % result.shape[main_axis]] + spot[main_axis + 1:]
    return result.at[tuple(spot)].set(least).at[tuple(next_to)].set(high)


def block_levels(rng, extent, shards, smallest, high):
    loudness = 1.0
    for dim, blocks in shards:
        draws = jax.random.uniform(jax.random.fold_in(jax.random.fold_in(rng, 6), dim), (blocks,), jnp.float32, smallest / len(shards), high / len(shards))
        loudness = loudness * jnp.repeat(jnp.exp(draws), extent[dim] // blocks).reshape((-1,) + (1,) * (len(extent) - 1 - dim))
    return loudness


def setup_inputs(seed: int = 0) -> dict:
    keys = jax.random.split(jax.random.key(seed), 9)
    return {
        "active_table": jnp.clip(jnp.exp(math.log(0.19921875) - 2.3038113 * jax.random.uniform(keys[0], (V, CPAD), jnp.float32) ** block_levels(keys[0], (V, CPAD), ((0, 256),), -0.2, 0.2)), 0.019897461, 0.19921875).astype(jnp.bfloat16),
        "passive_table": draw_passive_table(jax.random.fold_in(keys[8], 71), 0),
        "adjacency": draw_adjacency(jax.random.fold_in(keys[8], 71), 0),
        "tile_dst": touch_ends(jax.random.randint(keys[3], (N_BLK, N_CSET, REACH, TPP), 0, RDEV // TILE), jax.random.fold_in(keys[3], 1), 0, (RDEV // TILE) - 1).astype(jnp.int32),
        "tile_src": touch_ends(jax.random.randint(keys[4], (N_BLK, N_CSET, REACH, TPP), 0, RDEV * N_CSET // TILE), jax.random.fold_in(keys[4], 1), 0, (RDEV * N_CSET // TILE) - 1).astype(jnp.int32),
        "tile_count": draw_tile_count(jax.random.fold_in(keys[8], 71), 0),
        "split_active": draw_split_active(jax.random.fold_in(keys[8], 71), 0),
        "split_passive": draw_split_passive(jax.random.fold_in(keys[8], 71), 0),
    }


def reference(active_table, passive_table, adjacency, tile_dst, tile_src, tile_count, split_active, split_passive):
    device_count = N_BLK * N_CSET
    source_blocks = passive_table.reshape(N_BLK, PR // TILE, TILE, CPAD)
    tiles_flat = adjacency.reshape(device_count, REACH, TPP, TILE, TILE)
    dst_flat = tile_dst.reshape(device_count, REACH, TPP)
    src_flat = tile_src.reshape(device_count, REACH, TPP)
    count_flat = tile_count.reshape(device_count, REACH)
    slot_ids = jnp.arange(TPP, dtype=jnp.int32)
    reach_ids = jnp.arange(REACH, dtype=jnp.int32)
    row_tiles = jnp.arange(RDEV // TILE, dtype=jnp.int32)

    def one_device(device):
        block_index = device // N_CSET
        partitions = (block_index + reach_ids - REACH_HALF) % N_BLK
        chosen = source_blocks[partitions[:, None], src_flat[device]].astype(jnp.float32)
        live = (slot_ids[None, :] < count_flat[device][:, None]).astype(jnp.float32)
        weights = tiles_flat[device].astype(jnp.float32) * live[:, :, None, None]
        product = jnp.einsum('rtij,rtjc->rtic', weights, chosen, precision=lax.Precision.HIGHEST)
        placing = (dst_flat[device][:, :, None] == row_tiles[None, None, :]).astype(jnp.float32)
        summed = jnp.einsum('rtd,rtic->dic', placing, product, precision=lax.Precision.HIGHEST)
        return summed.reshape(RDEV, CPAD)

    neighbour = lax.map(one_device, jnp.arange(device_count, dtype=jnp.int32))
    neighbour = neighbour.reshape(V, CPAD).astype(jnp.bfloat16)

    def one_partition(index):
        start = index * PR
        left = lax.dynamic_slice_in_dim(active_table, start, PR, 0)
        right = lax.dynamic_slice_in_dim(neighbour, start, PR, 0)
        picked_left = jnp.take(left, split_active, axis=1).astype(jnp.float32)
        picked_right = jnp.take(right, split_passive, axis=1).astype(jnp.float32)
        joined = jnp.sum(picked_left * picked_right, axis=1).astype(jnp.bfloat16)
        return jnp.pad(joined, ((0, 0), (0, OUTPAD - OUT)))

    joined_table = lax.map(one_partition, jnp.arange(N_BLK, dtype=jnp.int32))
    return joined_table.reshape(V, OUTPAD)
```

```python
import jax
import jax.numpy as jnp
from jax import lax
from jax.experimental import pallas as pl
from jax.experimental.pallas import tpu as pltpu
from jax.sharding import PartitionSpec as P

SPLITS = 20
OUTPAD = 1024
TILE = 128
CHUNK = 256
VMEM_LIMIT = 40 * 1024 * 1024


def routed(block, chips, flip):
    nb, nc = lax.axis_size("blk"), lax.axis_size("cset")
    route = []
    for b in range(nb):
        for c in range(nc):
            target = c ^ (nc // 2) if flip else c
            route.append((b * nc + c, ((b + 2 * chips) % nb) * nc + target))
    return lax.ppermute(block, ("blk", "cset"), route)


def across_cset(block, step):
    nc = lax.axis_size("cset")
    return lax.ppermute(block, "cset", [(c, c ^ step) for c in range(nc)])


def across_cores(block):
    nb = lax.axis_size("blk")
    return lax.ppermute(block, "blk", [(b, b ^ 1) for b in range(nb)])


def pick_kernel(cols_ref, table_ref, out_ref):
    width = cols_ref.shape[2]
    channel = lax.broadcasted_iota(jnp.int32, (table_ref.shape[1], width), 0)
    onehot = (channel == cols_ref[0]).astype(jnp.bfloat16)
    out_ref[0] = jnp.dot(
        table_ref[...], onehot, preferred_element_type=jnp.float32
    ).astype(jnp.bfloat16)


def pick_columns(table, cols):
    rows, channels = table.shape
    splits, _, width = cols.shape
    return pl.pallas_call(
        pick_kernel,
        grid=(splits,),
        in_specs=[
            pl.BlockSpec((1, 1, width), lambda j: (j, 0, 0)),
            pl.BlockSpec((rows, channels), lambda j: (0, 0)),
        ],
        out_specs=pl.BlockSpec((1, rows, width), lambda j: (j, 0, 0)),
        out_shape=jax.ShapeDtypeStruct((splits, rows, width), jnp.bfloat16),
        compiler_params=pltpu.CompilerParams(vmem_limit_bytes=VMEM_LIMIT),
        cost_estimate=pl.CostEstimate(
            flops=2 * splits * rows * channels * width,
            bytes_accessed=2 * splits * rows * width,
            transcendentals=0,
        ),
        name="pick_active",
    )(cols, table)


def sum_kernel(place_ref, tiles_ref, sources_ref, out_ref, wide, gathered, sems):
    slots = tiles_ref.shape[0]
    copies = []
    for t in range(slots):
        copy = pltpu.make_async_copy(
            sources_ref.at[place_ref[0, t]], gathered.at[t], sems.at[t]
        )
        copy.start()
        copies.append(copy)
    wide[0 : 2 * TILE] = jnp.zeros((2 * TILE, slots * TILE), jnp.bfloat16)
    for t in range(slots):
        row = pl.multiple_of(place_ref[1, t] * TILE, TILE)
        wide[pl.ds(row, TILE), t * TILE : (t + 1) * TILE] = tiles_ref[t]
    for copy in copies:
        copy.wait()
    out_ref[...] = jnp.dot(
        wide[0 : 2 * TILE],
        gathered[...].reshape(slots * TILE, gathered.shape[2]),
        preferred_element_type=jnp.float32,
    ).astype(out_ref.dtype)


def sum_tiles(place, tiles, sources, dtype, name):
    slots = tiles.shape[0]
    channels = sources.shape[2]
    return pl.pallas_call(
        sum_kernel,
        in_specs=[
            pl.BlockSpec(memory_space=pltpu.SMEM),
            pl.BlockSpec(memory_space=pltpu.VMEM),
            pl.BlockSpec(memory_space=pl.ANY),
        ],
        out_specs=pl.BlockSpec(memory_space=pltpu.VMEM),
        out_shape=jax.ShapeDtypeStruct((2 * TILE, channels), dtype),
        scratch_shapes=[
            pltpu.VMEM((3 * TILE, slots * TILE), jnp.bfloat16),
            pltpu.VMEM((slots, TILE, channels), jnp.bfloat16),
            pltpu.SemaphoreType.DMA((slots,)),
        ],
        compiler_params=pltpu.CompilerParams(vmem_limit_bytes=VMEM_LIMIT),
        cost_estimate=pl.CostEstimate(
            flops=4 * TILE * TILE * slots * channels,
            bytes_accessed=2 * slots * TILE * (TILE + channels),
            transcendentals=0,
        ),
        name=name,
    )(place, tiles, sources)


def join_kernel(cols_ref, own_ref, n0, n1, n2, n3, picked_ref, out_ref):
    total = own_ref[...]
    for part in (n0, n1, n2, n3):
        total = total + part[...].astype(jnp.float32)
    neighbour = total.astype(jnp.bfloat16)
    width = picked_ref.shape[2]
    channel = lax.broadcasted_iota(jnp.int32, (neighbour.shape[1], width), 0)
    joined = jnp.zeros((neighbour.shape[0], width), jnp.float32)
    for j in range(SPLITS):
        onehot = (channel == cols_ref[j]).astype(jnp.bfloat16)
        joined = joined + picked_ref[j].astype(jnp.float32) * jnp.dot(
            neighbour, onehot, preferred_element_type=jnp.float32
        )
    for piece in range(width // TILE):
        out_ref[piece] = joined[:, piece * TILE : (piece + 1) * TILE].astype(out_ref.dtype)


def join(own, parts, picked, cols):
    rows, channels = own.shape
    splits, _, width = cols.shape
    whole = pl.BlockSpec((rows, channels), lambda q: (0, 0))
    return pl.pallas_call(
        join_kernel,
        grid=(width // CHUNK,),
        in_specs=[pl.BlockSpec((splits, 1, CHUNK), lambda q: (0, 0, q))]
        + [whole] * 5
        + [pl.BlockSpec((splits, rows, CHUNK), lambda q: (0, 0, q))],
        out_specs=pl.BlockSpec((CHUNK // TILE, rows, TILE), lambda q: (q, 0, 0)),
        out_shape=jax.ShapeDtypeStruct((width // TILE, rows, TILE), jnp.bfloat16),
        compiler_params=pltpu.CompilerParams(vmem_limit_bytes=VMEM_LIMIT),
        cost_estimate=pl.CostEstimate(
            flops=2 * splits * rows * channels * width,
            bytes_accessed=2 * splits * rows * width,
            transcendentals=0,
        ),
        name="join_sets",
    )(cols, own, *parts, picked)


def local(
    active_table,
    passive_table,
    adjacency,
    tile_dst,
    tile_src,
    tile_count,
    split_active,
    split_passive,
):
    tiles_all = adjacency[0, 0]
    dst_all, src_all, count_all = tile_dst[0, 0], tile_src[0, 0], tile_count[0, 0]
    reach, slots = dst_all.shape
    nc = lax.axis_size("cset")
    me = lax.axis_index("cset")
    core = lax.axis_index("blk") % 2

    slot_of = jnp.arange(slots, dtype=jnp.int32)[None, :]
    relative = jnp.arange(reach, dtype=jnp.int32) - reach // 2 + core
    parity = relative % 2
    group = relative // 2 + 2
    landing = jnp.where(group % 2 == 1, me ^ (nc // 2), me)
    held = (
        (parity != core).astype(jnp.int32)[:, None] * (2 * nc)
        + ((src_all // 2) ^ landing[:, None]) * 2
        + src_all % 2
    )
    row = jnp.where(slot_of < count_all[:, None], dst_all, 2)

    def pair(which):
        if which == 0:
            start = 0
        elif which == 4:
            start = reach - 2
        else:
            start = 2 * which - core
        rows = lax.dynamic_slice_in_dim(row, start, 2, 0)
        mine = lax.dynamic_slice_in_dim(group, start, 2, 0) == which
        rows = jnp.where(mine[:, None], rows, 2).reshape(-1)
        places = lax.dynamic_slice_in_dim(held, start, 2, 0).reshape(-1)
        tiles = lax.dynamic_slice_in_dim(tiles_all, start, 2, 0)
        return jnp.stack([places, rows]), tiles.reshape(2 * slots, TILE, TILE)

    own_place, own_tiles = pair(2)
    away = []
    for which in (1, 3, 0, 4):
        place, tiles = pair(which)
        chips, flip = which - 2, which % 2 == 1
        away.append((chips, flip, routed(place, chips, flip), routed(tiles, chips, flip)))

    held_rows = jnp.concatenate(
        [passive_table] + [across_cset(passive_table, step) for step in range(1, nc)], axis=0
    )
    both = jnp.concatenate([held_rows, across_cores(held_rows)], axis=0)
    sources = both.reshape(-1, TILE, both.shape[1])

    extra = OUTPAD - split_active.shape[1]
    left_cols = jnp.pad(split_active, ((0, 0), (0, extra)), constant_values=-1)[:, None, :]
    right_cols = jnp.pad(split_passive, ((0, 0), (0, extra)), constant_values=-1)[:, None, :]
    picked = pick_columns(active_table, left_cols)

    parts = []
    for chips, flip, place, tiles in away:
        part = sum_tiles(place, tiles, sources, jnp.bfloat16, "sum_for_others")
        parts.append(routed(part, -chips, flip))
    own = sum_tiles(own_place, own_tiles, sources, jnp.float32, "sum_own")
    joined = join(own, parts, picked, right_cols)
    spread = lax.all_to_all(joined, "cset", split_axis=0, concat_axis=0, tiled=True)
    return spread.reshape(-1, TILE)


def solution(mesh):
    in_specs = (
        P(("blk", "cset"), None),
        P(("blk", "cset"), None),
        P("blk", "cset", None, None, None, None),
        P("blk", "cset", None, None),
        P("blk", "cset", None, None),
        P("blk", "cset", None),
        P(),
        P(),
    )
    out_specs = P("blk", "cset")
    return jax.shard_map(local, mesh=mesh, in_specs=in_specs, out_specs=out_specs, check_vma=False)
```

```python
import jax
import jax.numpy as jnp
from jax import lax
from jax.experimental import pallas as pl
from jax.experimental.pallas import tpu as pltpu
from jax.sharding import PartitionSpec as P

SPLITS = 20
OUTPAD = 1024
TILE = 128
CHUNK = 256
SLOTS = 8
PAIR = 2 * SLOTS
TAIL = 16
AWAY = (1, 3, 0, 4)
VMEM_LIMIT = 16 * 1024 * 1024


def routed(block, chips, flip):
    nb, nc = lax.axis_size("blk"), lax.axis_size("cset")
    route = []
    for b in range(nb):
        for c in range(nc):
            target = c ^ (nc // 2) if flip else c
            route.append((b * nc + c, ((b + 2 * chips) % nb) * nc + target))
    return lax.ppermute(block, ("blk", "cset"), route)


def places(which, at_ref, dst_ref, src_ref, count_ref):
    core = at_ref[0]
    reach = 9
    nc = 8
    first = 2 * which - core
    start = jnp.clip(first, 0, reach - 2)
    held, rows = [], []
    for half in range(2):
        slot = start + half
        parity = slot - first
        for t in range(SLOTS):
            source = src_ref[slot, t]
            inside = jnp.logical_and(parity >= 0, parity < 2)
            held.append(source + jnp.where(parity == 1, 2 * nc, 0))
            live = jnp.logical_and(inside, t < count_ref[slot])
            rows.append(jnp.where(live, dst_ref[slot, t], 2))
    return start, held, rows


def pack_kernel(at_ref, dst_ref, src_ref, count_ref, tiles_ref, *rest):
    outs, tails, sems = rest[: len(AWAY)], rest[-2], rest[-1]
    copies = []
    lane = lax.broadcasted_iota(jnp.int32, (TAIL, TILE), 1)
    line = lax.broadcasted_iota(jnp.int32, (TAIL, TILE), 0)
    for n, which in enumerate(AWAY):
        start, held, rows = places(which, at_ref, dst_ref, src_ref, count_ref)
        begin = pl.multiple_of(start * (SLOTS * TILE), SLOTS * TILE)
        copy = pltpu.make_async_copy(
            tiles_ref.at[pl.ds(begin, PAIR * TILE)], outs[n].at[pl.ds(0, PAIR * TILE)], sems.at[2 * n]
        )
        copy.start()
        copies.append(copy)
        tail = jnp.zeros((TAIL, TILE), jnp.int32)
        for t in range(PAIR):
            tail = jnp.where(lane == t, jnp.where(line == 0, held[t], rows[t]), tail)
        tails[n] = tail.astype(jnp.float32).astype(jnp.bfloat16)
        copy = pltpu.make_async_copy(
            tails.at[n], outs[n].at[pl.ds(PAIR * TILE, TAIL)], sems.at[2 * n + 1]
        )
        copy.start()
        copies.append(copy)
    for copy in copies:
        copy.wait()


SMEM = pl.BlockSpec(memory_space=pltpu.SMEM)
VMEM = pl.BlockSpec(memory_space=pltpu.VMEM)
ANY = pl.BlockSpec(memory_space=pl.ANY)
HBM = pl.BlockSpec(memory_space=pltpu.HBM)


def pack_tiles(at, dst, src, count, tiles):
    return pl.pallas_call(
        pack_kernel,
        in_specs=[SMEM, SMEM, SMEM, SMEM, HBM],
        out_specs=[ANY] * len(AWAY),
        out_shape=[jax.ShapeDtypeStruct((PAIR * TILE + TAIL, TILE), jnp.bfloat16)] * len(AWAY),
        scratch_shapes=[
            pltpu.VMEM((len(AWAY), TAIL, TILE), jnp.bfloat16),
            pltpu.SemaphoreType.DMA((2 * len(AWAY),)),
        ],
        compiler_params=pltpu.CompilerParams(vmem_limit_bytes=VMEM_LIMIT),
        name="pack_tiles",
    )(at, dst, src, count, tiles)


def pick_kernel(cols_ref, table_ref, out_ref):
    width = cols_ref.shape[2]
    channel = lax.broadcasted_iota(jnp.int32, (table_ref.shape[1], width), 0)
    onehot = (channel == cols_ref[0]).astype(jnp.bfloat16)
    out_ref[0] = jnp.dot(
        table_ref[...], onehot, preferred_element_type=jnp.float32
    ).astype(jnp.bfloat16)


def pick_columns(table, cols):
    rows, channels = table.shape
    splits, _, width = cols.shape
    return pl.pallas_call(
        pick_kernel,
        grid=(splits,),
        in_specs=[
            pl.BlockSpec((1, 1, width), lambda j: (j, 0, 0)),
            pl.BlockSpec((rows, channels), lambda j: (0, 0)),
        ],
        out_specs=pl.BlockSpec((1, rows, width), lambda j: (j, 0, 0)),
        out_shape=jax.ShapeDtypeStruct((splits, rows, width), jnp.bfloat16),
        compiler_params=pltpu.CompilerParams(vmem_limit_bytes=VMEM_LIMIT),
        cost_estimate=pl.CostEstimate(
            flops=2 * splits * rows * channels * width,
            bytes_accessed=2 * splits * rows * width,
            transcendentals=0,
        ),
        name="pick_active",
    )(cols, table)


def products(held, rows, tiles, sources, wide):
    wide[0 : 2 * TILE] = jnp.zeros((2 * TILE, PAIR * TILE), jnp.bfloat16)
    for t in range(PAIR):
        row = pl.multiple_of(rows[t] * TILE, TILE)
        wide[pl.ds(row, TILE), t * TILE : (t + 1) * TILE] = tiles[t * TILE : (t + 1) * TILE]
    total = None
    for t in range(0, PAIR, 2):
        chosen = jnp.concatenate(
            [sources[pl.ds(pl.multiple_of(held[n] * TILE, TILE), TILE)] for n in (t, t + 1)], axis=0
        )
        product = jnp.dot(
            wide[0 : 2 * TILE, t * TILE : (t + 2) * TILE], chosen, preferred_element_type=jnp.float32
        )
        total = product if total is None else total + product
    return total


def sum_away_kernel(held_ref, *rest):
    count = len(AWAY)
    tiles_refs, outs = rest[:count], rest[count : 2 * count]
    sources, tiles, wide, tail, tail_s, sems = rest[2 * count :]
    heads = []
    for n in range(count):
        heads.append(pltpu.make_async_copy(tiles_refs[n], tiles.at[n], sems.at[n]))
    heads.append(pltpu.make_async_copy(held_ref, sources, sems.at[count]))
    for copy in heads:
        copy.start()
    for copy in heads:
        copy.wait()
    for n in range(count):
        tail[n] = tiles[n, PAIR * TILE : PAIR * TILE + TAIL].astype(jnp.float32).astype(jnp.int32)
    copy = pltpu.make_async_copy(tail, tail_s, sems.at[count + 1])
    copy.start()
    copy.wait()
    for n in range(count):
        held = [tail_s[n, 0, t] for t in range(PAIR)]
        placed = [tail_s[n, 1, t] for t in range(PAIR)]
        total = products(held, placed, tiles.at[n], sources, wide.at[n % 2])
        outs[n][...] = total.astype(jnp.bfloat16)


def sum_away(sources, messages):
    rows, channels = sources.shape
    count = len(messages)
    return pl.pallas_call(
        sum_away_kernel,
        in_specs=[ANY] * (1 + count),
        out_specs=[VMEM] * count,
        out_shape=[jax.ShapeDtypeStruct((2 * TILE, channels), jnp.bfloat16)] * count,
        scratch_shapes=[
            pltpu.VMEM((rows, channels), jnp.bfloat16),
            pltpu.VMEM((count,) + messages[0].shape, jnp.bfloat16),
            pltpu.VMEM((2, 3 * TILE, PAIR * TILE), jnp.bfloat16),
            pltpu.VMEM((count, TAIL, TILE), jnp.int32),
            pltpu.SMEM((count, TAIL, TILE), jnp.int32),
            pltpu.SemaphoreType.DMA((count + 2,)),
        ],
        compiler_params=pltpu.CompilerParams(vmem_limit_bytes=VMEM_LIMIT),
        cost_estimate=pl.CostEstimate(
            flops=count * 4 * TILE * TILE * PAIR * channels,
            bytes_accessed=2 * (rows * channels + count * PAIR * TILE * TILE),
            transcendentals=0,
        ),
        name="sum_away",
    )(sources, *messages)


def sum_own_kernel(at_ref, dst_ref, src_ref, count_ref, held_ref, tiles_ref, out_ref, *rest):
    sources, tiles, wide, sems = rest
    start, held, placed = places(2, at_ref, dst_ref, src_ref, count_ref)
    begin = pl.multiple_of(start * (SLOTS * TILE), SLOTS * TILE)
    heads = [
        pltpu.make_async_copy(tiles_ref.at[pl.ds(begin, PAIR * TILE)], tiles, sems.at[0]),
        pltpu.make_async_copy(held_ref, sources, sems.at[1]),
    ]
    for copy in heads:
        copy.start()
    for copy in heads:
        copy.wait()
    out_ref[...] = products(held, placed, tiles, sources, wide)


def sum_own(at, dst, src, count, sources, tiles):
    rows, channels = sources.shape
    return pl.pallas_call(
        sum_own_kernel,
        in_specs=[SMEM] * 4 + [ANY] + [HBM],
        out_specs=VMEM,
        out_shape=jax.ShapeDtypeStruct((2 * TILE, channels), jnp.float32),
        scratch_shapes=[
            pltpu.VMEM((rows, channels), jnp.bfloat16),
            pltpu.VMEM((PAIR * TILE, TILE), jnp.bfloat16),
            pltpu.VMEM((3 * TILE, PAIR * TILE), jnp.bfloat16),
            pltpu.SemaphoreType.DMA((2,)),
        ],
        compiler_params=pltpu.CompilerParams(vmem_limit_bytes=VMEM_LIMIT),
        cost_estimate=pl.CostEstimate(
            flops=4 * TILE * TILE * PAIR * channels,
            bytes_accessed=2 * (rows * channels + PAIR * TILE * TILE),
            transcendentals=0,
        ),
        name="sum_own",
    )(at, dst, src, count, sources, tiles)


def join_kernel(cols_ref, own_ref, n0, n1, n2, n3, picked_ref, out_ref):
    total = own_ref[...]
    for part in (n0, n1, n2, n3):
        total = total + part[...].astype(jnp.float32)
    neighbour = total.astype(jnp.bfloat16)
    width = picked_ref.shape[2]
    channel = lax.broadcasted_iota(jnp.int32, (neighbour.shape[1], width), 0)
    joined = jnp.zeros((neighbour.shape[0], width), jnp.float32)
    for j in range(SPLITS):
        onehot = (channel == cols_ref[j]).astype(jnp.bfloat16)
        joined = joined + picked_ref[j].astype(jnp.float32) * jnp.dot(
            neighbour, onehot, preferred_element_type=jnp.float32
        )
    for piece in range(width // TILE):
        out_ref[piece] = joined[:, piece * TILE : (piece + 1) * TILE].astype(out_ref.dtype)


def join(own, parts, picked, cols):
    rows, channels = own.shape
    splits, _, width = cols.shape
    whole = pl.BlockSpec((rows, channels), lambda q: (0, 0))
    return pl.pallas_call(
        join_kernel,
        grid=(width // CHUNK,),
        in_specs=[pl.BlockSpec((splits, 1, CHUNK), lambda q: (0, 0, q))]
        + [whole] * 5
        + [pl.BlockSpec((splits, rows, CHUNK), lambda q: (0, 0, q))],
        out_specs=pl.BlockSpec((CHUNK // TILE, rows, TILE), lambda q: (q, 0, 0)),
        out_shape=jax.ShapeDtypeStruct((width // TILE, rows, TILE), jnp.bfloat16),
        compiler_params=pltpu.CompilerParams(vmem_limit_bytes=VMEM_LIMIT),
        cost_estimate=pl.CostEstimate(
            flops=2 * splits * rows * channels * width,
            bytes_accessed=2 * splits * rows * width,
            transcendentals=0,
        ),
        name="join_sets",
    )(cols, own, *parts, picked)


def local(
    active_table,
    passive_table,
    adjacency,
    tile_dst,
    tile_src,
    tile_count,
    split_active,
    split_passive,
):
    tiles_all = adjacency.reshape(-1, TILE)
    dst, src, count = tile_dst[0, 0], tile_src[0, 0], tile_count[0, 0]
    nc = lax.axis_size("cset")
    at = (lax.axis_index("blk") % 2).astype(jnp.int32)[None]

    messages = pack_tiles(at, dst, src, count, tiles_all)
    *messages, passive_table = lax.optimization_barrier((*messages, passive_table))
    messages = [
        routed(message, which - 2, which % 2 == 1) for which, message in zip(AWAY, messages)
    ]
    copies = jnp.broadcast_to(passive_table[None], (nc,) + passive_table.shape)
    own_rows = lax.all_to_all(copies, "cset", split_axis=0, concat_axis=0, tiled=True)
    own_rows = own_rows.reshape(-1, passive_table.shape[1])
    groups = [[b, b + 1] for b in range(0, lax.axis_size("blk"), 2)]
    twice = jnp.broadcast_to(own_rows[None], (2,) + own_rows.shape)
    sources = lax.all_to_all(
        twice, "blk", split_axis=0, concat_axis=0, tiled=True, axis_index_groups=groups
    ).reshape(-1, own_rows.shape[1])

    parts = sum_away(sources, messages)
    *parts, active_table = lax.optimization_barrier((*parts, active_table))
    parts = [routed(part, 2 - which, which % 2 == 1) for which, part in zip(AWAY, parts)]

    extra = OUTPAD - split_active.shape[1]
    left_cols = jnp.pad(split_active, ((0, 0), (0, extra)), constant_values=-1)[:, None, :]
    right_cols = jnp.pad(split_passive, ((0, 0), (0, extra)), constant_values=-1)[:, None, :]
    picked = pick_columns(active_table, left_cols)
    own = sum_own(at, dst, src, count, sources, tiles_all)
    joined = join(own, parts, picked, right_cols)
    spread = lax.all_to_all(joined, "cset", split_axis=0, concat_axis=0, tiled=True)
    return spread.reshape(-1, TILE)


def solution(mesh):
    in_specs = (
        P(("blk", "cset"), None),
        P(("blk", "cset"), None),
        P("blk", "cset", None, None, None, None),
        P("blk", "cset", None, None),
        P("blk", "cset", None, None),
        P("blk", "cset", None),
        P(),
        P(),
    )
    out_specs = P("blk", "cset")
    return jax.shard_map(local, mesh=mesh, in_specs=in_specs, out_specs=out_specs, check_vma=False)
```

```python
import jax
import jax.numpy as jnp
from jax import lax
from jax.experimental import pallas as pl
from jax.experimental.pallas import tpu as pltpu
from jax.sharding import PartitionSpec as P

SPLITS = 20
OUTPAD = 1024
TILE = 128
CHUNK = 256
SLOTS = 8
PAIR = 2 * SLOTS
TAIL = 16
AWAY = (1, 3, 0, 4)
VMEM_LIMIT = 16 * 1024 * 1024
PACK_LIMIT = 60 * 1024 * 1024


def routed(block, chips, flip):
    nb, nc = lax.axis_size("blk"), lax.axis_size("cset")
    route = []
    for b in range(nb):
        for c in range(nc):
            target = c ^ (nc // 2) if flip else c
            route.append((b * nc + c, ((b + 2 * chips) % nb) * nc + target))
    return lax.ppermute(block, ("blk", "cset"), route)


def places(which, at_ref, dst_ref, src_ref, count_ref):
    core = at_ref[0]
    reach = 9
    nc = 8
    first = 2 * which - core
    start = jnp.clip(first, 0, reach - 2)
    held, rows = [], []
    for half in range(2):
        slot = start + half
        parity = slot - first
        for t in range(SLOTS):
            source = src_ref[0, 0, slot, t]
            inside = jnp.logical_and(parity >= 0, parity < 2)
            held.append(source + jnp.where(parity == 1, 2 * nc, 0))
            live = jnp.logical_and(inside, t < count_ref[0, 0, slot])
            rows.append(jnp.where(live, dst_ref[0, 0, slot, t], 2))
    return start, held, rows


def pack_kernel(at_ref, dst_ref, src_ref, count_ref, tiles_ref, *rest):
    outs, tails, sems = rest[: len(AWAY)], rest[-2], rest[-1]
    copies = []
    lane = lax.broadcasted_iota(jnp.int32, (TAIL, TILE), 1)
    line = lax.broadcasted_iota(jnp.int32, (TAIL, TILE), 0)
    for n, which in enumerate(AWAY):
        start, held, rows = places(which, at_ref, dst_ref, src_ref, count_ref)
        begin = pl.multiple_of(start * (SLOTS * TILE), SLOTS * TILE)
        copy = pltpu.make_async_copy(
            tiles_ref.at[pl.ds(begin, PAIR * TILE)], outs[n].at[pl.ds(0, PAIR * TILE)], sems.at[2 * n]
        )
        copy.start()
        copies.append(copy)
        tail = jnp.zeros((TAIL, TILE), jnp.int32)
        for t in range(PAIR):
            tail = jnp.where(lane == t, jnp.where(line == 0, held[t], rows[t]), tail)
        tails[n] = tail.astype(jnp.float32).astype(jnp.bfloat16)
        copy = pltpu.make_async_copy(
            tails.at[n], outs[n].at[pl.ds(PAIR * TILE, TAIL)], sems.at[2 * n + 1]
        )
        copy.start()
        copies.append(copy)
    for copy in copies:
        copy.wait()


SMEM = pl.BlockSpec(memory_space=pltpu.SMEM)
VMEM = pl.BlockSpec(memory_space=pltpu.VMEM)
ANY = pl.BlockSpec(memory_space=pl.ANY)
HBM = pl.BlockSpec(memory_space=pltpu.HBM)


def pack_tiles(at, dst, src, count, tiles):
    return pl.pallas_call(
        pack_kernel,
        in_specs=[SMEM, SMEM, SMEM, SMEM, HBM],
        out_specs=[ANY] * len(AWAY),
        out_shape=[jax.ShapeDtypeStruct((PAIR * TILE + TAIL, TILE), jnp.bfloat16)] * len(AWAY),
        scratch_shapes=[
            pltpu.VMEM((len(AWAY), TAIL, TILE), jnp.bfloat16),
            pltpu.SemaphoreType.DMA((2 * len(AWAY),)),
        ],
        compiler_params=pltpu.CompilerParams(vmem_limit_bytes=PACK_LIMIT),
        name="pack_tiles",
    )(at, dst, src, count, tiles)


def pick_kernel(cols_ref, table_ref, out_ref):
    width = cols_ref.shape[2]
    channel = lax.broadcasted_iota(jnp.int32, (table_ref.shape[1], width), 0)
    onehot = (channel == cols_ref[0]).astype(jnp.bfloat16)
    out_ref[0] = jnp.dot(
        table_ref[...], onehot, preferred_element_type=jnp.float32
    ).astype(jnp.bfloat16)


def pick_columns(table, cols):
    rows, channels = table.shape
    splits, _, width = cols.shape
    return pl.pallas_call(
        pick_kernel,
        grid=(splits,),
        in_specs=[
            pl.BlockSpec((1, 1, width), lambda j: (j, 0, 0)),
            pl.BlockSpec((rows, channels), lambda j: (0, 0)),
        ],
        out_specs=pl.BlockSpec((1, rows, width), lambda j: (j, 0, 0)),
        out_shape=jax.ShapeDtypeStruct((splits, rows, width), jnp.bfloat16),
        compiler_params=pltpu.CompilerParams(vmem_limit_bytes=PACK_LIMIT),
        cost_estimate=pl.CostEstimate(
            flops=2 * splits * rows * channels * width,
            bytes_accessed=2 * splits * rows * width,
            transcendentals=0,
        ),
        name="pick_active",
    )(cols, table)


def products(held, rows, tiles, sources):
    total = None
    for t in range(0, PAIR, 2):
        sides, chosen = [], []
        for n in (t, t + 1):
            tile = tiles[n * TILE : (n + 1) * TILE]
            empty = jnp.zeros_like(tile)
            sides.append(
                jnp.concatenate(
                    [jnp.where(rows[n] == 0, tile, empty), jnp.where(rows[n] == 1, tile, empty)], axis=0
                )
            )
            chosen.append(sources[pl.ds(pl.multiple_of(held[n] * TILE, TILE), TILE)])
        product = jnp.dot(
            jnp.concatenate(sides, axis=1),
            jnp.concatenate(chosen, axis=0),
            preferred_element_type=jnp.float32,
        )
        total = product if total is None else total + product
    return total


def sum_away_kernel(held_ref, *rest):
    count = len(AWAY)
    tiles_refs, outs = rest[:count], rest[count : 2 * count]
    sources, tiles, tail_b, tail, tail_s, sems = rest[2 * count :]
    ends = [
        pltpu.make_async_copy(
            tiles_refs[n].at[pl.ds(PAIR * TILE, TAIL)], tail_b.at[n], sems.at[count + 2 + n]
        )
        for n in range(count)
    ]
    whole = pltpu.make_async_copy(held_ref, sources, sems.at[count])
    heads = [
        pltpu.make_async_copy(tiles_refs[n].at[pl.ds(0, PAIR * TILE)], tiles.at[n], sems.at[n])
        for n in range(count)
    ]
    for copy in ends + [whole] + heads:
        copy.start()
    for copy in ends:
        copy.wait()
    tail[...] = tail_b[...].astype(jnp.float32).astype(jnp.int32)
    copy = pltpu.make_async_copy(tail, tail_s, sems.at[count + 1])
    copy.start()
    copy.wait()
    whole.wait()
    for n in range(count):
        held = [tail_s[n, 0, t] for t in range(PAIR)]
        placed = [tail_s[n, 1, t] for t in range(PAIR)]
        heads[n].wait()
        outs[n][...] = products(held, placed, tiles.at[n], sources).astype(jnp.bfloat16)


def sum_away(sources, messages):
    rows, channels = sources.shape
    count = len(messages)
    return pl.pallas_call(
        sum_away_kernel,
        in_specs=[ANY] * (1 + count),
        out_specs=[VMEM] * count,
        out_shape=[jax.ShapeDtypeStruct((2 * TILE, channels), jnp.bfloat16)] * count,
        scratch_shapes=[
            pltpu.VMEM((rows, channels), jnp.bfloat16),
            pltpu.VMEM((count, PAIR * TILE, TILE), jnp.bfloat16),
            pltpu.VMEM((count, TAIL, TILE), jnp.bfloat16),
            pltpu.VMEM((count, TAIL, TILE), jnp.int32),
            pltpu.SMEM((count, TAIL, TILE), jnp.int32),
            pltpu.SemaphoreType.DMA((2 * count + 2,)),
        ],
        compiler_params=pltpu.CompilerParams(vmem_limit_bytes=VMEM_LIMIT),
        cost_estimate=pl.CostEstimate(
            flops=count * 4 * TILE * TILE * PAIR * channels,
            bytes_accessed=2 * (rows * channels + count * PAIR * TILE * TILE),
            transcendentals=0,
        ),
        name="sum_away",
    )(sources, *messages)


def sum_own_kernel(at_ref, dst_ref, src_ref, count_ref, held_ref, tiles_ref, out_ref, *rest):
    sources, tiles, sems = rest
    start, held, placed = places(2, at_ref, dst_ref, src_ref, count_ref)
    begin = pl.multiple_of(start * (SLOTS * TILE), SLOTS * TILE)
    heads = [
        pltpu.make_async_copy(tiles_ref.at[pl.ds(begin, PAIR * TILE)], tiles, sems.at[0]),
        pltpu.make_async_copy(held_ref, sources, sems.at[1]),
    ]
    for copy in heads:
        copy.start()
    for copy in heads:
        copy.wait()
    out_ref[...] = products(held, placed, tiles, sources)


def sum_own(at, dst, src, count, sources, tiles):
    rows, channels = sources.shape
    return pl.pallas_call(
        sum_own_kernel,
        in_specs=[SMEM] * 4 + [ANY] + [HBM],
        out_specs=VMEM,
        out_shape=jax.ShapeDtypeStruct((2 * TILE, channels), jnp.float32),
        scratch_shapes=[
            pltpu.VMEM((rows, channels), jnp.bfloat16),
            pltpu.VMEM((PAIR * TILE, TILE), jnp.bfloat16),
            pltpu.SemaphoreType.DMA((2,)),
        ],
        compiler_params=pltpu.CompilerParams(vmem_limit_bytes=VMEM_LIMIT),
        cost_estimate=pl.CostEstimate(
            flops=4 * TILE * TILE * PAIR * channels,
            bytes_accessed=2 * (rows * channels + PAIR * TILE * TILE),
            transcendentals=0,
        ),
        name="sum_own",
    )(at, dst, src, count, sources, tiles)


def join_kernel(cols_ref, own_ref, n0, n1, n2, n3, picked_ref, out_ref):
    total = own_ref[...]
    for part in (n0, n1, n2, n3):
        total = total + part[...].astype(jnp.float32)
    neighbour = total.astype(jnp.bfloat16)
    width = picked_ref.shape[2]
    channel = lax.broadcasted_iota(jnp.int32, (neighbour.shape[1], width), 0)
    joined = jnp.zeros((neighbour.shape[0], width), jnp.float32)
    for j in range(SPLITS):
        onehot = (channel == cols_ref[j]).astype(jnp.bfloat16)
        joined = joined + picked_ref[j].astype(jnp.float32) * jnp.dot(
            neighbour, onehot, preferred_element_type=jnp.float32
        )
    for piece in range(width // TILE):
        out_ref[piece] = joined[:, piece * TILE : (piece + 1) * TILE].astype(out_ref.dtype)


def join(own, parts, picked, cols):
    rows, channels = own.shape
    splits, _, width = cols.shape
    whole = pl.BlockSpec((rows, channels), lambda q: (0, 0))
    return pl.pallas_call(
        join_kernel,
        grid=(width // CHUNK,),
        in_specs=[pl.BlockSpec((splits, 1, CHUNK), lambda q: (0, 0, q))]
        + [whole] * 5
        + [pl.BlockSpec((splits, rows, CHUNK), lambda q: (0, 0, q))],
        out_specs=pl.BlockSpec((CHUNK // TILE, rows, TILE), lambda q: (q, 0, 0)),
        out_shape=jax.ShapeDtypeStruct((width // TILE, rows, TILE), jnp.bfloat16),
        compiler_params=pltpu.CompilerParams(vmem_limit_bytes=VMEM_LIMIT),
        cost_estimate=pl.CostEstimate(
            flops=2 * splits * rows * channels * width,
            bytes_accessed=2 * splits * rows * width,
            transcendentals=0,
        ),
        name="join_sets",
    )(cols, own, *parts, picked)


def local(
    active_table,
    passive_table,
    adjacency,
    tile_dst,
    tile_src,
    tile_count,
    split_active,
    split_passive,
):
    tiles_all = adjacency.reshape(-1, TILE)
    dst, src, count = tile_dst, tile_src, tile_count
    nc = lax.axis_size("cset")
    at = (lax.axis_index("blk") % 2).astype(jnp.int32)[None]

    messages = pack_tiles(at, dst, src, count, tiles_all)
    *messages, passive_table = lax.optimization_barrier((*messages, passive_table))
    messages = [
        routed(message, which - 2, which % 2 == 1) for which, message in zip(AWAY, messages)
    ]
    copies = jnp.broadcast_to(passive_table[None], (nc,) + passive_table.shape)
    own_rows = lax.all_to_all(copies, "cset", split_axis=0, concat_axis=0, tiled=True)
    own_rows = own_rows.reshape(-1, passive_table.shape[1])
    groups = [[b, b + 1] for b in range(0, lax.axis_size("blk"), 2)]
    twice = jnp.broadcast_to(own_rows[None], (2,) + own_rows.shape)
    sources = lax.all_to_all(
        twice, "blk", split_axis=0, concat_axis=0, tiled=True, axis_index_groups=groups
    ).reshape(-1, own_rows.shape[1])

    extra = OUTPAD - split_active.shape[1]
    left_cols = jnp.pad(split_active, ((0, 0), (0, extra)), constant_values=-1)[:, None, :]
    right_cols = jnp.pad(split_passive, ((0, 0), (0, extra)), constant_values=-1)[:, None, :]
    picked = pick_columns(active_table, left_cols)
    own = sum_own(at, dst, src, count, sources, tiles_all)
    sources, picked, own, right_cols = lax.optimization_barrier((sources, picked, own, right_cols))
    parts = sum_away(sources, messages)
    parts = [routed(part, 2 - which, which % 2 == 1) for which, part in zip(AWAY, parts)]
    joined = join(own, parts, picked, right_cols)
    spread = lax.all_to_all(joined, "cset", split_axis=0, concat_axis=0, tiled=True)
    return spread.reshape(-1, TILE)


def solution(mesh):
    in_specs = (
        P(("blk", "cset"), None),
        P(("blk", "cset"), None),
        P("blk", "cset", None, None, None, None),
        P("blk", "cset", None, None),
        P("blk", "cset", None, None),
        P("blk", "cset", None),
        P(),
        P(),
    )
    out_specs = P("blk", "cset")
    return jax.shard_map(local, mesh=mesh, in_specs=in_specs, out_specs=out_specs, check_vma=False)
```

```python
import jax
import jax.numpy as jnp
from jax import lax
from jax.experimental import pallas as pl
from jax.experimental.pallas import tpu as pltpu
from jax.sharding import PartitionSpec as P

SPLITS = 20
OUTPAD = 1024
TILE = 128
CHUNK = 512
SLOTS = 8
PAIR = 2 * SLOTS
TAIL = 16
AWAY = (1, 3, 0, 4)
VMEM_LIMIT = 16 * 1024 * 1024
PACK_LIMIT = 60 * 1024 * 1024


def routed(block, chips, flip):
    nb, nc = lax.axis_size("blk"), lax.axis_size("cset")
    route = []
    for b in range(nb):
        for c in range(nc):
            target = c ^ (nc // 2) if flip else c
            route.append((b * nc + c, ((b + 2 * chips) % nb) * nc + target))
    return lax.ppermute(block, ("blk", "cset"), route)


def places(which, at_ref, dst_ref, src_ref, count_ref):
    core = at_ref[0]
    reach = 9
    nc = 8
    first = 2 * which - core
    start = jnp.clip(first, 0, reach - 2)
    held, rows = [], []
    for half in range(2):
        slot = start + half
        parity = slot - first
        for t in range(SLOTS):
            source = src_ref[t, slot]
            inside = jnp.logical_and(parity >= 0, parity < 2)
            held.append(source + jnp.where(parity == 1, 2 * nc, 0))
            live = jnp.logical_and(inside, t < count_ref[slot])
            rows.append(jnp.where(live, dst_ref[t, slot], 2))
    return start, held, rows


def pack_kernel(at_ref, dst_ref, src_ref, count_ref, tiles_ref, *rest):
    outs = rest[: len(AWAY)]
    held_tiles, sems_in, sems_out = rest[len(AWAY) :]
    lane = lax.broadcasted_iota(jnp.int32, (TAIL, TILE), 1)
    line = lax.broadcasted_iota(jnp.int32, (TAIL, TILE), 0)
    found = [places(which, at_ref, dst_ref, src_ref, count_ref) for which in AWAY]
    arriving, leaving = [], []
    for n in range(len(AWAY)):
        begin = pl.multiple_of(found[n][0] * (SLOTS * TILE), SLOTS * TILE)
        arriving.append(
            pltpu.make_async_copy(
                tiles_ref.at[pl.ds(begin, PAIR * TILE)],
                held_tiles.at[n, pl.ds(0, PAIR * TILE)],
                sems_in.at[n],
            )
        )
        arriving[n].start()
    for n in range(len(AWAY)):
        _, held, rows = found[n]
        tail = jnp.zeros((TAIL, TILE), jnp.int32)
        for t in range(PAIR):
            tail = jnp.where(lane == t, jnp.where(line == 0, held[t], rows[t]), tail)
        held_tiles[n, PAIR * TILE : PAIR * TILE + TAIL] = tail.astype(jnp.float32).astype(jnp.bfloat16)
        arriving[n].wait()
        leaving.append(pltpu.make_async_copy(held_tiles.at[n], outs[n], sems_out.at[n]))
        leaving[n].start()
    for copy in leaving:
        copy.wait()


SMEM = pl.BlockSpec(memory_space=pltpu.SMEM)
VMEM = pl.BlockSpec(memory_space=pltpu.VMEM)
ANY = pl.BlockSpec(memory_space=pl.ANY)
HBM = pl.BlockSpec(memory_space=pltpu.HBM)


def pack_tiles(at, dst, src, count, tiles):
    return pl.pallas_call(
        pack_kernel,
        in_specs=[SMEM, SMEM, SMEM, SMEM, HBM],
        out_specs=[ANY] * len(AWAY),
        out_shape=[jax.ShapeDtypeStruct((PAIR * TILE + TAIL, TILE), jnp.bfloat16)] * len(AWAY),
        scratch_shapes=[
            pltpu.VMEM((len(AWAY), PAIR * TILE + TAIL, TILE), jnp.bfloat16),
            pltpu.SemaphoreType.DMA((len(AWAY),)),
            pltpu.SemaphoreType.DMA((len(AWAY),)),
        ],
        compiler_params=pltpu.CompilerParams(vmem_limit_bytes=PACK_LIMIT),
        name="pack_tiles",
    )(at, dst, src, count, tiles)


def products(held, rows, tiles, sources):
    total = None
    for t in range(0, PAIR, 2):
        sides, chosen = [], []
        for n in (t, t + 1):
            tile = tiles[n * TILE : (n + 1) * TILE]
            empty = jnp.zeros_like(tile)
            sides.append(
                jnp.concatenate(
                    [jnp.where(rows[n] == 0, tile, empty), jnp.where(rows[n] == 1, tile, empty)], axis=0
                )
            )
            chosen.append(sources[pl.ds(pl.multiple_of(held[n] * TILE, TILE), TILE)])
        product = jnp.dot(
            jnp.concatenate(sides, axis=1),
            jnp.concatenate(chosen, axis=0),
            preferred_element_type=jnp.float32,
        )
        total = product if total is None else total + product
    return total


def sum_away_kernel(held_ref, *rest):
    count = len(AWAY)
    tiles_refs, outs = rest[:count], rest[count : 2 * count]
    sources, tiles, tail_b, tail, tail_s, sems = rest[2 * count :]
    ends = [
        pltpu.make_async_copy(
            tiles_refs[n].at[pl.ds(PAIR * TILE, TAIL)], tail_b.at[n], sems.at[count + 2 + n]
        )
        for n in range(count)
    ]
    whole = pltpu.make_async_copy(held_ref, sources, sems.at[count])
    heads = [
        pltpu.make_async_copy(tiles_refs[n].at[pl.ds(0, PAIR * TILE)], tiles.at[n], sems.at[n])
        for n in range(count)
    ]
    for copy in ends + [whole] + heads:
        copy.start()
    for copy in ends:
        copy.wait()
    tail[...] = tail_b[...].astype(jnp.float32).astype(jnp.int32)
    copy = pltpu.make_async_copy(tail, tail_s, sems.at[count + 1])
    copy.start()
    copy.wait()
    whole.wait()
    for n in range(count):
        held = [tail_s[n, 0, t] for t in range(PAIR)]
        placed = [tail_s[n, 1, t] for t in range(PAIR)]
        heads[n].wait()
        outs[n][...] = products(held, placed, tiles.at[n], sources).astype(jnp.bfloat16)


def sum_away(sources, messages):
    rows, channels = sources.shape
    count = len(messages)
    return pl.pallas_call(
        sum_away_kernel,
        in_specs=[ANY] * (1 + count),
        out_specs=[VMEM] * count,
        out_shape=[jax.ShapeDtypeStruct((2 * TILE, channels), jnp.bfloat16)] * count,
        scratch_shapes=[
            pltpu.VMEM((rows, channels), jnp.bfloat16),
            pltpu.VMEM((count, PAIR * TILE, TILE), jnp.bfloat16),
            pltpu.VMEM((count, TAIL, TILE), jnp.bfloat16),
            pltpu.VMEM((count, TAIL, TILE), jnp.int32),
            pltpu.SMEM((count, TAIL, TILE), jnp.int32),
            pltpu.SemaphoreType.DMA((2 * count + 2,)),
        ],
        compiler_params=pltpu.CompilerParams(vmem_limit_bytes=VMEM_LIMIT),
        cost_estimate=pl.CostEstimate(
            flops=count * 4 * TILE * TILE * PAIR * channels,
            bytes_accessed=2 * (rows * channels + count * PAIR * TILE * TILE),
            transcendentals=0,
        ),
        name="sum_away",
    )(sources, *messages)


def sum_own_kernel(at_ref, dst_ref, src_ref, count_ref, held_ref, tiles_ref, out_ref, *rest):
    sources, tiles, sems = rest
    start, held, placed = places(2, at_ref, dst_ref, src_ref, count_ref)
    begin = pl.multiple_of(start * (SLOTS * TILE), SLOTS * TILE)
    heads = [
        pltpu.make_async_copy(tiles_ref.at[pl.ds(begin, PAIR * TILE)], tiles, sems.at[0]),
        pltpu.make_async_copy(held_ref, sources, sems.at[1]),
    ]
    for copy in heads:
        copy.start()
    for copy in heads:
        copy.wait()
    out_ref[...] = products(held, placed, tiles, sources)


def sum_own(at, dst, src, count, sources, tiles):
    rows, channels = sources.shape
    return pl.pallas_call(
        sum_own_kernel,
        in_specs=[SMEM] * 4 + [ANY] + [HBM],
        out_specs=VMEM,
        out_shape=jax.ShapeDtypeStruct((2 * TILE, channels), jnp.float32),
        scratch_shapes=[
            pltpu.VMEM((rows, channels), jnp.bfloat16),
            pltpu.VMEM((PAIR * TILE, TILE), jnp.bfloat16),
            pltpu.SemaphoreType.DMA((2,)),
        ],
        compiler_params=pltpu.CompilerParams(vmem_limit_bytes=VMEM_LIMIT),
        cost_estimate=pl.CostEstimate(
            flops=4 * TILE * TILE * PAIR * channels,
            bytes_accessed=2 * (rows * channels + PAIR * TILE * TILE),
            transcendentals=0,
        ),
        name="sum_own",
    )(at, dst, src, count, sources, tiles)


def join_kernel(left_ref, right_ref, active_ref, own_ref, n0, n1, n2, n3, out_ref):
    total = own_ref[...]
    for part in (n0, n1, n2, n3):
        total = total + part[...].astype(jnp.float32)
    neighbour = total.astype(jnp.bfloat16)
    active = active_ref[...]
    shape = (active.shape[1], left_ref.shape[2])
    channel = lax.broadcasted_iota(jnp.int32, shape, 0).astype(jnp.float32).astype(jnp.bfloat16)
    one, zero = jnp.ones(shape, jnp.bfloat16), jnp.zeros(shape, jnp.bfloat16)
    joined = jnp.zeros((active.shape[0], shape[1]), jnp.float32)
    for j in range(SPLITS):
        left = jnp.where(channel == left_ref[j], one, zero)
        right = jnp.where(channel == right_ref[j], one, zero)
        joined = joined + jnp.dot(active, left, preferred_element_type=jnp.float32) * jnp.dot(
            neighbour, right, preferred_element_type=jnp.float32
        )
    for piece in range(shape[1] // TILE):
        out_ref[piece] = joined[:, piece * TILE : (piece + 1) * TILE].astype(out_ref.dtype)


def join(active, own, parts, left, right):
    rows, channels = own.shape
    splits, _, width = left.shape
    whole = pl.BlockSpec((rows, channels), lambda q: (0, 0))
    columns = pl.BlockSpec((splits, 1, CHUNK), lambda q: (0, 0, q))
    return pl.pallas_call(
        join_kernel,
        grid=(width // CHUNK,),
        in_specs=[columns] * 2 + [whole] * 6,
        out_specs=pl.BlockSpec((CHUNK // TILE, rows, TILE), lambda q: (q, 0, 0)),
        out_shape=jax.ShapeDtypeStruct((width // TILE, rows, TILE), jnp.bfloat16),
        compiler_params=pltpu.CompilerParams(vmem_limit_bytes=VMEM_LIMIT),
        cost_estimate=pl.CostEstimate(
            flops=4 * splits * rows * channels * width,
            bytes_accessed=2 * rows * width,
            transcendentals=0,
        ),
        name="join_sets",
    )(left, right, active, own, *parts)


def local(
    active_table,
    passive_table,
    adjacency,
    tile_dst,
    tile_src,
    tile_count,
    split_active,
    split_passive,
):
    tiles_all = adjacency.reshape(-1, TILE)
    dst, src, count = tile_dst[0, 0].T, tile_src[0, 0].T, tile_count[0, 0]
    nc = lax.axis_size("cset")
    at = (lax.axis_index("blk") % 2).astype(jnp.int32)[None]

    messages = pack_tiles(at, dst, src, count, tiles_all)
    *messages, passive_table = lax.optimization_barrier((*messages, passive_table))
    messages = [
        routed(message, which - 2, which % 2 == 1) for which, message in zip(AWAY, messages)
    ]
    copies = jnp.broadcast_to(passive_table[None], (nc,) + passive_table.shape)
    own_rows = lax.all_to_all(copies, "cset", split_axis=0, concat_axis=0, tiled=True)
    own_rows = own_rows.reshape(-1, passive_table.shape[1])
    groups = [[b, b + 1] for b in range(0, lax.axis_size("blk"), 2)]
    twice = jnp.broadcast_to(own_rows[None], (2,) + own_rows.shape)
    sources = lax.all_to_all(
        twice, "blk", split_axis=0, concat_axis=0, tiled=True, axis_index_groups=groups
    ).reshape(-1, own_rows.shape[1])

    extra = OUTPAD - split_active.shape[1]
    left, right = (
        jnp.pad(cols.astype(jnp.bfloat16), ((0, 0), (0, extra)), constant_values=-1)[:, None, :]
        for cols in (split_active, split_passive)
    )
    own = sum_own(at, dst, src, count, sources, tiles_all)
    sources, own, left, right = lax.optimization_barrier((sources, own, left, right))
    parts = sum_away(sources, messages)
    parts = [routed(part, 2 - which, which % 2 == 1) for which, part in zip(AWAY, parts)]
    joined = join(active_table, own, parts, left, right)
    spread = lax.all_to_all(joined, "cset", split_axis=0, concat_axis=0, tiled=True)
    return spread.reshape(-1, TILE)


def solution(mesh):
    in_specs = (
        P(("blk", "cset"), None),
        P(("blk", "cset"), None),
        P("blk", "cset", None, None, None, None),
        P("blk", "cset", None, None),
        P("blk", "cset", None, None),
        P("blk", "cset", None),
        P(),
        P(),
    )
    out_specs = P("blk", "cset")
    return jax.shard_map(local, mesh=mesh, in_specs=in_specs, out_specs=out_specs, check_vma=False)
```

```python
import jax
import jax.numpy as jnp
from jax import lax
from jax.experimental import pallas as pl
from jax.experimental.pallas import tpu as pltpu
from jax.sharding import PartitionSpec as P

SPLITS = 20
OUTPAD = 1024
TILE = 128
CHUNK = 512
SLOTS = 8
PAIR = 2 * SLOTS
TAIL = 16
REACH = 9
PART_TILES = 16
VMEM_LIMIT = 16 * 1024 * 1024


def routed(block, hops):
    nb, nc = lax.axis_size("blk"), lax.axis_size("cset")
    route = []
    for b in range(nb):
        chips = hops(b % 2)
        for c in range(nc):
            target = c ^ (nc // 2) if chips % 2 else c
            route.append((b * nc + c, ((b + 2 * chips) % nb) * nc + target))
    return lax.ppermute(block, ("blk", "cset"), route)


def places(slots, dst_ref, src_ref, count_ref):
    held, rows = [], []
    for slot, parity in slots:
        for t in range(SLOTS):
            held.append(src_ref[t, slot] + parity * PART_TILES)
            rows.append(jnp.where(t < count_ref[slot], dst_ref[t, slot], 2))
    return held, rows


def pair_slots(which, core):
    first = 2 * which - core
    return [(first, 0), (first + 1, 1)]


def message_slots(core):
    return [
        [(REACH - 1, core)],
        pair_slots(3, core),
        pair_slots(1, core),
        [(0, core)],
        [(1 + (REACH - 3) * core, 1 - core)],
    ]


HOPS = [
    lambda core: 2,
    lambda core: 1,
    lambda core: -1,
    lambda core: -2,
    lambda core: 4 * core - 2,
]
LENGTHS = [SLOTS, PAIR, PAIR, SLOTS, SLOTS]
BACK = [-2, -1, 1, 2]


def pack_kernel(at_ref, dst_ref, src_ref, count_ref, tiles_ref, *rest):
    outs, sems = rest[: len(HOPS)], rest[len(HOPS)]
    lane = lax.broadcasted_iota(jnp.int32, (TAIL, TILE), 1)
    line = lax.broadcasted_iota(jnp.int32, (TAIL, TILE), 0)
    slots = message_slots(at_ref[0])
    copies = []
    for n, length in enumerate(LENGTHS):
        begin = pl.multiple_of(slots[n][0][0] * (SLOTS * TILE), SLOTS * TILE)
        copies.append(
            pltpu.make_async_copy(
                tiles_ref.at[pl.ds(begin, length * TILE)],
                outs[n].at[pl.ds(0, length * TILE)],
                sems.at[n],
            )
        )
        copies[n].start()
    for n, length in enumerate(LENGTHS):
        held, rows = places(slots[n], dst_ref, src_ref, count_ref)
        tail = jnp.zeros((TAIL, TILE), jnp.int32)
        for t in range(length):
            tail = jnp.where(lane == t, jnp.where(line == 0, held[t], rows[t]), tail)
        outs[n][length * TILE : length * TILE + TAIL] = tail.astype(jnp.float32).astype(jnp.bfloat16)
    for copy in copies:
        copy.wait()


SMEM = pl.BlockSpec(memory_space=pltpu.SMEM)
VMEM = pl.BlockSpec(memory_space=pltpu.VMEM)
ANY = pl.BlockSpec(memory_space=pl.ANY)
HBM = pl.BlockSpec(memory_space=pltpu.HBM)


def in_space(space, *arrays):
    return [pltpu.with_memory_space_constraint(array, space) for array in arrays]


def pack_tiles(at, dst, src, count, tiles):
    return pl.pallas_call(
        pack_kernel,
        in_specs=[SMEM, SMEM, SMEM, SMEM, HBM],
        out_specs=[VMEM] * len(LENGTHS),
        out_shape=[pltpu.VMEM((length * TILE + TAIL, TILE), jnp.bfloat16) for length in LENGTHS],
        scratch_shapes=[pltpu.SemaphoreType.DMA((len(LENGTHS),))],
        compiler_params=pltpu.CompilerParams(vmem_limit_bytes=VMEM_LIMIT),
        name="pack_tiles",
    )(at, *in_space(pltpu.HBM, dst, src, count, tiles))


def products(held, rows, tiles, sources):
    total = None
    for t in range(0, PAIR, 2):
        sides, chosen = [], []
        for n in (t, t + 1):
            tile = tiles(n)
            empty = jnp.zeros_like(tile)
            sides.append(
                jnp.concatenate(
                    [jnp.where(rows[n] == 0, tile, empty), jnp.where(rows[n] == 1, tile, empty)], axis=0
                )
            )
            chosen.append(sources[pl.ds(pl.multiple_of(held[n] * TILE, TILE), TILE)])
        product = jnp.dot(
            jnp.concatenate(sides, axis=1),
            jnp.concatenate(chosen, axis=0),
            preferred_element_type=jnp.float32,
        )
        total = product if total is None else total + product
    return total


def sum_away_kernel(at_ref, sources, *rest):
    count = len(LENGTHS)
    messages, outs = rest[:count], rest[count : count + len(BACK)]
    tail, tail_s, sem = rest[count + len(BACK) :]
    core = at_ref[0]
    for n, length in enumerate(LENGTHS):
        end = messages[n][length * TILE : length * TILE + TAIL]
        tail[n] = end.astype(jnp.float32).astype(jnp.int32)
    copy = pltpu.make_async_copy(tail, tail_s, sem)
    copy.start()
    copy.wait()

    def part(n, keep=None):
        held = [tail_s[n, 0, t] for t in range(LENGTHS[n])]
        rows = [tail_s[n, 1, t] for t in range(LENGTHS[n])]
        if keep is not None:
            rows = [jnp.where(keep, row, 2) for row in rows]
        return [
            (held[t], rows[t], messages[n].at[t * TILE : (t + 1) * TILE]) for t in range(LENGTHS[n])
        ]

    odd_below, odd_above = part(4, core == 1), part(4, core == 0)
    for out, tiles in zip(outs, (part(0) + odd_below, part(1), part(2), part(3) + odd_above)):
        held, rows, refs = zip(*tiles)
        out[...] = products(held, rows, lambda n: refs[n][...], sources).astype(jnp.bfloat16)


def sum_away(at, sources, messages):
    rows, channels = sources.shape
    return pl.pallas_call(
        sum_away_kernel,
        in_specs=[SMEM] + [VMEM] * (1 + len(messages)),
        out_specs=[VMEM] * len(BACK),
        out_shape=[pltpu.VMEM((2 * TILE, channels), jnp.bfloat16)] * len(BACK),
        scratch_shapes=[
            pltpu.VMEM((len(messages), TAIL, TILE), jnp.int32),
            pltpu.SMEM((len(messages), TAIL, TILE), jnp.int32),
            pltpu.SemaphoreType.DMA,
        ],
        compiler_params=pltpu.CompilerParams(vmem_limit_bytes=VMEM_LIMIT),
        cost_estimate=pl.CostEstimate(
            flops=len(BACK) * 4 * TILE * TILE * PAIR * channels,
            bytes_accessed=2 * (rows * channels + len(BACK) * PAIR * TILE * TILE),
            transcendentals=0,
        ),
        name="sum_away",
    )(at, *in_space(pltpu.VMEM, sources, *messages))


def sum_own_kernel(at_ref, dst_ref, src_ref, count_ref, sources_ref, tiles_ref, out_ref, *rest):
    tiles, sem = rest
    slots = pair_slots(2, at_ref[0])
    held, placed = places(slots, dst_ref, src_ref, count_ref)
    begin = pl.multiple_of(slots[0][0] * (SLOTS * TILE), SLOTS * TILE)
    copy = pltpu.make_async_copy(tiles_ref.at[pl.ds(begin, PAIR * TILE)], tiles, sem)
    copy.start()
    copy.wait()
    out_ref[...] = products(held, placed, lambda n: tiles[n * TILE : (n + 1) * TILE], sources_ref)


def sum_own(at, dst, src, count, sources, tiles):
    rows, channels = sources.shape
    return pl.pallas_call(
        sum_own_kernel,
        in_specs=[SMEM] * 4 + [VMEM] + [HBM],
        out_specs=VMEM,
        out_shape=jax.ShapeDtypeStruct((2 * TILE, channels), jnp.float32),
        scratch_shapes=[
            pltpu.VMEM((PAIR * TILE, TILE), jnp.bfloat16),
            pltpu.SemaphoreType.DMA,
        ],
        compiler_params=pltpu.CompilerParams(vmem_limit_bytes=VMEM_LIMIT),
        cost_estimate=pl.CostEstimate(
            flops=4 * TILE * TILE * PAIR * channels,
            bytes_accessed=2 * (rows * channels + PAIR * TILE * TILE),
            transcendentals=0,
        ),
        name="sum_own",
    )(
        at,
        *in_space(pltpu.HBM, dst, src, count),
        *in_space(pltpu.VMEM, sources),
        *in_space(pltpu.HBM, tiles),
    )


def join_kernel(left_ref, right_ref, active_ref, own_ref, n0, n1, n2, n3, out_ref):
    total = own_ref[...]
    for part in (n0, n1, n2, n3):
        total = total + part[...].astype(jnp.float32)
    neighbour = total.astype(jnp.bfloat16)
    active = active_ref[...]
    shape = (active.shape[1], left_ref.shape[2])
    channel = lax.broadcasted_iota(jnp.int32, shape, 0).astype(jnp.float32).astype(jnp.bfloat16)
    one, zero = jnp.ones(shape, jnp.bfloat16), jnp.zeros(shape, jnp.bfloat16)
    joined = jnp.zeros((active.shape[0], shape[1]), jnp.float32)
    for j in range(SPLITS):
        left = jnp.where(channel == left_ref[j], one, zero)
        right = jnp.where(channel == right_ref[j], one, zero)
        joined = joined + jnp.dot(active, left, preferred_element_type=jnp.float32) * jnp.dot(
            neighbour, right, preferred_element_type=jnp.float32
        )
    for piece in range(shape[1] // TILE):
        out_ref[piece] = joined[:, piece * TILE : (piece + 1) * TILE].astype(out_ref.dtype)


def join(active, own, parts, left, right):
    rows, channels = own.shape
    splits, _, width = left.shape
    whole = pl.BlockSpec((rows, channels), lambda q: (0, 0))
    columns = pl.BlockSpec((splits, 1, CHUNK), lambda q: (0, 0, q))
    return pl.pallas_call(
        join_kernel,
        grid=(width // CHUNK,),
        in_specs=[columns] * 2 + [whole] * 6,
        out_specs=pl.BlockSpec((CHUNK // TILE, rows, TILE), lambda q: (q, 0, 0)),
        out_shape=jax.ShapeDtypeStruct((width // TILE, rows, TILE), jnp.bfloat16),
        compiler_params=pltpu.CompilerParams(vmem_limit_bytes=VMEM_LIMIT),
        cost_estimate=pl.CostEstimate(
            flops=4 * splits * rows * channels * width,
            bytes_accessed=2 * rows * width,
            transcendentals=0,
        ),
        name="join_sets",
    )(left, right, active, own, *parts)


def local(
    active_table,
    passive_table,
    adjacency,
    tile_dst,
    tile_src,
    tile_count,
    split_active,
    split_passive,
):
    tiles_all = adjacency.reshape(-1, TILE)
    dst, src, count = tile_dst[0, 0].T, tile_src[0, 0].T, tile_count[0, 0]
    nc = lax.axis_size("cset")
    at = (lax.axis_index("blk") % 2).astype(jnp.int32)[None]

    messages = pack_tiles(at, dst, src, count, tiles_all)
    *messages, passive_table = lax.optimization_barrier((*messages, passive_table))
    messages = [routed(message, hops) for message, hops in zip(messages, HOPS)]
    copies = jnp.broadcast_to(passive_table[None], (nc,) + passive_table.shape)
    own_rows = lax.all_to_all(copies, "cset", split_axis=0, concat_axis=0, tiled=True)
    own_rows = own_rows.reshape(-1, passive_table.shape[1])
    groups = [[b, b + 1] for b in range(0, lax.axis_size("blk"), 2)]
    twice = jnp.broadcast_to(own_rows[None], (2,) + own_rows.shape)
    sources = lax.all_to_all(
        twice, "blk", split_axis=0, concat_axis=0, tiled=True, axis_index_groups=groups
    ).reshape(-1, own_rows.shape[1])

    extra = OUTPAD - split_active.shape[1]
    left, right = (
        jnp.pad(cols.astype(jnp.bfloat16), ((0, 0), (0, extra)), constant_values=-1)[:, None, :]
        for cols in (split_active, split_passive)
    )
    own = sum_own(at, dst, src, count, sources, tiles_all)
    sources, own, left, right = lax.optimization_barrier((sources, own, left, right))
    parts = sum_away(at, sources, messages)
    parts = [routed(part, lambda core, chips=chips: chips) for part, chips in zip(parts, BACK)]
    joined = join(active_table, own, parts, left, right)
    spread = lax.all_to_all(joined, "cset", split_axis=0, concat_axis=0, tiled=True)
    return spread.reshape(-1, TILE)


def solution(mesh):
    in_specs = (
        P(("blk", "cset"), None),
        P(("blk", "cset"), None),
        P("blk", "cset", None, None, None, None),
        P("blk", "cset", None, None),
        P("blk", "cset", None, None),
        P("blk", "cset", None),
        P(),
        P(),
    )
    out_specs = P("blk", "cset")
    return jax.shard_map(local, mesh=mesh, in_specs=in_specs, out_specs=out_specs, check_vma=False)
```

```python
import jax
import jax.numpy as jnp
from jax import lax
from jax.experimental import pallas as pl
from jax.experimental.pallas import tpu as pltpu
from jax.sharding import PartitionSpec as P

SPLITS = 20
OUTPAD = 1024
TILE = 128
CHUNK = 512
SLOTS = 8
PAIR = 2 * SLOTS
TAIL = 16
REACH = 9
PART_TILES = 16
VMEM_LIMIT = 16 * 1024 * 1024


def routed(block, hops):
    nb, nc = lax.axis_size("blk"), lax.axis_size("cset")
    route = []
    for b in range(nb):
        chips = hops(b % 2)
        for c in range(nc):
            target = c ^ (nc // 2) if chips % 2 else c
            route.append((b * nc + c, ((b + 2 * chips) % nb) * nc + target))
    return lax.ppermute(block, ("blk", "cset"), route)


def places(slots, dst_ref, src_ref, count_ref):
    held, rows = [], []
    for slot, parity in slots:
        for t in range(SLOTS):
            held.append(src_ref[t, slot] + parity * PART_TILES)
            rows.append(jnp.where(t < count_ref[slot], dst_ref[t, slot], 2))
    return held, rows


def pair_slots(which, core):
    first = 2 * which - core
    return [(first, 0), (first + 1, 1)]


def message_slots(core):
    return [
        [(REACH - 1, core)],
        pair_slots(3, core),
        pair_slots(1, core),
        [(0, core)],
        [(1 + (REACH - 3) * core, 1 - core)],
    ]


HOPS = [
    lambda core: 2,
    lambda core: 1,
    lambda core: -1,
    lambda core: -2,
    lambda core: 4 * core - 2,
]
LENGTHS = [SLOTS, PAIR, PAIR, SLOTS, SLOTS]


def pack_kernel(at_ref, dst_ref, src_ref, count_ref, tiles_ref, rows_ref, *rest):
    outs, (repeated, sems) = rest[: len(HOPS)], rest[len(HOPS) :]
    lane = lax.broadcasted_iota(jnp.int32, (TAIL, TILE), 1)
    line = lax.broadcasted_iota(jnp.int32, (TAIL, TILE), 0)
    slots = message_slots(at_ref[0])
    copies = []
    for n, length in enumerate(LENGTHS):
        begin = pl.multiple_of(slots[n][0][0] * (SLOTS * TILE), SLOTS * TILE)
        copies.append(
            pltpu.make_async_copy(
                tiles_ref.at[pl.ds(begin, length * TILE)],
                outs[n].at[pl.ds(0, length * TILE)],
                sems.at[n],
            )
        )
    for n in range(repeated.shape[0]):
        copies.append(pltpu.make_async_copy(rows_ref, repeated.at[n], sems.at[len(HOPS) + n]))
    for copy in copies:
        copy.start()
    for n, length in enumerate(LENGTHS):
        held, rows = places(slots[n], dst_ref, src_ref, count_ref)
        tail = jnp.zeros((TAIL, TILE), jnp.int32)
        for t in range(length):
            tail = jnp.where(lane == t, jnp.where(line == 0, held[t], rows[t]), tail)
        outs[n][length * TILE : length * TILE + TAIL] = tail.astype(jnp.float32).astype(jnp.bfloat16)
    for copy in copies:
        copy.wait()


SMEM = pl.BlockSpec(memory_space=pltpu.SMEM)
VMEM = pl.BlockSpec(memory_space=pltpu.VMEM)
ANY = pl.BlockSpec(memory_space=pl.ANY)
HBM = pl.BlockSpec(memory_space=pltpu.HBM)


def in_space(space, *arrays):
    return [pltpu.with_memory_space_constraint(array, space) for array in arrays]


def pack_tiles(at, dst, src, count, tiles, rows, times):
    return pl.pallas_call(
        pack_kernel,
        in_specs=[SMEM, SMEM, SMEM, SMEM, HBM, HBM],
        out_specs=[VMEM] * (len(LENGTHS) + 1),
        out_shape=[pltpu.VMEM((length * TILE + TAIL, TILE), jnp.bfloat16) for length in LENGTHS]
        + [pltpu.VMEM((times,) + rows.shape, rows.dtype)],
        scratch_shapes=[pltpu.SemaphoreType.DMA((len(LENGTHS) + times,))],
        compiler_params=pltpu.CompilerParams(vmem_limit_bytes=VMEM_LIMIT),
        name="pack_tiles",
    )(at, *in_space(pltpu.HBM, dst, src, count, tiles, rows))


def products(held, rows, tiles, sources):
    total = None
    for t in range(0, PAIR, 2):
        sides, chosen = [], []
        for n in (t, t + 1):
            tile = tiles(n)
            empty = jnp.zeros_like(tile)
            sides.append(
                jnp.concatenate(
                    [jnp.where(rows[n] == 0, tile, empty), jnp.where(rows[n] == 1, tile, empty)], axis=0
                )
            )
            chosen.append(sources[pl.ds(pl.multiple_of(held[n] * TILE, TILE), TILE)])
        product = jnp.dot(
            jnp.concatenate(sides, axis=1),
            jnp.concatenate(chosen, axis=0),
            preferred_element_type=jnp.float32,
        )
        total = product if total is None else total + product
    return total


def read_places(messages, tail, tail_s, sem):
    lengths = [message.shape[0] // TILE for message in messages]
    for n, message in enumerate(messages):
        end = message[lengths[n] * TILE : lengths[n] * TILE + TAIL]
        tail[n] = end.astype(jnp.float32).astype(jnp.int32)
    copy = pltpu.make_async_copy(tail, tail_s, sem)
    copy.start()
    copy.wait()
    return [
        [
            (tail_s[n, 0, t], tail_s[n, 1, t], message.at[t * TILE : (t + 1) * TILE])
            for t in range(lengths[n])
        ]
        for n, message in enumerate(messages)
    ]


def write_products(out, tiles, sources):
    held, rows, refs = zip(*tiles)
    out[...] = products(held, rows, lambda n: refs[n][...], sources).astype(jnp.bfloat16)


def sum_near_kernel(at_ref, sources, from_below, from_above, to_below, to_above, *scratch):
    below, above = read_places((from_below, from_above), *scratch)
    write_products(to_below, below, sources)
    write_products(to_above, above, sources)


def sum_far_kernel(at_ref, sources, from_below, from_above, odd, to_below, to_above, *scratch):
    below, above, extra = read_places((from_below, from_above, odd), *scratch)

    def kept(core):
        return [(held, jnp.where(at_ref[0] == core, row, 2), tile) for held, row, tile in extra]

    write_products(to_below, below + kept(1), sources)
    write_products(to_above, above + kept(0), sources)


def sum_away(kernel, at, sources, messages, name):
    rows, channels = sources.shape
    return pl.pallas_call(
        kernel,
        in_specs=[SMEM] + [VMEM] * (1 + len(messages)),
        out_specs=[VMEM] * 2,
        out_shape=[pltpu.VMEM((2 * TILE, channels), jnp.bfloat16)] * 2,
        scratch_shapes=[
            pltpu.VMEM((len(messages), TAIL, TILE), jnp.int32),
            pltpu.SMEM((len(messages), TAIL, TILE), jnp.int32),
            pltpu.SemaphoreType.DMA,
        ],
        compiler_params=pltpu.CompilerParams(vmem_limit_bytes=VMEM_LIMIT),
        cost_estimate=pl.CostEstimate(
            flops=2 * 4 * TILE * TILE * PAIR * channels,
            bytes_accessed=2 * (rows * channels + 2 * PAIR * TILE * TILE),
            transcendentals=0,
        ),
        name=name,
    )(at, *in_space(pltpu.VMEM, sources, *messages))


def sum_own_kernel(at_ref, dst_ref, src_ref, count_ref, sources_ref, tiles_ref, out_ref, *rest):
    tiles, sem = rest
    slots = pair_slots(2, at_ref[0])
    held, placed = places(slots, dst_ref, src_ref, count_ref)
    begin = pl.multiple_of(slots[0][0] * (SLOTS * TILE), SLOTS * TILE)
    copy = pltpu.make_async_copy(tiles_ref.at[pl.ds(begin, PAIR * TILE)], tiles, sem)
    copy.start()
    copy.wait()
    out_ref[...] = products(held, placed, lambda n: tiles[n * TILE : (n + 1) * TILE], sources_ref)


def sum_own(at, dst, src, count, sources, tiles):
    rows, channels = sources.shape
    return pl.pallas_call(
        sum_own_kernel,
        in_specs=[SMEM] * 4 + [VMEM] + [HBM],
        out_specs=VMEM,
        out_shape=jax.ShapeDtypeStruct((2 * TILE, channels), jnp.float32),
        scratch_shapes=[
            pltpu.VMEM((PAIR * TILE, TILE), jnp.bfloat16),
            pltpu.SemaphoreType.DMA,
        ],
        compiler_params=pltpu.CompilerParams(vmem_limit_bytes=VMEM_LIMIT),
        cost_estimate=pl.CostEstimate(
            flops=4 * TILE * TILE * PAIR * channels,
            bytes_accessed=2 * (rows * channels + PAIR * TILE * TILE),
            transcendentals=0,
        ),
        name="sum_own",
    )(
        at,
        *in_space(pltpu.HBM, dst, src, count),
        *in_space(pltpu.VMEM, sources),
        *in_space(pltpu.HBM, tiles),
    )


def join_kernel(left_ref, right_ref, active_ref, own_ref, n0, n1, n2, n3, out_ref):
    total = own_ref[...]
    for part in (n0, n1, n2, n3):
        total = total + part[...].astype(jnp.float32)
    neighbour = total.astype(jnp.bfloat16)
    active = active_ref[...]
    shape = (active.shape[1], left_ref.shape[2])
    channel = lax.broadcasted_iota(jnp.int32, shape, 0).astype(jnp.float32).astype(jnp.bfloat16)
    one, zero = jnp.ones(shape, jnp.bfloat16), jnp.zeros(shape, jnp.bfloat16)
    joined = jnp.zeros((active.shape[0], shape[1]), jnp.float32)
    for j in range(SPLITS):
        left = jnp.where(channel == left_ref[j], one, zero)
        right = jnp.where(channel == right_ref[j], one, zero)
        joined = joined + jnp.dot(active, left, preferred_element_type=jnp.float32) * jnp.dot(
            neighbour, right, preferred_element_type=jnp.float32
        )
    for piece in range(shape[1] // TILE):
        out_ref[piece] = joined[:, piece * TILE : (piece + 1) * TILE].astype(out_ref.dtype)


def join(active, own, parts, left, right):
    rows, channels = own.shape
    splits, _, width = left.shape
    whole = pl.BlockSpec((rows, channels), lambda q: (0, 0))
    columns = pl.BlockSpec((splits, 1, CHUNK), lambda q: (0, 0, q))
    return pl.pallas_call(
        join_kernel,
        grid=(width // CHUNK,),
        in_specs=[columns] * 2 + [whole] * 6,
        out_specs=pl.BlockSpec((CHUNK // TILE, rows, TILE), lambda q: (q, 0, 0)),
        out_shape=jax.ShapeDtypeStruct((width // TILE, rows, TILE), jnp.bfloat16),
        compiler_params=pltpu.CompilerParams(vmem_limit_bytes=VMEM_LIMIT),
        cost_estimate=pl.CostEstimate(
            flops=4 * splits * rows * channels * width,
            bytes_accessed=2 * rows * width,
            transcendentals=0,
        ),
        name="join_sets",
    )(left, right, active, own, *parts)


def local(
    active_table,
    passive_table,
    adjacency,
    tile_dst,
    tile_src,
    tile_count,
    split_active,
    split_passive,
):
    tiles_all = adjacency.reshape(-1, TILE)
    dst, src, count = tile_dst[0, 0].T, tile_src[0, 0].T, tile_count[0, 0]
    nc = lax.axis_size("cset")
    at = (lax.axis_index("blk") % 2).astype(jnp.int32)[None]

    *messages, copies = pack_tiles(at, dst, src, count, tiles_all, passive_table, nc)
    messages = [routed(message, hops) for message, hops in zip(messages, HOPS)]
    own_rows = lax.all_to_all(copies, "cset", split_axis=0, concat_axis=0, tiled=True)
    own_rows = own_rows.reshape(-1, passive_table.shape[1])
    groups = [[b, b + 1] for b in range(0, lax.axis_size("blk"), 2)]
    twice = jnp.broadcast_to(own_rows[None], (2,) + own_rows.shape)
    sources = lax.all_to_all(
        twice, "blk", split_axis=0, concat_axis=0, tiled=True, axis_index_groups=groups
    ).reshape(-1, own_rows.shape[1])

    extra = OUTPAD - split_active.shape[1]
    left, right = (
        jnp.pad(cols.astype(jnp.bfloat16), ((0, 0), (0, extra)), constant_values=-1)[:, None, :]
        for cols in (split_active, split_passive)
    )
    own = sum_own(at, dst, src, count, sources, tiles_all)
    sources, left, right = lax.optimization_barrier((sources, left, right))
    far_up, near_up, near_down, far_down, odd = messages
    far_below, far_above = sum_away(
        sum_far_kernel, at, sources, (far_up, far_down, odd), "sum_far"
    )
    far_below, far_above, sources = lax.optimization_barrier((far_below, far_above, sources))
    near_below, near_above = sum_away(
        sum_near_kernel, at, sources, (near_up, near_down), "sum_near"
    )
    parts = [
        routed(far_above, lambda core: 2),
        routed(far_below, lambda core: -2),
        routed(near_above, lambda core: 1),
        routed(near_below, lambda core: -1),
    ]
    joined = join(active_table, own, parts, left, right)
    spread = lax.all_to_all(joined, "cset", split_axis=0, concat_axis=0, tiled=True)
    return spread.reshape(-1, TILE)


def solution(mesh):
    in_specs = (
        P(("blk", "cset"), None),
        P(("blk", "cset"), None),
        P("blk", "cset", None, None, None, None),
        P("blk", "cset", None, None),
        P("blk", "cset", None, None),
        P("blk", "cset", None),
        P(),
        P(),
    )
    out_specs = P("blk", "cset")
    return jax.shard_map(local, mesh=mesh, in_specs=in_specs, out_specs=out_specs, check_vma=False)
```

```python
import jax
import jax.numpy as jnp
from jax import lax
from jax.experimental import pallas as pl
from jax.experimental.pallas import tpu as pltpu
from jax.sharding import PartitionSpec as P

SPLITS = 20
OUTPAD = 1024
TILE = 128
CHUNK = 512
SLOTS = 8
PAIR = 2 * SLOTS
TAIL = 16
REACH = 9
PART_TILES = 16
VMEM_LIMIT = 16 * 1024 * 1024


def routed(block, hops):
    nb, nc = lax.axis_size("blk"), lax.axis_size("cset")
    route = []
    for b in range(nb):
        chips = hops(b % 2)
        for c in range(nc):
            target = c ^ (nc // 2) if chips % 2 else c
            route.append((b * nc + c, ((b + 2 * chips) % nb) * nc + target))
    return lax.ppermute(block, ("blk", "cset"), route)


def places(slots, dst_ref, src_ref, count_ref):
    held, rows = [], []
    for slot, parity in slots:
        for t in range(SLOTS):
            held.append(src_ref[t, slot] + parity * PART_TILES)
            rows.append(jnp.where(t < count_ref[slot], dst_ref[t, slot], 2))
    return held, rows


def pair_slots(which, core):
    first = 2 * which - core
    return [(first, 0), (first + 1, 1)]


def message_slots(core):
    return [
        [(REACH - 1, core)],
        pair_slots(3, core),
        pair_slots(1, core),
        [(0, core)],
        [(1 + (REACH - 3) * core, 1 - core)],
    ]


HOPS = [
    lambda core: 2,
    lambda core: 1,
    lambda core: -1,
    lambda core: -2,
    lambda core: 4 * core - 2,
]
LENGTHS = [SLOTS, PAIR, PAIR, SLOTS, SLOTS]


def pack_kernel(at_ref, dst_ref, src_ref, count_ref, tiles_ref, rows_ref, *rest):
    outs, (repeated, sems) = rest[: len(HOPS)], rest[len(HOPS) :]
    lane = lax.broadcasted_iota(jnp.int32, (TAIL, TILE), 1)
    line = lax.broadcasted_iota(jnp.int32, (TAIL, TILE), 0)
    slots = message_slots(at_ref[0])
    copies = []
    for n, length in enumerate(LENGTHS):
        begin = pl.multiple_of(slots[n][0][0] * (SLOTS * TILE), SLOTS * TILE)
        copies.append(
            pltpu.make_async_copy(
                tiles_ref.at[pl.ds(begin, length * TILE)],
                outs[n].at[pl.ds(0, length * TILE)],
                sems.at[n],
            )
        )
    for copy in copies:
        copy.start()
    for n in range(repeated.shape[0]):
        repeated[n] = rows_ref[...]
    for n, length in enumerate(LENGTHS):
        held, rows = places(slots[n], dst_ref, src_ref, count_ref)
        tail = jnp.zeros((TAIL, TILE), jnp.int32)
        for t in range(length):
            tail = jnp.where(lane == t, jnp.where(line == 0, held[t], rows[t]), tail)
        outs[n][length * TILE : length * TILE + TAIL] = tail.astype(jnp.float32).astype(jnp.bfloat16)
    for copy in copies:
        copy.wait()


SMEM = pl.BlockSpec(memory_space=pltpu.SMEM)
VMEM = pl.BlockSpec(memory_space=pltpu.VMEM)
ANY = pl.BlockSpec(memory_space=pl.ANY)
HBM = pl.BlockSpec(memory_space=pltpu.HBM)


def in_space(space, *arrays):
    return [pltpu.with_memory_space_constraint(array, space) for array in arrays]


def pack_tiles(at, dst, src, count, tiles, rows, times):
    return pl.pallas_call(
        pack_kernel,
        in_specs=[SMEM, SMEM, SMEM, SMEM, HBM, VMEM],
        out_specs=[VMEM] * (len(LENGTHS) + 1),
        out_shape=[pltpu.VMEM((length * TILE + TAIL, TILE), jnp.bfloat16) for length in LENGTHS]
        + [pltpu.VMEM((times,) + rows.shape, rows.dtype)],
        scratch_shapes=[pltpu.SemaphoreType.DMA((len(LENGTHS),))],
        compiler_params=pltpu.CompilerParams(vmem_limit_bytes=VMEM_LIMIT),
        name="pack_tiles",
    )(at, *in_space(pltpu.HBM, dst, src, count, tiles), rows)


def products(held, rows, tiles, sources):
    total = None
    for t in range(0, PAIR, 2):
        sides, chosen = [], []
        for n in (t, t + 1):
            tile = tiles(n)
            empty = jnp.zeros_like(tile)
            sides.append(
                jnp.concatenate(
                    [jnp.where(rows[n] == 0, tile, empty), jnp.where(rows[n] == 1, tile, empty)], axis=0
                )
            )
            chosen.append(sources[pl.ds(pl.multiple_of(held[n] * TILE, TILE), TILE)])
        product = jnp.dot(
            jnp.concatenate(sides, axis=1),
            jnp.concatenate(chosen, axis=0),
            preferred_element_type=jnp.float32,
        )
        total = product if total is None else total + product
    return total


def read_places(messages, tail, tail_s, sem):
    lengths = [message.shape[0] // TILE for message in messages]
    for n, message in enumerate(messages):
        end = message[lengths[n] * TILE : lengths[n] * TILE + TAIL]
        tail[n] = end.astype(jnp.float32).astype(jnp.int32)
    copy = pltpu.make_async_copy(tail, tail_s, sem)
    copy.start()
    copy.wait()
    return [
        [
            (tail_s[n, 0, t], tail_s[n, 1, t], message.at[t * TILE : (t + 1) * TILE])
            for t in range(lengths[n])
        ]
        for n, message in enumerate(messages)
    ]


def write_products(out, tiles, sources):
    held, rows, refs = zip(*tiles)
    out[...] = products(held, rows, lambda n: refs[n][...], sources).astype(jnp.bfloat16)


def sum_near_kernel(at_ref, sources, from_below, from_above, to_below, to_above, *scratch):
    below, above = read_places((from_below, from_above), *scratch)
    write_products(to_below, below, sources)
    write_products(to_above, above, sources)


def sum_far_kernel(at_ref, sources, from_below, from_above, odd, to_below, to_above, *scratch):
    below, above, extra = read_places((from_below, from_above, odd), *scratch)

    def kept(core):
        return [(held, jnp.where(at_ref[0] == core, row, 2), tile) for held, row, tile in extra]

    write_products(to_below, below + kept(1), sources)
    write_products(to_above, above + kept(0), sources)


def sum_away(kernel, at, sources, messages, name):
    rows, channels = sources.shape
    return pl.pallas_call(
        kernel,
        in_specs=[SMEM] + [VMEM] * (1 + len(messages)),
        out_specs=[VMEM] * 2,
        out_shape=[pltpu.VMEM((2 * TILE, channels), jnp.bfloat16)] * 2,
        scratch_shapes=[
            pltpu.VMEM((len(messages), TAIL, TILE), jnp.int32),
            pltpu.SMEM((len(messages), TAIL, TILE), jnp.int32),
            pltpu.SemaphoreType.DMA,
        ],
        compiler_params=pltpu.CompilerParams(vmem_limit_bytes=VMEM_LIMIT),
        cost_estimate=pl.CostEstimate(
            flops=2 * 4 * TILE * TILE * PAIR * channels,
            bytes_accessed=2 * (rows * channels + 2 * PAIR * TILE * TILE),
            transcendentals=0,
        ),
        name=name,
    )(at, *in_space(pltpu.VMEM, sources, *messages))


def sum_own_kernel(at_ref, dst_ref, src_ref, count_ref, sources_ref, tiles_ref, out_ref, *rest):
    tiles, sem = rest
    slots = pair_slots(2, at_ref[0])
    held, placed = places(slots, dst_ref, src_ref, count_ref)
    begin = pl.multiple_of(slots[0][0] * (SLOTS * TILE), SLOTS * TILE)
    copy = pltpu.make_async_copy(tiles_ref.at[pl.ds(begin, PAIR * TILE)], tiles, sem)
    copy.start()
    copy.wait()
    out_ref[...] = products(held, placed, lambda n: tiles[n * TILE : (n + 1) * TILE], sources_ref)


def sum_own(at, dst, src, count, sources, tiles):
    rows, channels = sources.shape
    return pl.pallas_call(
        sum_own_kernel,
        in_specs=[SMEM] * 4 + [VMEM] + [HBM],
        out_specs=VMEM,
        out_shape=jax.ShapeDtypeStruct((2 * TILE, channels), jnp.float32),
        scratch_shapes=[
            pltpu.VMEM((PAIR * TILE, TILE), jnp.bfloat16),
            pltpu.SemaphoreType.DMA,
        ],
        compiler_params=pltpu.CompilerParams(vmem_limit_bytes=VMEM_LIMIT),
        cost_estimate=pl.CostEstimate(
            flops=4 * TILE * TILE * PAIR * channels,
            bytes_accessed=2 * (rows * channels + PAIR * TILE * TILE),
            transcendentals=0,
        ),
        name="sum_own",
    )(
        at,
        dst,
        src,
        count,
        *in_space(pltpu.VMEM, sources),
        tiles,
    )


def onehot(columns, channels):
    shape = (channels, columns.shape[1])
    channel = lax.broadcasted_iota(jnp.int32, shape, 0).astype(jnp.float32).astype(jnp.bfloat16)
    one, zero = jnp.ones(shape, jnp.bfloat16), jnp.zeros(shape, jnp.bfloat16)
    return jnp.where(channel == columns, one, zero)


def columns_kernel(left_ref, right_ref, left_out, right_out):
    for ref, out in ((left_ref, left_out), (right_ref, right_out)):
        out[...] = jnp.full(out.shape, -1, jnp.bfloat16)
        for j in range(SPLITS):
            row = ref[j : j + 1].astype(jnp.float32).astype(jnp.bfloat16)
            out[j, :, : ref.shape[1]] = row


def as_columns(left, right):
    return pl.pallas_call(
        columns_kernel,
        in_specs=[VMEM] * 2,
        out_specs=[VMEM] * 2,
        out_shape=[pltpu.VMEM((SPLITS, 1, OUTPAD), jnp.bfloat16)] * 2,
        compiler_params=pltpu.CompilerParams(vmem_limit_bytes=VMEM_LIMIT),
        name="as_columns",
    )(left, right)


def pick_kernel(columns_ref, table_ref, out_ref):
    table = table_ref[...]
    for j in range(SPLITS):
        for begin in range(0, out_ref.shape[2], CHUNK):
            part = slice(begin, begin + CHUNK)
            picked = jnp.dot(
                table,
                onehot(columns_ref[j, :, part], table.shape[1]),
                preferred_element_type=jnp.float32,
            )
            out_ref[j, :, part] = picked.astype(jnp.bfloat16)


def pick_columns(table, columns):
    rows, channels = table.shape
    splits, _, width = columns.shape
    return pl.pallas_call(
        pick_kernel,
        in_specs=[VMEM] * 2,
        out_specs=VMEM,
        out_shape=pltpu.VMEM((splits, rows, width), jnp.bfloat16),
        compiler_params=pltpu.CompilerParams(vmem_limit_bytes=VMEM_LIMIT),
        cost_estimate=pl.CostEstimate(
            flops=2 * splits * rows * channels * width,
            bytes_accessed=2 * splits * rows * width,
            transcendentals=0,
        ),
        name="pick_active",
    )(columns, table)


def join_kernel(columns_ref, picked_ref, own_ref, n0, n1, n2, n3, out_ref):
    total = own_ref[...]
    for part in (n0, n1, n2, n3):
        total = total + part[...].astype(jnp.float32)
    neighbour = total.astype(jnp.bfloat16)
    rows, channels = neighbour.shape
    for begin in range(0, picked_ref.shape[2], CHUNK):
        part = slice(begin, begin + CHUNK)
        joined = jnp.zeros((rows, CHUNK), jnp.float32)
        for j in range(SPLITS):
            joined = joined + picked_ref[j, :, part].astype(jnp.float32) * jnp.dot(
                neighbour,
                onehot(columns_ref[j, :, part], channels),
                preferred_element_type=jnp.float32,
            )
        for piece in range(CHUNK // TILE):
            out_ref[begin // TILE + piece] = joined[:, piece * TILE : (piece + 1) * TILE].astype(
                out_ref.dtype
            )


def join(picked, own, parts, columns):
    splits, rows, width = picked.shape
    channels = own.shape[1]
    return pl.pallas_call(
        join_kernel,
        in_specs=[VMEM] * 7,
        out_specs=VMEM,
        out_shape=pltpu.VMEM((width // TILE, rows, TILE), jnp.bfloat16),
        compiler_params=pltpu.CompilerParams(vmem_limit_bytes=VMEM_LIMIT),
        cost_estimate=pl.CostEstimate(
            flops=2 * splits * rows * channels * width,
            bytes_accessed=2 * rows * width,
            transcendentals=0,
        ),
        name="join_sets",
    )(columns, *in_space(pltpu.VMEM, picked, own, *parts))


def local(
    active_table,
    passive_table,
    adjacency,
    tile_dst,
    tile_src,
    tile_count,
    split_active,
    split_passive,
):
    tiles_all = adjacency.reshape(-1, TILE)
    dst, src, count = tile_dst[0, 0].T, tile_src[0, 0].T, tile_count[0, 0]
    nc = lax.axis_size("cset")
    at = (lax.axis_index("blk") % 2).astype(jnp.int32)[None]

    *messages, copies = pack_tiles(at, dst, src, count, tiles_all, passive_table, nc)
    messages = [routed(message, hops) for message, hops in zip(messages, HOPS)]
    own_rows = lax.all_to_all(copies, "cset", split_axis=0, concat_axis=0, tiled=True)
    own_rows = own_rows.reshape(-1, passive_table.shape[1])
    groups = [[b, b + 1] for b in range(0, lax.axis_size("blk"), 2)]
    twice = jnp.broadcast_to(own_rows[None], (2,) + own_rows.shape)
    sources = lax.all_to_all(
        twice, "blk", split_axis=0, concat_axis=0, tiled=True, axis_index_groups=groups
    ).reshape(-1, own_rows.shape[1])

    left, right = as_columns(split_active, split_passive)
    own = sum_own(at, dst, src, count, sources, tiles_all)
    sources, own, left, right = lax.optimization_barrier((sources, own, left, right))
    far_up, near_up, near_down, far_down, odd = messages
    far_below, far_above = sum_away(
        sum_far_kernel, at, sources, (far_up, far_down, odd), "sum_far"
    )
    far_below, far_above, sources = lax.optimization_barrier((far_below, far_above, sources))
    near_below, near_above = sum_away(
        sum_near_kernel, at, sources, (near_up, near_down), "sum_near"
    )
    near_below, near_above, left = lax.optimization_barrier((near_below, near_above, left))
    picked = pick_columns(active_table, left)
    parts = [
        routed(far_above, lambda core: 2),
        routed(far_below, lambda core: -2),
        routed(near_above, lambda core: 1),
        routed(near_below, lambda core: -1),
    ]
    joined = join(picked, own, parts, right)
    spread = lax.all_to_all(joined, "cset", split_axis=0, concat_axis=0, tiled=True)
    return spread.reshape(-1, TILE)


def solution(mesh):
    in_specs = (
        P(("blk", "cset"), None),
        P(("blk", "cset"), None),
        P("blk", "cset", None, None, None, None),
        P("blk", "cset", None, None),
        P("blk", "cset", None, None),
        P("blk", "cset", None),
        P(),
        P(),
    )
    out_specs = P("blk", "cset")
    return jax.shard_map(local, mesh=mesh, in_specs=in_specs, out_specs=out_specs, check_vma=False)
```

```python
import jax
import jax.numpy as jnp
from jax import lax
from jax.experimental import pallas as pl
from jax.experimental.pallas import tpu as pltpu
from jax.sharding import PartitionSpec as P

SPLITS = 20
OUTPAD = 1024
TILE = 128
CHUNK = 512
SLOTS = 8
PAIR = 2 * SLOTS
TAIL = 16
REACH = 9
PART_TILES = 16
VMEM_LIMIT = 16 * 1024 * 1024


def routed(block, hops):
    nb, nc = lax.axis_size("blk"), lax.axis_size("cset")
    route = []
    for b in range(nb):
        chips = hops(b % 2)
        for c in range(nc):
            target = c ^ (nc // 2) if chips % 2 else c
            route.append((b * nc + c, ((b + 2 * chips) % nb) * nc + target))
    return lax.ppermute(block, ("blk", "cset"), route)


def places(slots, dst_ref, src_ref, count_ref):
    held, rows = [], []
    for slot, parity in slots:
        for t in range(SLOTS):
            held.append(src_ref[t, slot] + parity * PART_TILES)
            rows.append(jnp.where(t < count_ref[slot], dst_ref[t, slot], 2))
    return held, rows


def pair_slots(which, core):
    first = 2 * which - core
    return [(first, 0), (first + 1, 1)]


def message_slots(core):
    return [
        pair_slots(3, core),
        pair_slots(1, core),
        [(REACH - 1, core)],
        [(0, core)],
        [(1 + (REACH - 3) * core, 1 - core)],
    ]


HOPS = [
    lambda core: 1,
    lambda core: -1,
    lambda core: 2,
    lambda core: -2,
    lambda core: 4 * core - 2,
]
LENGTHS = [PAIR, PAIR, SLOTS, SLOTS, SLOTS]


def pack_kernel(at_ref, dst_ref, src_ref, count_ref, tiles_ref, *rest):
    outs, sems = rest[: len(HOPS)], rest[len(HOPS)]
    lane = lax.broadcasted_iota(jnp.int32, (TAIL, TILE), 1)
    line = lax.broadcasted_iota(jnp.int32, (TAIL, TILE), 0)
    slots = message_slots(at_ref[0])
    copies = []
    for n, length in enumerate(LENGTHS):
        begin = pl.multiple_of(slots[n][0][0] * (SLOTS * TILE), SLOTS * TILE)
        copies.append(
            pltpu.make_async_copy(
                tiles_ref.at[pl.ds(begin, length * TILE)],
                outs[n].at[pl.ds(0, length * TILE)],
                sems.at[n],
            )
        )
    for copy in copies:
        copy.start()
    for n, length in enumerate(LENGTHS):
        held, rows = places(slots[n], dst_ref, src_ref, count_ref)
        tail = jnp.zeros((TAIL, TILE), jnp.int32)
        for t in range(length):
            tail = jnp.where(lane == t, jnp.where(line == 0, held[t], rows[t]), tail)
        outs[n][length * TILE : length * TILE + TAIL] = tail.astype(jnp.float32).astype(jnp.bfloat16)
    for copy in copies:
        copy.wait()


SMEM = pl.BlockSpec(memory_space=pltpu.SMEM)
VMEM = pl.BlockSpec(memory_space=pltpu.VMEM)
ANY = pl.BlockSpec(memory_space=pl.ANY)
HBM = pl.BlockSpec(memory_space=pltpu.HBM)


def in_space(space, *arrays):
    return [pltpu.with_memory_space_constraint(array, space) for array in arrays]


def pack_tiles(at, dst, src, count, tiles):
    return pl.pallas_call(
        pack_kernel,
        in_specs=[SMEM, SMEM, SMEM, SMEM, HBM],
        out_specs=[VMEM] * len(LENGTHS),
        out_shape=[pltpu.VMEM((length * TILE + TAIL, TILE), jnp.bfloat16) for length in LENGTHS],
        scratch_shapes=[pltpu.SemaphoreType.DMA((len(LENGTHS),))],
        compiler_params=pltpu.CompilerParams(vmem_limit_bytes=VMEM_LIMIT),
        name="pack_tiles",
    )(at, *in_space(pltpu.HBM, dst, src, count, tiles))


def products(held, rows, tiles, sources):
    total = None
    for t in range(0, PAIR, 2):
        sides, chosen = [], []
        for n in (t, t + 1):
            tile = tiles(n)
            empty = jnp.zeros_like(tile)
            sides.append(
                jnp.concatenate(
                    [jnp.where(rows[n] == 0, tile, empty), jnp.where(rows[n] == 1, tile, empty)], axis=0
                )
            )
            chosen.append(sources[pl.ds(pl.multiple_of(held[n] * TILE, TILE), TILE)])
        product = jnp.dot(
            jnp.concatenate(sides, axis=1),
            jnp.concatenate(chosen, axis=0),
            preferred_element_type=jnp.float32,
        )
        total = product if total is None else total + product
    return total


def read_places(messages, tail, tail_s, sem):
    lengths = [message.shape[0] // TILE for message in messages]
    for n, message in enumerate(messages):
        end = message[lengths[n] * TILE : lengths[n] * TILE + TAIL]
        tail[n] = end.astype(jnp.float32).astype(jnp.int32)
    copy = pltpu.make_async_copy(tail, tail_s, sem)
    copy.start()
    copy.wait()
    return [
        [
            (tail_s[n, 0, t], tail_s[n, 1, t], message.at[t * TILE : (t + 1) * TILE])
            for t in range(lengths[n])
        ]
        for n, message in enumerate(messages)
    ]


def write_products(out, tiles, sources):
    held, rows, refs = zip(*tiles)
    out[...] = products(held, rows, lambda n: refs[n][...], sources).astype(jnp.bfloat16)


def sum_near_kernel(at_ref, sources, from_below, from_above, to_below, to_above, *scratch):
    below, above = read_places((from_below, from_above), *scratch)
    write_products(to_below, below, sources)
    write_products(to_above, above, sources)


def sum_far_kernel(at_ref, sources, from_below, from_above, odd, to_below, to_above, *scratch):
    below, above, extra = read_places((from_below, from_above, odd), *scratch)

    def kept(core):
        return [(held, jnp.where(at_ref[0] == core, row, 2), tile) for held, row, tile in extra]

    write_products(to_below, below + kept(1), sources)
    write_products(to_above, above + kept(0), sources)


def sum_away(kernel, at, sources, messages, name):
    rows, channels = sources.shape
    return pl.pallas_call(
        kernel,
        in_specs=[SMEM] + [VMEM] * (1 + len(messages)),
        out_specs=[VMEM] * 2,
        out_shape=[pltpu.VMEM((2 * TILE, channels), jnp.bfloat16)] * 2,
        scratch_shapes=[
            pltpu.VMEM((len(messages), TAIL, TILE), jnp.int32),
            pltpu.SMEM((len(messages), TAIL, TILE), jnp.int32),
            pltpu.SemaphoreType.DMA,
        ],
        compiler_params=pltpu.CompilerParams(vmem_limit_bytes=VMEM_LIMIT),
        cost_estimate=pl.CostEstimate(
            flops=2 * 4 * TILE * TILE * PAIR * channels,
            bytes_accessed=2 * (rows * channels + 2 * PAIR * TILE * TILE),
            transcendentals=0,
        ),
        name=name,
    )(at, *in_space(pltpu.VMEM, sources, *messages))


def sum_own_kernel(at_ref, dst_ref, src_ref, count_ref, sources_ref, tiles_ref, out_ref, *rest):
    tiles, sem = rest
    slots = pair_slots(2, at_ref[0])
    held, placed = places(slots, dst_ref, src_ref, count_ref)
    begin = pl.multiple_of(slots[0][0] * (SLOTS * TILE), SLOTS * TILE)
    copy = pltpu.make_async_copy(tiles_ref.at[pl.ds(begin, PAIR * TILE)], tiles, sem)
    copy.start()
    copy.wait()
    out_ref[...] = products(held, placed, lambda n: tiles[n * TILE : (n + 1) * TILE], sources_ref)


def sum_own(at, dst, src, count, sources, tiles):
    rows, channels = sources.shape
    return pl.pallas_call(
        sum_own_kernel,
        in_specs=[SMEM] * 4 + [VMEM] + [HBM],
        out_specs=VMEM,
        out_shape=jax.ShapeDtypeStruct((2 * TILE, channels), jnp.float32),
        scratch_shapes=[
            pltpu.VMEM((PAIR * TILE, TILE), jnp.bfloat16),
            pltpu.SemaphoreType.DMA,
        ],
        compiler_params=pltpu.CompilerParams(vmem_limit_bytes=VMEM_LIMIT),
        cost_estimate=pl.CostEstimate(
            flops=4 * TILE * TILE * PAIR * channels,
            bytes_accessed=2 * (rows * channels + PAIR * TILE * TILE),
            transcendentals=0,
        ),
        name="sum_own",
    )(
        at,
        dst,
        src,
        count,
        *in_space(pltpu.VMEM, sources),
        tiles,
    )


def onehot(columns, channels):
    shape = (channels, columns.shape[1])
    channel = lax.broadcasted_iota(jnp.int32, shape, 0).astype(jnp.float32).astype(jnp.bfloat16)
    one, zero = jnp.ones(shape, jnp.bfloat16), jnp.zeros(shape, jnp.bfloat16)
    return jnp.where(channel == columns, one, zero)


def columns_kernel(left_ref, right_ref, left_out, right_out):
    for ref, out in ((left_ref, left_out), (right_ref, right_out)):
        out[...] = jnp.full(out.shape, -1, jnp.bfloat16)
        for j in range(SPLITS):
            row = ref[j : j + 1].astype(jnp.float32).astype(jnp.bfloat16)
            out[j, :, : ref.shape[1]] = row


def as_columns(left, right):
    return pl.pallas_call(
        columns_kernel,
        in_specs=[VMEM] * 2,
        out_specs=[VMEM] * 2,
        out_shape=[pltpu.VMEM((SPLITS, 1, OUTPAD), jnp.bfloat16)] * 2,
        compiler_params=pltpu.CompilerParams(vmem_limit_bytes=VMEM_LIMIT),
        cost_estimate=pl.CostEstimate(flops=10000000000, bytes_accessed=1, transcendentals=0),
        name="as_columns",
    )(left, right)


def pick_kernel(columns_ref, table_ref, out_ref):
    table = table_ref[...]
    for j in range(SPLITS):
        for begin in range(0, out_ref.shape[2], CHUNK):
            part = slice(begin, begin + CHUNK)
            picked = jnp.dot(
                table,
                onehot(columns_ref[j, :, part], table.shape[1]),
                preferred_element_type=jnp.float32,
            )
            out_ref[j, :, part] = picked.astype(jnp.bfloat16)


def pick_columns(table, columns):
    rows, channels = table.shape
    splits, _, width = columns.shape
    return pl.pallas_call(
        pick_kernel,
        in_specs=[VMEM] * 2,
        out_specs=VMEM,
        out_shape=pltpu.VMEM((splits, rows, width), jnp.bfloat16),
        compiler_params=pltpu.CompilerParams(vmem_limit_bytes=VMEM_LIMIT),
        cost_estimate=pl.CostEstimate(
            flops=2 * splits * rows * channels * width,
            bytes_accessed=2 * splits * rows * width,
            transcendentals=0,
        ),
        name="pick_active",
    )(columns, table)


def join_kernel(columns_ref, picked_ref, own_ref, n0, n1, n2, n3, out_ref):
    total = own_ref[...]
    for part in (n0, n1, n2, n3):
        total = total + part[...].astype(jnp.float32)
    neighbour = total.astype(jnp.bfloat16)
    rows, channels = neighbour.shape
    for begin in range(0, picked_ref.shape[2], CHUNK):
        part = slice(begin, begin + CHUNK)
        joined = jnp.zeros((rows, CHUNK), jnp.float32)
        for j in range(SPLITS):
            joined = joined + picked_ref[j, :, part].astype(jnp.float32) * jnp.dot(
                neighbour,
                onehot(columns_ref[j, :, part], channels),
                preferred_element_type=jnp.float32,
            )
        for piece in range(CHUNK // TILE):
            out_ref[begin // TILE + piece] = joined[:, piece * TILE : (piece + 1) * TILE].astype(
                out_ref.dtype
            )


def join(picked, own, parts, columns):
    splits, rows, width = picked.shape
    channels = own.shape[1]
    return pl.pallas_call(
        join_kernel,
        in_specs=[VMEM] * 7,
        out_specs=VMEM,
        out_shape=pltpu.VMEM((width // TILE, rows, TILE), jnp.bfloat16),
        compiler_params=pltpu.CompilerParams(vmem_limit_bytes=VMEM_LIMIT),
        cost_estimate=pl.CostEstimate(
            flops=2 * splits * rows * channels * width,
            bytes_accessed=2 * rows * width,
            transcendentals=0,
        ),
        name="join_sets",
    )(columns, *in_space(pltpu.VMEM, picked, own, *parts))


def local(
    active_table,
    passive_table,
    adjacency,
    tile_dst,
    tile_src,
    tile_count,
    split_active,
    split_passive,
):
    tiles_all = adjacency.reshape(-1, TILE)
    dst, src, count = tile_dst[0, 0].T, tile_src[0, 0].T, tile_count[0, 0]
    nc = lax.axis_size("cset")
    at = (lax.axis_index("blk") % 2).astype(jnp.int32)[None]

    messages = pack_tiles(at, dst, src, count, tiles_all)
    *messages, passive_table = lax.optimization_barrier((*messages, passive_table))
    messages = [routed(message, hops) for message, hops in zip(messages, HOPS)]
    copies = jnp.broadcast_to(passive_table[None], (nc,) + passive_table.shape)
    own_rows = lax.all_to_all(copies, "cset", split_axis=0, concat_axis=0, tiled=True)
    own_rows = own_rows.reshape(-1, passive_table.shape[1])
    groups = [[b, b + 1] for b in range(0, lax.axis_size("blk"), 2)]
    twice = jnp.broadcast_to(own_rows[None], (2,) + own_rows.shape)
    sources = lax.all_to_all(
        twice, "blk", split_axis=0, concat_axis=0, tiled=True, axis_index_groups=groups
    ).reshape(-1, own_rows.shape[1])

    left, right = as_columns(split_active, split_passive)
    own = sum_own(at, dst, src, count, sources, tiles_all)
    sources, own, left, right = lax.optimization_barrier((sources, own, left, right))
    near_up, near_down, far_up, far_down, odd = messages
    far_below, far_above = sum_away(
        sum_far_kernel, at, sources, (far_up, far_down, odd), "sum_far"
    )
    far_below, far_above, sources = lax.optimization_barrier((far_below, far_above, sources))
    near_below, near_above = sum_away(
        sum_near_kernel, at, sources, (near_up, near_down), "sum_near"
    )
    near_below, near_above, left = lax.optimization_barrier((near_below, near_above, left))
    picked = pick_columns(active_table, left)
    parts = [
        routed(far_above, lambda core: 2),
        routed(far_below, lambda core: -2),
        routed(near_above, lambda core: 1),
        routed(near_below, lambda core: -1),
    ]
    joined = join(picked, own, parts, right)
    spread = lax.all_to_all(joined, "cset", split_axis=0, concat_axis=0, tiled=True)
    return spread.reshape(-1, TILE)


def solution(mesh):
    in_specs = (
        P(("blk", "cset"), None),
        P(("blk", "cset"), None),
        P("blk", "cset", None, None, None, None),
        P("blk", "cset", None, None),
        P("blk", "cset", None, None),
        P("blk", "cset", None),
        P(),
        P(),
    )
    out_specs = P("blk", "cset")
    return jax.shard_map(local, mesh=mesh, in_specs=in_specs, out_specs=out_specs, check_vma=False)
```

```python
import functools

import jax
import jax.numpy as jnp
from jax import lax
from jax.experimental import pallas as pl
from jax.experimental.pallas import tpu as pltpu
from jax.sharding import PartitionSpec as P

SPLITS = 20
OUTPAD = 1024
TILE = 128
CHUNK = 512
SLOTS = 8
PAIR = 2 * SLOTS
TAIL = 16
REACH = 9
PART_TILES = 16
VMEM_LIMIT = 16 * 1024 * 1024


def routed(block, hops):
    nb, nc = lax.axis_size("blk"), lax.axis_size("cset")
    route = []
    for b in range(nb):
        chips = hops(b % 2)
        for c in range(nc):
            target = c ^ (nc // 2) if chips % 2 else c
            route.append((b * nc + c, ((b + 2 * chips) % nb) * nc + target))
    return lax.ppermute(block, ("blk", "cset"), route)


def places(slots, dst_ref, src_ref, count_ref):
    held, rows = [], []
    for slot, parity in slots:
        for t in range(SLOTS):
            held.append(src_ref[t, slot] + parity * PART_TILES)
            rows.append(jnp.where(t < count_ref[slot], dst_ref[t, slot], 2))
    return held, rows


def pair_slots(which, core):
    first = 2 * which - core
    return [(first, 0), (first + 1, 1)]


def message_slots(core):
    return [
        pair_slots(3, core),
        pair_slots(1, core),
        [(REACH - 1, core)],
        [(0, core)],
        [(1 + (REACH - 3) * core, 1 - core)],
    ]


HOPS = [
    lambda core: 1,
    lambda core: -1,
    lambda core: 2,
    lambda core: -2,
    lambda core: 4 * core - 2,
]
LENGTHS = [PAIR, PAIR, SLOTS, SLOTS, SLOTS]


def pack_kernel(which, at_ref, dst_ref, src_ref, count_ref, tiles_ref, *rest):
    outs, sems = rest[: len(which)], rest[len(which)]
    lengths = [LENGTHS[n] for n in which]
    lane = lax.broadcasted_iota(jnp.int32, (TAIL, TILE), 1)
    line = lax.broadcasted_iota(jnp.int32, (TAIL, TILE), 0)
    slots = [message_slots(at_ref[0])[n] for n in which]
    copies = []
    for n, length in enumerate(lengths):
        begin = pl.multiple_of(slots[n][0][0] * (SLOTS * TILE), SLOTS * TILE)
        copies.append(
            pltpu.make_async_copy(
                tiles_ref.at[pl.ds(begin, length * TILE)],
                outs[n].at[pl.ds(0, length * TILE)],
                sems.at[n],
            )
        )
    for copy in copies:
        copy.start()
    for n, length in enumerate(lengths):
        held, rows = places(slots[n], dst_ref, src_ref, count_ref)
        tail = jnp.zeros((TAIL, TILE), jnp.int32)
        for t in range(length):
            tail = jnp.where(lane == t, jnp.where(line == 0, held[t], rows[t]), tail)
        outs[n][length * TILE : length * TILE + TAIL] = tail.astype(jnp.float32).astype(jnp.bfloat16)
    for copy in copies:
        copy.wait()


SMEM = pl.BlockSpec(memory_space=pltpu.SMEM)
VMEM = pl.BlockSpec(memory_space=pltpu.VMEM)
ANY = pl.BlockSpec(memory_space=pl.ANY)
HBM = pl.BlockSpec(memory_space=pltpu.HBM)


def in_space(space, *arrays):
    return [pltpu.with_memory_space_constraint(array, space) for array in arrays]


def pack_tiles(which, at, dst, src, count, tiles, name):
    shapes = [(LENGTHS[n] * TILE + TAIL, TILE) for n in which]
    return pl.pallas_call(
        functools.partial(pack_kernel, which),
        in_specs=[SMEM, SMEM, SMEM, SMEM, HBM],
        out_specs=[VMEM] * len(which),
        out_shape=[pltpu.VMEM(shape, jnp.bfloat16) for shape in shapes],
        scratch_shapes=[pltpu.SemaphoreType.DMA((len(which),))],
        compiler_params=pltpu.CompilerParams(vmem_limit_bytes=VMEM_LIMIT),
        cost_estimate=pl.CostEstimate(
            flops=0, bytes_accessed=sum(2 * rows * cols for rows, cols in shapes), transcendentals=0
        ),
        name=name,
    )(at, *in_space(pltpu.HBM, dst, src, count, tiles))


def products(held, rows, tiles, sources):
    total = None
    for t in range(0, PAIR, 2):
        sides, chosen = [], []
        for n in (t, t + 1):
            tile = tiles(n)
            empty = jnp.zeros_like(tile)
            sides.append(
                jnp.concatenate(
                    [jnp.where(rows[n] == 0, tile, empty), jnp.where(rows[n] == 1, tile, empty)], axis=0
                )
            )
            chosen.append(sources[pl.ds(pl.multiple_of(held[n] * TILE, TILE), TILE)])
        product = jnp.dot(
            jnp.concatenate(sides, axis=1),
            jnp.concatenate(chosen, axis=0),
            preferred_element_type=jnp.float32,
        )
        total = product if total is None else total + product
    return total


def read_places(messages, tail, tail_s, sem):
    lengths = [message.shape[0] // TILE for message in messages]
    for n, message in enumerate(messages):
        end = message[lengths[n] * TILE : lengths[n] * TILE + TAIL]
        tail[n] = end.astype(jnp.float32).astype(jnp.int32)
    copy = pltpu.make_async_copy(tail, tail_s, sem)
    copy.start()
    copy.wait()
    return [
        [
            (tail_s[n, 0, t], tail_s[n, 1, t], message.at[t * TILE : (t + 1) * TILE])
            for t in range(lengths[n])
        ]
        for n, message in enumerate(messages)
    ]


def write_products(out, tiles, sources):
    held, rows, refs = zip(*tiles)
    out[...] = products(held, rows, lambda n: refs[n][...], sources).astype(jnp.bfloat16)


def sum_near_kernel(at_ref, sources, from_below, from_above, to_below, to_above, *scratch):
    below, above = read_places((from_below, from_above), *scratch)
    write_products(to_below, below, sources)
    write_products(to_above, above, sources)


def sum_far_kernel(at_ref, sources, from_below, from_above, odd, to_below, to_above, *scratch):
    below, above, extra = read_places((from_below, from_above, odd), *scratch)

    def kept(core):
        return [(held, jnp.where(at_ref[0] == core, row, 2), tile) for held, row, tile in extra]

    write_products(to_below, below + kept(1), sources)
    write_products(to_above, above + kept(0), sources)


def sum_away(kernel, at, sources, messages, name):
    rows, channels = sources.shape
    return pl.pallas_call(
        kernel,
        in_specs=[SMEM] + [VMEM] * (1 + len(messages)),
        out_specs=[VMEM] * 2,
        out_shape=[pltpu.VMEM((2 * TILE, channels), jnp.bfloat16)] * 2,
        scratch_shapes=[
            pltpu.VMEM((len(messages), TAIL, TILE), jnp.int32),
            pltpu.SMEM((len(messages), TAIL, TILE), jnp.int32),
            pltpu.SemaphoreType.DMA,
        ],
        compiler_params=pltpu.CompilerParams(vmem_limit_bytes=VMEM_LIMIT),
        cost_estimate=pl.CostEstimate(
            flops=2 * 4 * TILE * TILE * PAIR * channels,
            bytes_accessed=2 * (rows * channels + 2 * PAIR * TILE * TILE),
            transcendentals=0,
        ),
        name=name,
    )(at, *in_space(pltpu.VMEM, sources, *messages))


def sum_own_kernel(at_ref, dst_ref, src_ref, count_ref, sources_ref, tiles_ref, out_ref, *rest):
    tiles, sem = rest
    slots = pair_slots(2, at_ref[0])
    held, placed = places(slots, dst_ref, src_ref, count_ref)
    begin = pl.multiple_of(slots[0][0] * (SLOTS * TILE), SLOTS * TILE)
    copy = pltpu.make_async_copy(tiles_ref.at[pl.ds(begin, PAIR * TILE)], tiles, sem)
    copy.start()
    copy.wait()
    out_ref[...] = products(held, placed, lambda n: tiles[n * TILE : (n + 1) * TILE], sources_ref)


def sum_own(at, dst, src, count, sources, tiles):
    rows, channels = sources.shape
    return pl.pallas_call(
        sum_own_kernel,
        in_specs=[SMEM] * 4 + [VMEM] + [HBM],
        out_specs=VMEM,
        out_shape=jax.ShapeDtypeStruct((2 * TILE, channels), jnp.float32),
        scratch_shapes=[
            pltpu.VMEM((PAIR * TILE, TILE), jnp.bfloat16),
            pltpu.SemaphoreType.DMA,
        ],
        compiler_params=pltpu.CompilerParams(vmem_limit_bytes=VMEM_LIMIT),
        cost_estimate=pl.CostEstimate(
            flops=4 * TILE * TILE * PAIR * channels,
            bytes_accessed=2 * (rows * channels + PAIR * TILE * TILE),
            transcendentals=0,
        ),
        name="sum_own",
    )(
        at,
        dst,
        src,
        count,
        *in_space(pltpu.VMEM, sources),
        tiles,
    )


def onehot(columns, channels):
    shape = (channels, columns.shape[1])
    channel = lax.broadcasted_iota(jnp.int32, shape, 0).astype(jnp.float32).astype(jnp.bfloat16)
    one, zero = jnp.ones(shape, jnp.bfloat16), jnp.zeros(shape, jnp.bfloat16)
    return jnp.where(channel == columns, one, zero)


def columns_kernel(left_ref, right_ref, left_out, right_out):
    for ref, out in ((left_ref, left_out), (right_ref, right_out)):
        out[...] = jnp.full(out.shape, -1, jnp.bfloat16)
        for j in range(SPLITS):
            row = ref[j : j + 1].astype(jnp.float32).astype(jnp.bfloat16)
            out[j, :, : ref.shape[1]] = row


def as_columns(left, right):
    return pl.pallas_call(
        columns_kernel,
        in_specs=[VMEM] * 2,
        out_specs=[VMEM] * 2,
        out_shape=[pltpu.VMEM((SPLITS, 1, OUTPAD), jnp.bfloat16)] * 2,
        compiler_params=pltpu.CompilerParams(vmem_limit_bytes=VMEM_LIMIT),
        cost_estimate=pl.CostEstimate(flops=10000000000, bytes_accessed=1, transcendentals=0),
        name="as_columns",
    )(left, right)


def pick_kernel(columns_ref, table_ref, out_ref):
    table = table_ref[...]
    for j in range(SPLITS):
        for begin in range(0, out_ref.shape[2], CHUNK):
            part = slice(begin, begin + CHUNK)
            picked = jnp.dot(
                table,
                onehot(columns_ref[j, :, part], table.shape[1]),
                preferred_element_type=jnp.float32,
            )
            out_ref[j, :, part] = picked.astype(jnp.bfloat16)


def pick_columns(table, columns):
    rows, channels = table.shape
    splits, _, width = columns.shape
    return pl.pallas_call(
        pick_kernel,
        in_specs=[VMEM] * 2,
        out_specs=VMEM,
        out_shape=pltpu.VMEM((splits, rows, width), jnp.bfloat16),
        compiler_params=pltpu.CompilerParams(vmem_limit_bytes=VMEM_LIMIT),
        cost_estimate=pl.CostEstimate(
            flops=2 * splits * rows * channels * width,
            bytes_accessed=2 * splits * rows * width,
            transcendentals=0,
        ),
        name="pick_active",
    )(columns, table)


def join_kernel(columns_ref, picked_ref, own_ref, n0, n1, n2, n3, out_ref):
    total = own_ref[...]
    for part in (n0, n1, n2, n3):
        total = total + part[...].astype(jnp.float32)
    neighbour = total.astype(jnp.bfloat16)
    rows, channels = neighbour.shape
    for begin in range(0, picked_ref.shape[2], CHUNK):
        part = slice(begin, begin + CHUNK)
        joined = jnp.zeros((rows, CHUNK), jnp.float32)
        for j in range(SPLITS):
            joined = joined + picked_ref[j, :, part].astype(jnp.float32) * jnp.dot(
                neighbour,
                onehot(columns_ref[j, :, part], channels),
                preferred_element_type=jnp.float32,
            )
        for piece in range(CHUNK // TILE):
            out_ref[begin // TILE + piece] = joined[:, piece * TILE : (piece + 1) * TILE].astype(
                out_ref.dtype
            )


def join(picked, own, parts, columns):
    splits, rows, width = picked.shape
    channels = own.shape[1]
    return pl.pallas_call(
        join_kernel,
        in_specs=[VMEM] * 7,
        out_specs=VMEM,
        out_shape=pltpu.VMEM((width // TILE, rows, TILE), jnp.bfloat16),
        compiler_params=pltpu.CompilerParams(vmem_limit_bytes=VMEM_LIMIT),
        cost_estimate=pl.CostEstimate(
            flops=2 * splits * rows * channels * width,
            bytes_accessed=2 * rows * width,
            transcendentals=0,
        ),
        name="join_sets",
    )(columns, *in_space(pltpu.VMEM, picked, own, *parts))


def local(
    active_table,
    passive_table,
    adjacency,
    tile_dst,
    tile_src,
    tile_count,
    split_active,
    split_passive,
):
    tiles_all = adjacency.reshape(-1, TILE)
    dst, src, count = tile_dst[0, 0].T, tile_src[0, 0].T, tile_count[0, 0]
    nc = lax.axis_size("cset")
    at = (lax.axis_index("blk") % 2).astype(jnp.int32)[None]

    near = pack_tiles((0, 1), at, dst, src, count, tiles_all, "pack_near")
    *near, passive_table = lax.optimization_barrier((*near, passive_table))
    left, right = as_columns(split_active, split_passive)
    left, later = lax.optimization_barrier((left, at))
    far = pack_tiles((2, 3, 4), later, dst, src, count, tiles_all, "pack_far")
    messages = [routed(message, hops) for message, hops in zip((*near, *far), HOPS)]
    copies = jnp.broadcast_to(passive_table[None], (nc,) + passive_table.shape)
    own_rows = lax.all_to_all(copies, "cset", split_axis=0, concat_axis=0, tiled=True)
    own_rows = own_rows.reshape(-1, passive_table.shape[1])
    groups = [[b, b + 1] for b in range(0, lax.axis_size("blk"), 2)]
    twice = jnp.broadcast_to(own_rows[None], (2,) + own_rows.shape)
    sources = lax.all_to_all(
        twice, "blk", split_axis=0, concat_axis=0, tiled=True, axis_index_groups=groups
    ).reshape(-1, own_rows.shape[1])

    sources, left, right = lax.optimization_barrier((sources, left, right))
    near_up, near_down, far_up, far_down, odd = messages
    far_below, far_above = sum_away(
        sum_far_kernel, at, sources, (far_up, far_down, odd), "sum_far"
    )
    far_below, far_above, sources = lax.optimization_barrier((far_below, far_above, sources))
    near_below, near_above = sum_away(
        sum_near_kernel, at, sources, (near_up, near_down), "sum_near"
    )
    near_below, near_above, left = lax.optimization_barrier((near_below, near_above, left))
    picked = pick_columns(active_table, left)
    own = sum_own(at, dst, src, count, sources, tiles_all)
    parts = [
        routed(far_above, lambda core: 2),
        routed(far_below, lambda core: -2),
        routed(near_above, lambda core: 1),
        routed(near_below, lambda core: -1),
    ]
    joined = join(picked, own, parts, right)
    spread = lax.all_to_all(joined, "cset", split_axis=0, concat_axis=0, tiled=True)
    return spread.reshape(-1, TILE)


def solution(mesh):
    in_specs = (
        P(("blk", "cset"), None),
        P(("blk", "cset"), None),
        P("blk", "cset", None, None, None, None),
        P("blk", "cset", None, None),
        P("blk", "cset", None, None),
        P("blk", "cset", None),
        P(),
        P(),
    )
    out_specs = P("blk", "cset")
    return jax.shard_map(local, mesh=mesh, in_specs=in_specs, out_specs=out_specs, check_vma=False)
```

```python
import functools

import jax
import jax.numpy as jnp
from jax import lax
from jax.experimental import pallas as pl
from jax.experimental.pallas import tpu as pltpu
from jax.sharding import PartitionSpec as P

SPLITS = 20
OUTPAD = 1024
TILE = 128
CHUNK = 512
SLOTS = 8
PAIR = 2 * SLOTS
TAIL = 16
REACH = 9
PART_TILES = 16
VMEM_LIMIT = 16 * 1024 * 1024


def routed(block, hops):
    nb, nc = lax.axis_size("blk"), lax.axis_size("cset")
    route = []
    for b in range(nb):
        chips = hops(b % 2)
        for c in range(nc):
            target = c ^ (nc // 2) if chips % 2 else c
            route.append((b * nc + c, ((b + 2 * chips) % nb) * nc + target))
    return lax.ppermute(block, ("blk", "cset"), route)


def places(slots, dst_ref, src_ref, count_ref):
    held, rows = [], []
    for slot, parity in slots:
        for t in range(SLOTS):
            held.append(src_ref[t, slot] + parity * PART_TILES)
            rows.append(jnp.where(t < count_ref[slot], dst_ref[t, slot], 2))
    return held, rows


def pair_slots(which, core):
    first = 2 * which - core
    return [(first, 0), (first + 1, 1)]


def message_slots(core):
    return [
        pair_slots(3, core),
        pair_slots(1, core),
        [(REACH - 1, core)],
        [(0, core)],
        [(1 + (REACH - 3) * core, 1 - core)],
    ]


HOPS = [
    lambda core: 1,
    lambda core: -1,
    lambda core: 2,
    lambda core: -2,
    lambda core: 4 * core - 2,
]
LENGTHS = [PAIR, PAIR, SLOTS, SLOTS, SLOTS]


def pack_kernel(which, at_ref, dst_ref, src_ref, count_ref, tiles_ref, *rest):
    outs, sems = rest[: len(which)], rest[len(which)]
    lengths = [LENGTHS[n] for n in which]
    lane = lax.broadcasted_iota(jnp.int32, (TAIL, TILE), 1)
    line = lax.broadcasted_iota(jnp.int32, (TAIL, TILE), 0)
    slots = [message_slots(at_ref[0])[n] for n in which]
    copies = []
    for n, length in enumerate(lengths):
        begin = pl.multiple_of(slots[n][0][0] * (SLOTS * TILE), SLOTS * TILE)
        copies.append(
            pltpu.make_async_copy(
                tiles_ref.at[pl.ds(begin, length * TILE)],
                outs[n].at[pl.ds(0, length * TILE)],
                sems.at[n],
            )
        )
    for copy in copies:
        copy.start()
    for n, length in enumerate(lengths):
        held, rows = places(slots[n], dst_ref, src_ref, count_ref)
        tail = jnp.zeros((TAIL, TILE), jnp.int32)
        for t in range(length):
            tail = jnp.where(lane == t, jnp.where(line == 0, held[t], rows[t]), tail)
        outs[n][length * TILE : length * TILE + TAIL] = tail.astype(jnp.float32).astype(jnp.bfloat16)
    for copy in copies:
        copy.wait()


SMEM = pl.BlockSpec(memory_space=pltpu.SMEM)
VMEM = pl.BlockSpec(memory_space=pltpu.VMEM)
ANY = pl.BlockSpec(memory_space=pl.ANY)
HBM = pl.BlockSpec(memory_space=pltpu.HBM)


def in_space(space, *arrays):
    return [pltpu.with_memory_space_constraint(array, space) for array in arrays]


def pack_tiles(which, at, dst, src, count, tiles, name):
    shapes = [(LENGTHS[n] * TILE + TAIL, TILE) for n in which]
    return pl.pallas_call(
        functools.partial(pack_kernel, which),
        in_specs=[SMEM, SMEM, SMEM, SMEM, HBM],
        out_specs=[VMEM] * len(which),
        out_shape=[pltpu.VMEM(shape, jnp.bfloat16) for shape in shapes],
        scratch_shapes=[pltpu.SemaphoreType.DMA((len(which),))],
        compiler_params=pltpu.CompilerParams(vmem_limit_bytes=VMEM_LIMIT),
        cost_estimate=pl.CostEstimate(
            flops=0, bytes_accessed=sum(2 * rows * cols for rows, cols in shapes), transcendentals=0
        ),
        name=name,
    )(at, *in_space(pltpu.HBM, dst, src, count, tiles))


def products(held, rows, tiles, sources):
    total = None
    for t in range(0, PAIR, 2):
        sides, chosen = [], []
        for n in (t, t + 1):
            tile = tiles(n)
            empty = jnp.zeros_like(tile)
            sides.append(
                jnp.concatenate(
                    [jnp.where(rows[n] == 0, tile, empty), jnp.where(rows[n] == 1, tile, empty)], axis=0
                )
            )
            chosen.append(sources[pl.ds(pl.multiple_of(held[n] * TILE, TILE), TILE)])
        product = jnp.dot(
            jnp.concatenate(sides, axis=1),
            jnp.concatenate(chosen, axis=0),
            preferred_element_type=jnp.float32,
        )
        total = product if total is None else total + product
    return total


def read_places(messages, tail, tail_s, sem):
    lengths = [message.shape[0] // TILE for message in messages]
    for n, message in enumerate(messages):
        end = message[lengths[n] * TILE : lengths[n] * TILE + TAIL]
        tail[n] = end.astype(jnp.float32).astype(jnp.int32)
    copy = pltpu.make_async_copy(tail, tail_s, sem)
    copy.start()
    copy.wait()
    return [
        [
            (tail_s[n, 0, t], tail_s[n, 1, t], message.at[t * TILE : (t + 1) * TILE])
            for t in range(lengths[n])
        ]
        for n, message in enumerate(messages)
    ]


def write_products(out, tiles, sources):
    held, rows, refs = zip(*tiles)
    out[...] = products(held, rows, lambda n: refs[n][...], sources).astype(jnp.bfloat16)


def sum_side_kernel(core, at_ref, sources, near, far, odd, to_near, to_far, *scratch):
    near, far, odd = read_places((near, far, odd), *scratch)
    odd = [(held, jnp.where(at_ref[0] == core, row, 2), tile) for held, row, tile in odd]
    write_products(to_near, near, sources)
    write_products(to_far, far + odd, sources)


def sum_away(kernel, at, sources, messages, name):
    rows, channels = sources.shape
    return pl.pallas_call(
        kernel,
        in_specs=[SMEM] + [VMEM] * (1 + len(messages)),
        out_specs=[VMEM] * 2,
        out_shape=[pltpu.VMEM((2 * TILE, channels), jnp.bfloat16)] * 2,
        scratch_shapes=[
            pltpu.VMEM((len(messages), TAIL, TILE), jnp.int32),
            pltpu.SMEM((len(messages), TAIL, TILE), jnp.int32),
            pltpu.SemaphoreType.DMA,
        ],
        compiler_params=pltpu.CompilerParams(vmem_limit_bytes=VMEM_LIMIT),
        cost_estimate=pl.CostEstimate(
            flops=2 * 4 * TILE * TILE * PAIR * channels,
            bytes_accessed=2 * (rows * channels + 2 * PAIR * TILE * TILE),
            transcendentals=0,
        ),
        name=name,
    )(at, *in_space(pltpu.VMEM, sources, *messages))


def sum_own_kernel(at_ref, dst_ref, src_ref, count_ref, sources_ref, tiles_ref, out_ref, *rest):
    tiles, sem = rest
    slots = pair_slots(2, at_ref[0])
    held, placed = places(slots, dst_ref, src_ref, count_ref)
    begin = pl.multiple_of(slots[0][0] * (SLOTS * TILE), SLOTS * TILE)
    copy = pltpu.make_async_copy(tiles_ref.at[pl.ds(begin, PAIR * TILE)], tiles, sem)
    copy.start()
    copy.wait()
    out_ref[...] = products(held, placed, lambda n: tiles[n * TILE : (n + 1) * TILE], sources_ref)


def sum_own(at, dst, src, count, sources, tiles):
    rows, channels = sources.shape
    return pl.pallas_call(
        sum_own_kernel,
        in_specs=[SMEM] * 4 + [VMEM] + [HBM],
        out_specs=VMEM,
        out_shape=jax.ShapeDtypeStruct((2 * TILE, channels), jnp.float32),
        scratch_shapes=[
            pltpu.VMEM((PAIR * TILE, TILE), jnp.bfloat16),
            pltpu.SemaphoreType.DMA,
        ],
        compiler_params=pltpu.CompilerParams(vmem_limit_bytes=VMEM_LIMIT),
        cost_estimate=pl.CostEstimate(
            flops=4 * TILE * TILE * PAIR * channels,
            bytes_accessed=2 * (rows * channels + PAIR * TILE * TILE),
            transcendentals=0,
        ),
        name="sum_own",
    )(
        at,
        dst,
        src,
        count,
        *in_space(pltpu.VMEM, sources),
        tiles,
    )


def onehot(columns, channels):
    shape = (channels, columns.shape[1])
    channel = lax.broadcasted_iota(jnp.int32, shape, 0).astype(jnp.float32).astype(jnp.bfloat16)
    one, zero = jnp.ones(shape, jnp.bfloat16), jnp.zeros(shape, jnp.bfloat16)
    return jnp.where(channel == columns, one, zero)


def columns_kernel(left_ref, right_ref, left_out, right_out):
    for ref, out in ((left_ref, left_out), (right_ref, right_out)):
        out[...] = jnp.full(out.shape, -1, jnp.bfloat16)
        for j in range(SPLITS):
            row = ref[j : j + 1].astype(jnp.float32).astype(jnp.bfloat16)
            out[j, :, : ref.shape[1]] = row


def as_columns(left, right):
    return pl.pallas_call(
        columns_kernel,
        in_specs=[VMEM] * 2,
        out_specs=[VMEM] * 2,
        out_shape=[pltpu.VMEM((SPLITS, 1, OUTPAD), jnp.bfloat16)] * 2,
        compiler_params=pltpu.CompilerParams(vmem_limit_bytes=VMEM_LIMIT),
        cost_estimate=pl.CostEstimate(flops=10000000000, bytes_accessed=1, transcendentals=0),
        name="as_columns",
    )(left, right)


def pick_kernel(columns_ref, table_ref, out_ref):
    table = table_ref[...]
    for j in range(SPLITS):
        for begin in range(0, out_ref.shape[2], CHUNK):
            part = slice(begin, begin + CHUNK)
            picked = jnp.dot(
                table,
                onehot(columns_ref[j, :, part], table.shape[1]),
                preferred_element_type=jnp.float32,
            )
            out_ref[j, :, part] = picked.astype(jnp.bfloat16)


def pick_columns(table, columns):
    rows, channels = table.shape
    splits, _, width = columns.shape
    return pl.pallas_call(
        pick_kernel,
        in_specs=[VMEM] * 2,
        out_specs=VMEM,
        out_shape=pltpu.VMEM((splits, rows, width), jnp.bfloat16),
        compiler_params=pltpu.CompilerParams(vmem_limit_bytes=VMEM_LIMIT),
        cost_estimate=pl.CostEstimate(
            flops=2 * splits * rows * channels * width,
            bytes_accessed=2 * splits * rows * width,
            transcendentals=0,
        ),
        name="pick_active",
    )(columns, table)


def join_kernel(columns_ref, picked_ref, own_ref, n0, n1, n2, n3, out_ref):
    total = own_ref[...]
    for part in (n0, n1, n2, n3):
        total = total + part[...].astype(jnp.float32)
    neighbour = total.astype(jnp.bfloat16)
    rows, channels = neighbour.shape
    for begin in range(0, picked_ref.shape[2], CHUNK):
        part = slice(begin, begin + CHUNK)
        joined = jnp.zeros((rows, CHUNK), jnp.float32)
        for j in range(SPLITS):
            joined = joined + picked_ref[j, :, part].astype(jnp.float32) * jnp.dot(
                neighbour,
                onehot(columns_ref[j, :, part], channels),
                preferred_element_type=jnp.float32,
            )
        for piece in range(CHUNK // TILE):
            out_ref[begin // TILE + piece] = joined[:, piece * TILE : (piece + 1) * TILE].astype(
                out_ref.dtype
            )


def join(picked, own, parts, columns):
    splits, rows, width = picked.shape
    channels = own.shape[1]
    return pl.pallas_call(
        join_kernel,
        in_specs=[VMEM] * 7,
        out_specs=VMEM,
        out_shape=pltpu.VMEM((width // TILE, rows, TILE), jnp.bfloat16),
        compiler_params=pltpu.CompilerParams(vmem_limit_bytes=VMEM_LIMIT),
        cost_estimate=pl.CostEstimate(
            flops=2 * splits * rows * channels * width,
            bytes_accessed=2 * rows * width,
            transcendentals=0,
        ),
        name="join_sets",
    )(columns, *in_space(pltpu.VMEM, picked, own, *parts))


def local(
    active_table,
    passive_table,
    adjacency,
    tile_dst,
    tile_src,
    tile_count,
    split_active,
    split_passive,
):
    tiles_all = adjacency.reshape(-1, TILE)
    dst, src, count = tile_dst[0, 0].T, tile_src[0, 0].T, tile_count[0, 0]
    nc = lax.axis_size("cset")
    at = (lax.axis_index("blk") % 2).astype(jnp.int32)[None]

    first = pack_tiles((0,), at, dst, src, count, tiles_all, "pack_first")
    *first, passive_table = lax.optimization_barrier((*first, passive_table))
    left, right = as_columns(split_active, split_passive)
    left, later = lax.optimization_barrier((left, at))
    rest = pack_tiles((1, 2, 3, 4), later, dst, src, count, tiles_all, "pack_rest")
    messages = [routed(message, hops) for message, hops in zip((*first, *rest), HOPS)]
    copies = jnp.broadcast_to(passive_table[None], (nc,) + passive_table.shape)
    own_rows = lax.all_to_all(copies, "cset", split_axis=0, concat_axis=0, tiled=True)
    own_rows = own_rows.reshape(-1, passive_table.shape[1])
    groups = [[b, b + 1] for b in range(0, lax.axis_size("blk"), 2)]
    twice = jnp.broadcast_to(own_rows[None], (2,) + own_rows.shape)
    sources = lax.all_to_all(
        twice, "blk", split_axis=0, concat_axis=0, tiled=True, axis_index_groups=groups
    ).reshape(-1, own_rows.shape[1])

    sources, left, right = lax.optimization_barrier((sources, left, right))
    near_up, near_down, far_up, far_down, odd = messages
    near_above, far_above = sum_away(
        functools.partial(sum_side_kernel, 0), at, sources, (near_down, far_down, odd), "sum_above"
    )
    near_above, far_above, sources = lax.optimization_barrier((near_above, far_above, sources))
    near_below, far_below = sum_away(
        functools.partial(sum_side_kernel, 1), at, sources, (near_up, far_up, odd), "sum_below"
    )
    near_below, far_below, left = lax.optimization_barrier((near_below, far_below, left))
    picked = pick_columns(active_table, left)
    own = sum_own(at, dst, src, count, sources, tiles_all)
    parts = [
        routed(near_above, lambda core: 1),
        routed(far_above, lambda core: 2),
        routed(near_below, lambda core: -1),
        routed(far_below, lambda core: -2),
    ]
    joined = join(picked, own, parts, right)
    spread = lax.all_to_all(joined, "cset", split_axis=0, concat_axis=0, tiled=True)
    return spread.reshape(-1, TILE)


def solution(mesh):
    in_specs = (
        P(("blk", "cset"), None),
        P(("blk", "cset"), None),
        P("blk", "cset", None, None, None, None),
        P("blk", "cset", None, None),
        P("blk", "cset", None, None),
        P("blk", "cset", None),
        P(),
        P(),
    )
    out_specs = P("blk", "cset")
    return jax.shard_map(local, mesh=mesh, in_specs=in_specs, out_specs=out_specs, check_vma=False)
```

```python
import functools

import jax
import jax.numpy as jnp
from jax import lax
from jax.experimental import pallas as pl
from jax.experimental.pallas import tpu as pltpu
from jax.sharding import PartitionSpec as P

SPLITS = 20
OUTPAD = 1024
TILE = 128
CHUNK = 512
SLOTS = 8
PAIR = 2 * SLOTS
TAIL = 16
REACH = 9
PART_TILES = 16
VMEM_LIMIT = 16 * 1024 * 1024


def routed(block, hops):
    nb, nc = lax.axis_size("blk"), lax.axis_size("cset")
    route = []
    for b in range(nb):
        chips = hops(b % 2)
        for c in range(nc):
            target = c ^ (nc // 2) if chips % 2 else c
            route.append((b * nc + c, ((b + 2 * chips) % nb) * nc + target))
    return lax.ppermute(block, ("blk", "cset"), route)


def places(slots, dst_ref, src_ref, count_ref):
    held, rows = [], []
    for slot, parity in slots:
        for t in range(SLOTS):
            held.append(src_ref[t, slot] + parity * PART_TILES)
            rows.append(jnp.where(t < count_ref[slot], dst_ref[t, slot], 2))
    return held, rows


def pair_slots(which, core):
    first = 2 * which - core
    return [(first, 0), (first + 1, 1)]


def message_slots(core):
    return [
        pair_slots(3, core),
        pair_slots(1, core),
        [(REACH - 1, core)],
        [(0, core)],
        [(1 + (REACH - 3) * core, 1 - core)],
    ]


HOPS = [
    lambda core: 1,
    lambda core: -1,
    lambda core: 2,
    lambda core: -2,
    lambda core: 4 * core - 2,
]
LENGTHS = [PAIR, PAIR, SLOTS, SLOTS, SLOTS]


def pack_kernel(which, at_ref, dst_ref, src_ref, count_ref, tiles_ref, *rest):
    outs, sems = rest[: len(which)], rest[len(which)]
    lengths = [LENGTHS[n] for n in which]
    lane = lax.broadcasted_iota(jnp.int32, (TAIL, TILE), 1)
    line = lax.broadcasted_iota(jnp.int32, (TAIL, TILE), 0)
    slots = [message_slots(at_ref[0])[n] for n in which]
    copies = []
    for n, length in enumerate(lengths):
        begin = pl.multiple_of(slots[n][0][0] * (SLOTS * TILE), SLOTS * TILE)
        copies.append(
            pltpu.make_async_copy(
                tiles_ref.at[pl.ds(begin, length * TILE)],
                outs[n].at[pl.ds(0, length * TILE)],
                sems.at[n],
            )
        )
    for copy in copies:
        copy.start()
    for n, length in enumerate(lengths):
        held, rows = places(slots[n], dst_ref, src_ref, count_ref)
        tail = jnp.zeros((TAIL, TILE), jnp.int32)
        for t in range(length):
            tail = jnp.where(lane == t, jnp.where(line == 0, held[t], rows[t]), tail)
        outs[n][length * TILE : length * TILE + TAIL] = tail.astype(jnp.float32).astype(jnp.bfloat16)
    for copy in copies:
        copy.wait()


SMEM = pl.BlockSpec(memory_space=pltpu.SMEM)
VMEM = pl.BlockSpec(memory_space=pltpu.VMEM)
ANY = pl.BlockSpec(memory_space=pl.ANY)
HBM = pl.BlockSpec(memory_space=pltpu.HBM)


def in_space(space, *arrays):
    return [pltpu.with_memory_space_constraint(array, space) for array in arrays]


def pack_tiles(which, at, dst, src, count, tiles, name):
    shapes = [(LENGTHS[n] * TILE + TAIL, TILE) for n in which]
    return pl.pallas_call(
        functools.partial(pack_kernel, which),
        in_specs=[SMEM, SMEM, SMEM, SMEM, HBM],
        out_specs=[VMEM] * len(which),
        out_shape=[pltpu.VMEM(shape, jnp.bfloat16) for shape in shapes],
        scratch_shapes=[pltpu.SemaphoreType.DMA((len(which),))],
        compiler_params=pltpu.CompilerParams(vmem_limit_bytes=VMEM_LIMIT),
        cost_estimate=pl.CostEstimate(
            flops=0, bytes_accessed=sum(2 * rows * cols for rows, cols in shapes), transcendentals=0
        ),
        name=name,
    )(at, *in_space(pltpu.HBM, dst, src, count, tiles))


def products(held, rows, tiles, sources):
    total = None
    for t in range(0, PAIR, 2):
        sides, chosen = [], []
        for n in (t, t + 1):
            tile = tiles(n)
            empty = jnp.zeros_like(tile)
            sides.append(
                jnp.concatenate(
                    [jnp.where(rows[n] == 0, tile, empty), jnp.where(rows[n] == 1, tile, empty)], axis=0
                )
            )
            chosen.append(sources[pl.ds(pl.multiple_of(held[n] * TILE, TILE), TILE)])
        product = jnp.dot(
            jnp.concatenate(sides, axis=1),
            jnp.concatenate(chosen, axis=0),
            preferred_element_type=jnp.float32,
        )
        total = product if total is None else total + product
    return total


def read_places(messages, tail, tail_s, sem):
    lengths = [message.shape[0] // TILE for message in messages]
    for n, message in enumerate(messages):
        end = message[lengths[n] * TILE : lengths[n] * TILE + TAIL]
        tail[n] = end.astype(jnp.float32).astype(jnp.int32)
    copy = pltpu.make_async_copy(tail, tail_s, sem)
    copy.start()
    copy.wait()
    return [
        [
            (tail_s[n, 0, t], tail_s[n, 1, t], message.at[t * TILE : (t + 1) * TILE])
            for t in range(lengths[n])
        ]
        for n, message in enumerate(messages)
    ]


def write_products(out, tiles, sources):
    held, rows, refs = zip(*tiles)
    out[...] = products(held, rows, lambda n: refs[n][...], sources).astype(jnp.bfloat16)


def sum_near_kernel(at_ref, sources, from_below, from_above, to_below, to_above, *scratch):
    below, above = read_places((from_below, from_above), *scratch)
    write_products(to_below, below, sources)
    write_products(to_above, above, sources)


def sum_far_kernel(at_ref, sources, from_below, from_above, odd, to_below, to_above, *scratch):
    below, above, extra = read_places((from_below, from_above, odd), *scratch)

    def kept(core):
        return [(held, jnp.where(at_ref[0] == core, row, 2), tile) for held, row, tile in extra]

    write_products(to_below, below + kept(1), sources)
    write_products(to_above, above + kept(0), sources)


def sum_away(kernel, at, sources, messages, name):
    rows, channels = sources.shape
    return pl.pallas_call(
        kernel,
        in_specs=[SMEM] + [VMEM] * (1 + len(messages)),
        out_specs=[VMEM] * 2,
        out_shape=[pltpu.VMEM((2 * TILE, channels), jnp.bfloat16)] * 2,
        scratch_shapes=[
            pltpu.VMEM((len(messages), TAIL, TILE), jnp.int32),
            pltpu.SMEM((len(messages), TAIL, TILE), jnp.int32),
            pltpu.SemaphoreType.DMA,
        ],
        compiler_params=pltpu.CompilerParams(vmem_limit_bytes=VMEM_LIMIT),
        cost_estimate=pl.CostEstimate(
            flops=2 * 4 * TILE * TILE * PAIR * channels,
            bytes_accessed=2 * (rows * channels + 2 * PAIR * TILE * TILE),
            transcendentals=0,
        ),
        name=name,
    )(at, *in_space(pltpu.VMEM, sources, *messages))


def sum_own_kernel(at_ref, dst_ref, src_ref, count_ref, sources_ref, tiles_ref, out_ref, *rest):
    tiles, sem = rest
    slots = pair_slots(2, at_ref[0])
    held, placed = places(slots, dst_ref, src_ref, count_ref)
    begin = pl.multiple_of(slots[0][0] * (SLOTS * TILE), SLOTS * TILE)
    copy = pltpu.make_async_copy(tiles_ref.at[pl.ds(begin, PAIR * TILE)], tiles, sem)
    copy.start()
    copy.wait()
    out_ref[...] = products(held, placed, lambda n: tiles[n * TILE : (n + 1) * TILE], sources_ref)


def sum_own(at, dst, src, count, sources, tiles):
    rows, channels = sources.shape
    return pl.pallas_call(
        sum_own_kernel,
        in_specs=[SMEM] * 4 + [VMEM] + [HBM],
        out_specs=VMEM,
        out_shape=jax.ShapeDtypeStruct((2 * TILE, channels), jnp.float32),
        scratch_shapes=[
            pltpu.VMEM((PAIR * TILE, TILE), jnp.bfloat16),
            pltpu.SemaphoreType.DMA,
        ],
        compiler_params=pltpu.CompilerParams(vmem_limit_bytes=VMEM_LIMIT),
        cost_estimate=pl.CostEstimate(
            flops=4 * TILE * TILE * PAIR * channels,
            bytes_accessed=2 * (rows * channels + PAIR * TILE * TILE),
            transcendentals=0,
        ),
        name="sum_own",
    )(
        at,
        dst,
        src,
        count,
        *in_space(pltpu.VMEM, sources),
        tiles,
    )


def onehot(columns, channels):
    shape = (channels, columns.shape[1])
    channel = lax.broadcasted_iota(jnp.int32, shape, 0).astype(jnp.float32).astype(jnp.bfloat16)
    one, zero = jnp.ones(shape, jnp.bfloat16), jnp.zeros(shape, jnp.bfloat16)
    return jnp.where(channel == columns, one, zero)


def columns_kernel(left_ref, right_ref, left_out, right_out):
    for ref, out in ((left_ref, left_out), (right_ref, right_out)):
        out[...] = jnp.full(out.shape, -1, jnp.bfloat16)
        for j in range(SPLITS):
            row = ref[j : j + 1].astype(jnp.float32).astype(jnp.bfloat16)
            out[j, :, : ref.shape[1]] = row


def as_columns(left, right):
    return pl.pallas_call(
        columns_kernel,
        in_specs=[VMEM] * 2,
        out_specs=[VMEM] * 2,
        out_shape=[pltpu.VMEM((SPLITS, 1, OUTPAD), jnp.bfloat16)] * 2,
        compiler_params=pltpu.CompilerParams(vmem_limit_bytes=VMEM_LIMIT),
        cost_estimate=pl.CostEstimate(flops=10000000000, bytes_accessed=1, transcendentals=0),
        name="as_columns",
    )(left, right)


def pick_kernel(columns_ref, table_ref, out_ref):
    table = table_ref[...]
    for j in range(SPLITS):
        for begin in range(0, out_ref.shape[2], CHUNK):
            part = slice(begin, begin + CHUNK)
            picked = jnp.dot(
                table,
                onehot(columns_ref[j, :, part], table.shape[1]),
                preferred_element_type=jnp.float32,
            )
            out_ref[j, :, part] = picked.astype(jnp.bfloat16)


def pick_columns(table, columns):
    rows, channels = table.shape
    splits, _, width = columns.shape
    return pl.pallas_call(
        pick_kernel,
        in_specs=[VMEM] * 2,
        out_specs=VMEM,
        out_shape=pltpu.VMEM((splits, rows, width), jnp.bfloat16),
        compiler_params=pltpu.CompilerParams(vmem_limit_bytes=VMEM_LIMIT),
        cost_estimate=pl.CostEstimate(
            flops=2 * splits * rows * channels * width,
            bytes_accessed=2 * splits * rows * width,
            transcendentals=0,
        ),
        name="pick_active",
    )(columns, table)


def join_kernel(columns_ref, picked_ref, own_ref, n0, n1, n2, n3, out_ref):
    total = own_ref[...]
    for part in (n0, n1, n2, n3):
        total = total + part[...].astype(jnp.float32)
    neighbour = total.astype(jnp.bfloat16)
    rows, channels = neighbour.shape
    for begin in range(0, picked_ref.shape[2], CHUNK):
        part = slice(begin, begin + CHUNK)
        joined = jnp.zeros((rows, CHUNK), jnp.float32)
        for j in range(SPLITS):
            joined = joined + picked_ref[j, :, part].astype(jnp.float32) * jnp.dot(
                neighbour,
                onehot(columns_ref[j, :, part], channels),
                preferred_element_type=jnp.float32,
            )
        for piece in range(CHUNK // TILE):
            out_ref[begin // TILE + piece] = joined[:, piece * TILE : (piece + 1) * TILE].astype(
                out_ref.dtype
            )


def join(picked, own, parts, columns):
    splits, rows, width = picked.shape
    channels = own.shape[1]
    return pl.pallas_call(
        join_kernel,
        in_specs=[VMEM] * 7,
        out_specs=VMEM,
        out_shape=pltpu.VMEM((width // TILE, rows, TILE), jnp.bfloat16),
        compiler_params=pltpu.CompilerParams(vmem_limit_bytes=VMEM_LIMIT),
        cost_estimate=pl.CostEstimate(
            flops=2 * splits * rows * channels * width,
            bytes_accessed=2 * rows * width,
            transcendentals=0,
        ),
        name="join_sets",
    )(columns, *in_space(pltpu.VMEM, picked, own, *parts))


def local(
    active_table,
    passive_table,
    adjacency,
    tile_dst,
    tile_src,
    tile_count,
    split_active,
    split_passive,
):
    tiles_all = adjacency.reshape(-1, TILE)
    dst, src, count = tile_dst[0, 0].T, tile_src[0, 0].T, tile_count[0, 0]
    nc = lax.axis_size("cset")
    at = (lax.axis_index("blk") % 2).astype(jnp.int32)[None]

    first = pack_tiles((0,), at, dst, src, count, tiles_all, "pack_first")
    *first, passive_table = lax.optimization_barrier((*first, passive_table))
    left, right = as_columns(split_active, split_passive)
    left, later = lax.optimization_barrier((left, at))
    rest = pack_tiles((1, 2, 3, 4), later, dst, src, count, tiles_all, "pack_rest")
    messages = [routed(message, hops) for message, hops in zip((*first, *rest), HOPS)]
    copies = jnp.broadcast_to(passive_table[None], (nc,) + passive_table.shape)
    own_rows = lax.all_to_all(copies, "cset", split_axis=0, concat_axis=0, tiled=True)
    own_rows = own_rows.reshape(-1, passive_table.shape[1])
    groups = [[b, b + 1] for b in range(0, lax.axis_size("blk"), 2)]
    twice = jnp.broadcast_to(own_rows[None], (2,) + own_rows.shape)
    sources = lax.all_to_all(
        twice, "blk", split_axis=0, concat_axis=0, tiled=True, axis_index_groups=groups
    ).reshape(-1, own_rows.shape[1])

    sources, left, right = lax.optimization_barrier((sources, left, right))
    near_up, near_down, far_up, far_down, odd = messages
    far_below, far_above = sum_away(
        sum_far_kernel, at, sources, (far_up, far_down, odd), "sum_far"
    )
    far_below, far_above, sources = lax.optimization_barrier((far_below, far_above, sources))
    near_below, near_above = sum_away(
        sum_near_kernel, at, sources, (near_up, near_down), "sum_near"
    )
    near_below, near_above, far_below, left = lax.optimization_barrier(
        (near_below, near_above, far_below, left)
    )
    picked = pick_columns(active_table, left)
    own = sum_own(at, dst, src, count, sources, tiles_all)
    parts = [
        routed(near_above, lambda core: 1),
        routed(far_above, lambda core: 2),
        routed(near_below, lambda core: -1),
        routed(far_below, lambda core: -2),
    ]
    joined = join(picked, own, parts, right)
    spread = lax.all_to_all(joined, "cset", split_axis=0, concat_axis=0, tiled=True)
    return spread.reshape(-1, TILE)


def solution(mesh):
    in_specs = (
        P(("blk", "cset"), None),
        P(("blk", "cset"), None),
        P("blk", "cset", None, None, None, None),
        P("blk", "cset", None, None),
        P("blk", "cset", None, None),
        P("blk", "cset", None),
        P(),
        P(),
    )
    out_specs = P("blk", "cset")
    return jax.shard_map(local, mesh=mesh, in_specs=in_specs, out_specs=out_specs, check_vma=False)
```

```python
import functools

import jax
import jax.numpy as jnp
from jax import lax
from jax.experimental import pallas as pl
from jax.experimental.pallas import tpu as pltpu
from jax.sharding import PartitionSpec as P

SPLITS = 20
OUTPAD = 1024
TILE = 128
CHUNK = 512
SLOTS = 8
PAIR = 2 * SLOTS
TAIL = 16
REACH = 9
PART_TILES = 16
VMEM_LIMIT = 16 * 1024 * 1024


def routed(block, hops):
    nb, nc = lax.axis_size("blk"), lax.axis_size("cset")
    route = []
    for b in range(nb):
        chips = hops(b % 2)
        for c in range(nc):
            target = c ^ (nc // 2) if chips % 2 else c
            route.append((b * nc + c, ((b + 2 * chips) % nb) * nc + target))
    return lax.ppermute(block, ("blk", "cset"), route)


def places(slots, dst_ref, src_ref, count_ref):
    held, rows = [], []
    for slot, parity in slots:
        for t in range(SLOTS):
            held.append(src_ref[t, slot] + parity * PART_TILES)
            rows.append(jnp.where(t < count_ref[slot], dst_ref[t, slot], 2))
    return held, rows


def pair_slots(which, core):
    first = 2 * which - core
    return [(first, 0), (first + 1, 1)]


def message_slots(core):
    return [
        pair_slots(1, core),
        pair_slots(3, core),
        [(REACH - 1, core)],
        [(0, core)],
        [(1 + (REACH - 3) * core, 1 - core)],
    ]


HOPS = [
    lambda core: -1,
    lambda core: 1,
    lambda core: 2,
    lambda core: -2,
    lambda core: 4 * core - 2,
]
LENGTHS = [PAIR, PAIR, SLOTS, SLOTS, SLOTS]


def pack_kernel(which, at_ref, dst_ref, src_ref, count_ref, tiles_ref, *rest):
    outs, sems = rest[: len(which)], rest[len(which)]
    lengths = [LENGTHS[n] for n in which]
    lane = lax.broadcasted_iota(jnp.int32, (TAIL, TILE), 1)
    line = lax.broadcasted_iota(jnp.int32, (TAIL, TILE), 0)
    slots = [message_slots(at_ref[0])[n] for n in which]
    copies = []
    for n, length in enumerate(lengths):
        begin = pl.multiple_of(slots[n][0][0] * (SLOTS * TILE), SLOTS * TILE)
        copies.append(
            pltpu.make_async_copy(
                tiles_ref.at[pl.ds(begin, length * TILE)],
                outs[n].at[pl.ds(0, length * TILE)],
                sems.at[n],
            )
        )
    for copy in copies:
        copy.start()
    for n, length in enumerate(lengths):
        held, rows = places(slots[n], dst_ref, src_ref, count_ref)
        tail = jnp.zeros((TAIL, TILE), jnp.int32)
        for t in range(length):
            tail = jnp.where(lane == t, jnp.where(line == 0, held[t], rows[t]), tail)
        outs[n][length * TILE : length * TILE + TAIL] = tail.astype(jnp.float32).astype(jnp.bfloat16)
    for copy in copies:
        copy.wait()


SMEM = pl.BlockSpec(memory_space=pltpu.SMEM)
VMEM = pl.BlockSpec(memory_space=pltpu.VMEM)
ANY = pl.BlockSpec(memory_space=pl.ANY)
HBM = pl.BlockSpec(memory_space=pltpu.HBM)


def in_space(space, *arrays):
    return [pltpu.with_memory_space_constraint(array, space) for array in arrays]


def pack_tiles(which, at, dst, src, count, tiles, name):
    shapes = [(LENGTHS[n] * TILE + TAIL, TILE) for n in which]
    return pl.pallas_call(
        functools.partial(pack_kernel, which),
        in_specs=[SMEM, SMEM, SMEM, SMEM, HBM],
        out_specs=[VMEM] * len(which),
        out_shape=[pltpu.VMEM(shape, jnp.bfloat16) for shape in shapes],
        scratch_shapes=[pltpu.SemaphoreType.DMA((len(which),))],
        compiler_params=pltpu.CompilerParams(vmem_limit_bytes=VMEM_LIMIT),
        cost_estimate=pl.CostEstimate(
            flops=0, bytes_accessed=sum(2 * rows * cols for rows, cols in shapes), transcendentals=0
        ),
        name=name,
    )(at, *in_space(pltpu.HBM, dst, src, count, tiles))


def products(held, rows, tiles, sources):
    total = None
    for t in range(0, PAIR, 2):
        sides, chosen = [], []
        for n in (t, t + 1):
            tile = tiles(n)
            empty = jnp.zeros_like(tile)
            sides.append(
                jnp.concatenate(
                    [jnp.where(rows[n] == 0, tile, empty), jnp.where(rows[n] == 1, tile, empty)], axis=0
                )
            )
            chosen.append(sources[pl.ds(pl.multiple_of(held[n] * TILE, TILE), TILE)])
        product = jnp.dot(
            jnp.concatenate(sides, axis=1),
            jnp.concatenate(chosen, axis=0),
            preferred_element_type=jnp.float32,
        )
        total = product if total is None else total + product
    return total


def read_places(messages, tail, tail_s, sem):
    lengths = [message.shape[0] // TILE for message in messages]
    for n, message in enumerate(messages):
        end = message[lengths[n] * TILE : lengths[n] * TILE + TAIL]
        tail[n] = end.astype(jnp.float32).astype(jnp.int32)
    copy = pltpu.make_async_copy(tail, tail_s, sem)
    copy.start()
    copy.wait()
    return [
        [
            (tail_s[n, 0, t], tail_s[n, 1, t], message.at[t * TILE : (t + 1) * TILE])
            for t in range(lengths[n])
        ]
        for n, message in enumerate(messages)
    ]


def write_products(out, tiles, sources):
    held, rows, refs = zip(*tiles)
    out[...] = products(held, rows, lambda n: refs[n][...], sources).astype(jnp.bfloat16)


def sum_near_kernel(at_ref, sources, from_above, from_below, to_above, to_below, *scratch):
    above, below = read_places((from_above, from_below), *scratch)
    write_products(to_above, above, sources)
    write_products(to_below, below, sources)


def sum_far_kernel(at_ref, sources, from_below, from_above, odd, to_below, to_above, *scratch):
    below, above, extra = read_places((from_below, from_above, odd), *scratch)

    def kept(core):
        return [(held, jnp.where(at_ref[0] == core, row, 2), tile) for held, row, tile in extra]

    write_products(to_below, below + kept(1), sources)
    write_products(to_above, above + kept(0), sources)


def sum_away(kernel, at, sources, messages, name):
    rows, channels = sources.shape
    return pl.pallas_call(
        kernel,
        in_specs=[SMEM] + [VMEM] * (1 + len(messages)),
        out_specs=[VMEM] * 2,
        out_shape=[pltpu.VMEM((2 * TILE, channels), jnp.bfloat16)] * 2,
        scratch_shapes=[
            pltpu.VMEM((len(messages), TAIL, TILE), jnp.int32),
            pltpu.SMEM((len(messages), TAIL, TILE), jnp.int32),
            pltpu.SemaphoreType.DMA,
        ],
        compiler_params=pltpu.CompilerParams(vmem_limit_bytes=VMEM_LIMIT),
        cost_estimate=pl.CostEstimate(
            flops=2 * 4 * TILE * TILE * PAIR * channels,
            bytes_accessed=2 * (rows * channels + 2 * PAIR * TILE * TILE),
            transcendentals=0,
        ),
        name=name,
    )(at, *in_space(pltpu.VMEM, sources, *messages))


def sum_own_kernel(at_ref, dst_ref, src_ref, count_ref, sources_ref, tiles_ref, out_ref, *rest):
    tiles, sem = rest
    slots = pair_slots(2, at_ref[0])
    held, placed = places(slots, dst_ref, src_ref, count_ref)
    begin = pl.multiple_of(slots[0][0] * (SLOTS * TILE), SLOTS * TILE)
    copy = pltpu.make_async_copy(tiles_ref.at[pl.ds(begin, PAIR * TILE)], tiles, sem)
    copy.start()
    copy.wait()
    out_ref[...] = products(held, placed, lambda n: tiles[n * TILE : (n + 1) * TILE], sources_ref)


def sum_own(at, dst, src, count, sources, tiles):
    rows, channels = sources.shape
    return pl.pallas_call(
        sum_own_kernel,
        in_specs=[SMEM] * 4 + [VMEM] + [HBM],
        out_specs=VMEM,
        out_shape=jax.ShapeDtypeStruct((2 * TILE, channels), jnp.float32),
        scratch_shapes=[
            pltpu.VMEM((PAIR * TILE, TILE), jnp.bfloat16),
            pltpu.SemaphoreType.DMA,
        ],
        compiler_params=pltpu.CompilerParams(vmem_limit_bytes=VMEM_LIMIT),
        cost_estimate=pl.CostEstimate(
            flops=4 * TILE * TILE * PAIR * channels,
            bytes_accessed=2 * (rows * channels + PAIR * TILE * TILE),
            transcendentals=0,
        ),
        name="sum_own",
    )(
        at,
        dst,
        src,
        count,
        *in_space(pltpu.VMEM, sources),
        tiles,
    )


def onehot(columns, channels):
    shape = (channels, columns.shape[1])
    channel = lax.broadcasted_iota(jnp.int32, shape, 0).astype(jnp.float32).astype(jnp.bfloat16)
    one, zero = jnp.ones(shape, jnp.bfloat16), jnp.zeros(shape, jnp.bfloat16)
    return jnp.where(channel == columns, one, zero)


def columns_kernel(left_ref, right_ref, left_out, right_out):
    for ref, out in ((left_ref, left_out), (right_ref, right_out)):
        out[...] = jnp.full(out.shape, -1, jnp.bfloat16)
        for j in range(SPLITS):
            row = ref[j : j + 1].astype(jnp.float32).astype(jnp.bfloat16)
            out[j, :, : ref.shape[1]] = row


def as_columns(left, right):
    return pl.pallas_call(
        columns_kernel,
        in_specs=[VMEM] * 2,
        out_specs=[VMEM] * 2,
        out_shape=[pltpu.VMEM((SPLITS, 1, OUTPAD), jnp.bfloat16)] * 2,
        compiler_params=pltpu.CompilerParams(vmem_limit_bytes=VMEM_LIMIT),
        cost_estimate=pl.CostEstimate(flops=10000000000, bytes_accessed=1, transcendentals=0),
        name="as_columns",
    )(left, right)


def pick_kernel(columns_ref, table_ref, out_ref):
    table = table_ref[...]
    for j in range(SPLITS):
        for begin in range(0, out_ref.shape[2], CHUNK):
            part = slice(begin, begin + CHUNK)
            picked = jnp.dot(
                table,
                onehot(columns_ref[j, :, part], table.shape[1]),
                preferred_element_type=jnp.float32,
            )
            out_ref[j, :, part] = picked.astype(jnp.bfloat16)


def pick_columns(table, columns):
    rows, channels = table.shape
    splits, _, width = columns.shape
    return pl.pallas_call(
        pick_kernel,
        in_specs=[VMEM] * 2,
        out_specs=VMEM,
        out_shape=pltpu.VMEM((splits, rows, width), jnp.bfloat16),
        compiler_params=pltpu.CompilerParams(vmem_limit_bytes=VMEM_LIMIT),
        cost_estimate=pl.CostEstimate(
            flops=2 * splits * rows * channels * width,
            bytes_accessed=2 * splits * rows * width,
            transcendentals=0,
        ),
        name="pick_active",
    )(columns, table)


def join_kernel(columns_ref, picked_ref, own_ref, n0, n1, n2, n3, out_ref):
    total = own_ref[...]
    for part in (n0, n1, n2, n3):
        total = total + part[...].astype(jnp.float32)
    neighbour = total.astype(jnp.bfloat16)
    rows, channels = neighbour.shape
    for begin in range(0, picked_ref.shape[2], CHUNK):
        part = slice(begin, begin + CHUNK)
        joined = jnp.zeros((rows, CHUNK), jnp.float32)
        for j in range(SPLITS):
            joined = joined + picked_ref[j, :, part].astype(jnp.float32) * jnp.dot(
                neighbour,
                onehot(columns_ref[j, :, part], channels),
                preferred_element_type=jnp.float32,
            )
        for piece in range(CHUNK // TILE):
            out_ref[begin // TILE + piece] = joined[:, piece * TILE : (piece + 1) * TILE].astype(
                out_ref.dtype
            )


def join(picked, own, parts, columns):
    splits, rows, width = picked.shape
    channels = own.shape[1]
    return pl.pallas_call(
        join_kernel,
        in_specs=[VMEM] * 7,
        out_specs=VMEM,
        out_shape=pltpu.VMEM((width // TILE, rows, TILE), jnp.bfloat16),
        compiler_params=pltpu.CompilerParams(vmem_limit_bytes=VMEM_LIMIT),
        cost_estimate=pl.CostEstimate(
            flops=2 * splits * rows * channels * width,
            bytes_accessed=2 * rows * width,
            transcendentals=0,
        ),
        name="join_sets",
    )(columns, *in_space(pltpu.VMEM, picked, own, *parts))


def local(
    active_table,
    passive_table,
    adjacency,
    tile_dst,
    tile_src,
    tile_count,
    split_active,
    split_passive,
):
    tiles_all = adjacency.reshape(-1, TILE)
    dst, src, count = tile_dst[0, 0].T, tile_src[0, 0].T, tile_count[0, 0]
    nc = lax.axis_size("cset")
    at = (lax.axis_index("blk") % 2).astype(jnp.int32)[None]

    near = pack_tiles((0, 1), at, dst, src, count, tiles_all, "pack_near")
    *near, passive_table = lax.optimization_barrier((*near, passive_table))
    left, right = as_columns(split_active, split_passive)
    left, later = lax.optimization_barrier((left, at))
    far = pack_tiles((2, 3, 4), later, dst, src, count, tiles_all, "pack_far")
    messages = [routed(message, hops) for message, hops in zip((*near, *far), HOPS)]
    copies = jnp.broadcast_to(passive_table[None], (nc,) + passive_table.shape)
    own_rows = lax.all_to_all(copies, "cset", split_axis=0, concat_axis=0, tiled=True)
    own_rows = own_rows.reshape(-1, passive_table.shape[1])
    groups = [[b, b + 1] for b in range(0, lax.axis_size("blk"), 2)]
    twice = jnp.broadcast_to(own_rows[None], (2,) + own_rows.shape)
    sources = lax.all_to_all(
        twice, "blk", split_axis=0, concat_axis=0, tiled=True, axis_index_groups=groups
    ).reshape(-1, own_rows.shape[1])

    sources, left, right = lax.optimization_barrier((sources, left, right))
    near_down, near_up, far_up, far_down, odd = messages
    far_below, far_above = sum_away(
        sum_far_kernel, at, sources, (far_up, far_down, odd), "sum_far"
    )
    far_below, far_above, sources = lax.optimization_barrier((far_below, far_above, sources))
    near_above, near_below = sum_away(
        sum_near_kernel, at, sources, (near_down, near_up), "sum_near"
    )
    near_below, near_above, left = lax.optimization_barrier((near_below, near_above, left))
    picked = pick_columns(active_table, left)
    own = sum_own(at, dst, src, count, sources, tiles_all)
    parts = [
        routed(far_above, lambda core: 2),
        routed(far_below, lambda core: -2),
        routed(near_above, lambda core: 1),
        routed(near_below, lambda core: -1),
    ]
    joined = join(picked, own, parts, right)
    spread = lax.all_to_all(joined, "cset", split_axis=0, concat_axis=0, tiled=True)
    return spread.reshape(-1, TILE)


def solution(mesh):
    in_specs = (
        P(("blk", "cset"), None),
        P(("blk", "cset"), None),
        P("blk", "cset", None, None, None, None),
        P("blk", "cset", None, None),
        P("blk", "cset", None, None),
        P("blk", "cset", None),
        P(),
        P(),
    )
    out_specs = P("blk", "cset")
    return jax.shard_map(local, mesh=mesh, in_specs=in_specs, out_specs=out_specs, check_vma=False)
```

```python
import functools

import jax
import jax.numpy as jnp
from jax import lax
from jax.experimental import pallas as pl
from jax.experimental.pallas import tpu as pltpu
from jax.sharding import PartitionSpec as P

SPLITS = 20
OUTPAD = 1024
TILE = 128
CHUNK = 512
SLOTS = 8
PAIR = 2 * SLOTS
TAIL = 16
REACH = 9
PART_TILES = 16
VMEM_LIMIT = 16 * 1024 * 1024


def routed(block, hops):
    nb, nc = lax.axis_size("blk"), lax.axis_size("cset")
    route = []
    for b in range(nb):
        chips = hops(b % 2)
        for c in range(nc):
            target = c ^ (nc // 2) if chips % 2 else c
            route.append((b * nc + c, ((b + 2 * chips) % nb) * nc + target))
    return lax.ppermute(block, ("blk", "cset"), route)


def places(slots, dst_ref, src_ref, count_ref):
    held, rows = [], []
    for slot, parity in slots:
        for t in range(SLOTS):
            held.append(src_ref[t, slot] + parity * PART_TILES)
            rows.append(jnp.where(t < count_ref[slot], dst_ref[t, slot], 2))
    return held, rows


def pair_slots(which, core):
    first = 2 * which - core
    return [(first, 0), (first + 1, 1)]


def message_slots(core):
    return [
        pair_slots(3, core),
        pair_slots(1, core),
        [(REACH - 1, core)],
        [(0, core)],
        [(1 + (REACH - 3) * core, 1 - core)],
    ]


HOPS = [
    lambda core: 1,
    lambda core: -1,
    lambda core: 2,
    lambda core: -2,
    lambda core: 4 * core - 2,
]
LENGTHS = [PAIR, PAIR, SLOTS, SLOTS, SLOTS]


def pack_kernel(which, at_ref, dst_ref, src_ref, count_ref, tiles_ref, *rest):
    outs, sems = rest[: len(which)], rest[len(which)]
    lengths = [LENGTHS[n] for n in which]
    lane = lax.broadcasted_iota(jnp.int32, (TAIL, TILE), 1)
    line = lax.broadcasted_iota(jnp.int32, (TAIL, TILE), 0)
    slots = [message_slots(at_ref[0])[n] for n in which]
    copies = []
    for n, length in enumerate(lengths):
        begin = pl.multiple_of(slots[n][0][0] * (SLOTS * TILE), SLOTS * TILE)
        copies.append(
            pltpu.make_async_copy(
                tiles_ref.at[pl.ds(begin, length * TILE)],
                outs[n].at[pl.ds(0, length * TILE)],
                sems.at[n],
            )
        )
    for copy in copies:
        copy.start()
    for n, length in enumerate(lengths):
        held, rows = places(slots[n], dst_ref, src_ref, count_ref)
        tail = jnp.zeros((TAIL, TILE), jnp.int32)
        for t in range(length):
            tail = jnp.where(lane == t, jnp.where(line == 0, held[t], rows[t]), tail)
        outs[n][length * TILE : length * TILE + TAIL] = tail.astype(jnp.float32).astype(jnp.bfloat16)
    for copy in copies:
        copy.wait()


SMEM = pl.BlockSpec(memory_space=pltpu.SMEM)
VMEM = pl.BlockSpec(memory_space=pltpu.VMEM)
ANY = pl.BlockSpec(memory_space=pl.ANY)
HBM = pl.BlockSpec(memory_space=pltpu.HBM)


def in_space(space, *arrays):
    return [pltpu.with_memory_space_constraint(array, space) for array in arrays]


def pack_tiles(which, at, dst, src, count, tiles, name):
    shapes = [(LENGTHS[n] * TILE + TAIL, TILE) for n in which]
    return pl.pallas_call(
        functools.partial(pack_kernel, which),
        in_specs=[SMEM, SMEM, SMEM, SMEM, HBM],
        out_specs=[VMEM] * len(which),
        out_shape=[pltpu.VMEM(shape, jnp.bfloat16) for shape in shapes],
        scratch_shapes=[pltpu.SemaphoreType.DMA((len(which),))],
        compiler_params=pltpu.CompilerParams(vmem_limit_bytes=VMEM_LIMIT),
        cost_estimate=pl.CostEstimate(
            flops=0, bytes_accessed=sum(2 * rows * cols for rows, cols in shapes), transcendentals=0
        ),
        name=name,
    )(at, *in_space(pltpu.HBM, dst, src, count, tiles))


def products(held, rows, tiles, sources):
    total = None
    for t in range(0, PAIR, 2):
        sides, chosen = [], []
        for n in (t, t + 1):
            tile = tiles(n)
            empty = jnp.zeros_like(tile)
            sides.append(
                jnp.concatenate(
                    [jnp.where(rows[n] == 0, tile, empty), jnp.where(rows[n] == 1, tile, empty)], axis=0
                )
            )
            chosen.append(sources[pl.ds(pl.multiple_of(held[n] * TILE, TILE), TILE)])
        product = jnp.dot(
            jnp.concatenate(sides, axis=1),
            jnp.concatenate(chosen, axis=0),
            preferred_element_type=jnp.float32,
        )
        total = product if total is None else total + product
    return total


def read_places(messages, tail, tail_s, sem):
    lengths = [message.shape[0] // TILE for message in messages]
    for n, message in enumerate(messages):
        end = message[lengths[n] * TILE : lengths[n] * TILE + TAIL]
        tail[n] = end.astype(jnp.float32).astype(jnp.int32)
    copy = pltpu.make_async_copy(tail, tail_s, sem)
    copy.start()
    copy.wait()
    return [
        [
            (tail_s[n, 0, t], tail_s[n, 1, t], message.at[t * TILE : (t + 1) * TILE])
            for t in range(lengths[n])
        ]
        for n, message in enumerate(messages)
    ]


def write_products(out, tiles, sources):
    held, rows, refs = zip(*tiles)
    out[...] = products(held, rows, lambda n: refs[n][...], sources).astype(jnp.bfloat16)


def sum_side_kernel(core, at_ref, sources, near, far, odd, to_near, to_far, *scratch):
    near, far, odd = read_places((near, far, odd), *scratch)
    odd = [(held, jnp.where(at_ref[0] == core, row, 2), tile) for held, row, tile in odd]
    write_products(to_near, near, sources)
    write_products(to_far, far + odd, sources)


def sum_away(kernel, at, sources, messages, name):
    rows, channels = sources.shape
    return pl.pallas_call(
        kernel,
        in_specs=[SMEM] + [VMEM] * (1 + len(messages)),
        out_specs=[VMEM] * 2,
        out_shape=[pltpu.VMEM((2 * TILE, channels), jnp.bfloat16)] * 2,
        scratch_shapes=[
            pltpu.VMEM((len(messages), TAIL, TILE), jnp.int32),
            pltpu.SMEM((len(messages), TAIL, TILE), jnp.int32),
            pltpu.SemaphoreType.DMA,
        ],
        compiler_params=pltpu.CompilerParams(vmem_limit_bytes=VMEM_LIMIT),
        cost_estimate=pl.CostEstimate(
            flops=2 * 4 * TILE * TILE * PAIR * channels,
            bytes_accessed=2 * (rows * channels + 2 * PAIR * TILE * TILE),
            transcendentals=0,
        ),
        name=name,
    )(at, *in_space(pltpu.VMEM, sources, *messages))


def sum_own_kernel(at_ref, dst_ref, src_ref, count_ref, sources_ref, tiles_ref, out_ref, *rest):
    tiles, sem = rest
    slots = pair_slots(2, at_ref[0])
    held, placed = places(slots, dst_ref, src_ref, count_ref)
    begin = pl.multiple_of(slots[0][0] * (SLOTS * TILE), SLOTS * TILE)
    copy = pltpu.make_async_copy(tiles_ref.at[pl.ds(begin, PAIR * TILE)], tiles, sem)
    copy.start()
    copy.wait()
    out_ref[...] = products(held, placed, lambda n: tiles[n * TILE : (n + 1) * TILE], sources_ref)


def sum_own(at, dst, src, count, sources, tiles):
    rows, channels = sources.shape
    return pl.pallas_call(
        sum_own_kernel,
        in_specs=[SMEM] * 4 + [VMEM] + [HBM],
        out_specs=VMEM,
        out_shape=jax.ShapeDtypeStruct((2 * TILE, channels), jnp.float32),
        scratch_shapes=[
            pltpu.VMEM((PAIR * TILE, TILE), jnp.bfloat16),
            pltpu.SemaphoreType.DMA,
        ],
        compiler_params=pltpu.CompilerParams(vmem_limit_bytes=VMEM_LIMIT),
        cost_estimate=pl.CostEstimate(
            flops=4 * TILE * TILE * PAIR * channels,
            bytes_accessed=2 * (rows * channels + PAIR * TILE * TILE),
            transcendentals=0,
        ),
        name="sum_own",
    )(
        at,
        dst,
        src,
        count,
        *in_space(pltpu.VMEM, sources),
        tiles,
    )


def onehot(columns, channels):
    shape = (channels, columns.shape[1])
    channel = lax.broadcasted_iota(jnp.int32, shape, 0).astype(jnp.float32).astype(jnp.bfloat16)
    one, zero = jnp.ones(shape, jnp.bfloat16), jnp.zeros(shape, jnp.bfloat16)
    return jnp.where(channel == columns, one, zero)


def columns_kernel(left_ref, right_ref, left_out, right_out):
    for ref, out in ((left_ref, left_out), (right_ref, right_out)):
        out[...] = jnp.full(out.shape, -1, jnp.bfloat16)
        for j in range(SPLITS):
            row = ref[j : j + 1].astype(jnp.float32).astype(jnp.bfloat16)
            out[j, :, : ref.shape[1]] = row


def as_columns(left, right):
    return pl.pallas_call(
        columns_kernel,
        in_specs=[VMEM] * 2,
        out_specs=[VMEM] * 2,
        out_shape=[pltpu.VMEM((SPLITS, 1, OUTPAD), jnp.bfloat16)] * 2,
        compiler_params=pltpu.CompilerParams(vmem_limit_bytes=VMEM_LIMIT),
        cost_estimate=pl.CostEstimate(flops=10000000000, bytes_accessed=1, transcendentals=0),
        name="as_columns",
    )(left, right)


def pick_kernel(columns_ref, table_ref, out_ref):
    table = table_ref[...]
    for j in range(SPLITS):
        for begin in range(0, out_ref.shape[2], CHUNK):
            part = slice(begin, begin + CHUNK)
            picked = jnp.dot(
                table,
                onehot(columns_ref[j, :, part], table.shape[1]),
                preferred_element_type=jnp.float32,
            )
            out_ref[j, :, part] = picked.astype(jnp.bfloat16)


def pick_columns(table, columns):
    rows, channels = table.shape
    splits, _, width = columns.shape
    return pl.pallas_call(
        pick_kernel,
        in_specs=[VMEM] * 2,
        out_specs=VMEM,
        out_shape=pltpu.VMEM((splits, rows, width), jnp.bfloat16),
        compiler_params=pltpu.CompilerParams(vmem_limit_bytes=VMEM_LIMIT),
        cost_estimate=pl.CostEstimate(
            flops=2 * splits * rows * channels * width,
            bytes_accessed=2 * splits * rows * width,
            transcendentals=0,
        ),
        name="pick_active",
    )(columns, table)


def join_kernel(columns_ref, picked_ref, own_ref, n0, n1, n2, n3, out_ref):
    total = own_ref[...]
    for part in (n0, n1, n2, n3):
        total = total + part[...].astype(jnp.float32)
    neighbour = total.astype(jnp.bfloat16)
    rows, channels = neighbour.shape
    for begin in range(0, picked_ref.shape[2], CHUNK):
        part = slice(begin, begin + CHUNK)
        joined = jnp.zeros((rows, CHUNK), jnp.float32)
        for j in range(SPLITS):
            joined = joined + picked_ref[j, :, part].astype(jnp.float32) * jnp.dot(
                neighbour,
                onehot(columns_ref[j, :, part], channels),
                preferred_element_type=jnp.float32,
            )
        for piece in range(CHUNK // TILE):
            out_ref[begin // TILE + piece] = joined[:, piece * TILE : (piece + 1) * TILE].astype(
                out_ref.dtype
            )


def join(picked, own, parts, columns):
    splits, rows, width = picked.shape
    channels = own.shape[1]
    return pl.pallas_call(
        join_kernel,
        in_specs=[VMEM] * 7,
        out_specs=VMEM,
        out_shape=pltpu.VMEM((width // TILE, rows, TILE), jnp.bfloat16),
        compiler_params=pltpu.CompilerParams(vmem_limit_bytes=VMEM_LIMIT),
        cost_estimate=pl.CostEstimate(
            flops=2 * splits * rows * channels * width,
            bytes_accessed=2 * rows * width,
            transcendentals=0,
        ),
        name="join_sets",
    )(columns, *in_space(pltpu.VMEM, picked, own, *parts))


def local(
    active_table,
    passive_table,
    adjacency,
    tile_dst,
    tile_src,
    tile_count,
    split_active,
    split_passive,
):
    tiles_all = adjacency.reshape(-1, TILE)
    dst, src, count = tile_dst[0, 0].T, tile_src[0, 0].T, tile_count[0, 0]
    nc = lax.axis_size("cset")
    at = (lax.axis_index("blk") % 2).astype(jnp.int32)[None]

    up, down = pack_tiles((0, 1), at, dst, src, count, tiles_all, "pack_near")
    up, down, passive_table = lax.optimization_barrier((up, down, passive_table))
    left, right = as_columns(split_active, split_passive)
    left, later, down = lax.optimization_barrier((left, at, down))
    far = pack_tiles((2, 3, 4), later, dst, src, count, tiles_all, "pack_far")
    messages = [routed(message, hops) for message, hops in zip((up, down, *far), HOPS)]
    copies = jnp.broadcast_to(passive_table[None], (nc,) + passive_table.shape)
    own_rows = lax.all_to_all(copies, "cset", split_axis=0, concat_axis=0, tiled=True)
    own_rows = own_rows.reshape(-1, passive_table.shape[1])
    groups = [[b, b + 1] for b in range(0, lax.axis_size("blk"), 2)]
    twice = jnp.broadcast_to(own_rows[None], (2,) + own_rows.shape)
    sources = lax.all_to_all(
        twice, "blk", split_axis=0, concat_axis=0, tiled=True, axis_index_groups=groups
    ).reshape(-1, own_rows.shape[1])

    sources, left, right = lax.optimization_barrier((sources, left, right))
    near_up, near_down, far_up, far_down, odd = messages
    near_below, far_below = sum_away(
        functools.partial(sum_side_kernel, 1), at, sources, (near_up, far_up, odd), "sum_below"
    )
    near_below, far_below, sources = lax.optimization_barrier((near_below, far_below, sources))
    near_above, far_above = sum_away(
        functools.partial(sum_side_kernel, 0), at, sources, (near_down, far_down, odd), "sum_above"
    )
    near_above, far_above, left = lax.optimization_barrier((near_above, far_above, left))
    picked = pick_columns(active_table, left)
    own = sum_own(at, dst, src, count, sources, tiles_all)
    parts = [
        routed(near_above, lambda core: 1),
        routed(far_above, lambda core: 2),
        routed(near_below, lambda core: -1),
        routed(far_below, lambda core: -2),
    ]
    joined = join(picked, own, parts, right)
    spread = lax.all_to_all(joined, "cset", split_axis=0, concat_axis=0, tiled=True)
    return spread.reshape(-1, TILE)


def solution(mesh):
    in_specs = (
        P(("blk", "cset"), None),
        P(("blk", "cset"), None),
        P("blk", "cset", None, None, None, None),
        P("blk", "cset", None, None),
        P("blk", "cset", None, None),
        P("blk", "cset", None),
        P(),
        P(),
    )
    out_specs = P("blk", "cset")
    return jax.shard_map(local, mesh=mesh, in_specs=in_specs, out_specs=out_specs, check_vma=False)
```

```python
import functools

import jax
import jax.numpy as jnp
from jax import lax
from jax.experimental import pallas as pl
from jax.experimental.pallas import tpu as pltpu
from jax.sharding import PartitionSpec as P

SPLITS = 20
OUTPAD = 1024
TILE = 128
CHUNK = 1024
SLOTS = 8
PAIR = 2 * SLOTS
TAIL = 16
REACH = 9
PART_TILES = 16
VMEM_LIMIT = 16 * 1024 * 1024


def routed(block, hops):
    nb, nc = lax.axis_size("blk"), lax.axis_size("cset")
    route = []
    for b in range(nb):
        chips = hops(b % 2)
        for c in range(nc):
            target = c ^ (nc // 2) if chips % 2 else c
            route.append((b * nc + c, ((b + 2 * chips) % nb) * nc + target))
    return lax.ppermute(block, ("blk", "cset"), route)


def places(slots, dst_ref, src_ref, count_ref):
    held, rows = [], []
    for slot, parity in slots:
        for t in range(SLOTS):
            held.append(src_ref[t, slot] + parity * PART_TILES)
            rows.append(jnp.where(t < count_ref[slot], dst_ref[t, slot], 2))
    return held, rows


def pair_slots(which, core):
    first = 2 * which - core
    return [(first, 0), (first + 1, 1)]


def message_slots(core):
    return [
        pair_slots(3, core),
        pair_slots(1, core),
        [(REACH - 1, core)],
        [(0, core)],
        [(1 + (REACH - 3) * core, 1 - core)],
    ]


HOPS = [
    lambda core: 1,
    lambda core: -1,
    lambda core: 2,
    lambda core: -2,
    lambda core: 4 * core - 2,
]
LENGTHS = [PAIR, PAIR, SLOTS, SLOTS, SLOTS]


def pack_kernel(which, at_ref, dst_ref, src_ref, count_ref, tiles_ref, *rest):
    outs, sems = rest[: len(which)], rest[len(which)]
    lengths = [LENGTHS[n] for n in which]
    lane = lax.broadcasted_iota(jnp.int32, (TAIL, TILE), 1)
    line = lax.broadcasted_iota(jnp.int32, (TAIL, TILE), 0)
    slots = [message_slots(at_ref[0])[n] for n in which]
    copies = []
    for n, length in enumerate(lengths):
        begin = pl.multiple_of(slots[n][0][0] * (SLOTS * TILE), SLOTS * TILE)
        copies.append(
            pltpu.make_async_copy(
                tiles_ref.at[pl.ds(begin, length * TILE)],
                outs[n].at[pl.ds(0, length * TILE)],
                sems.at[n],
            )
        )
    for copy in copies:
        copy.start()
    for n, length in enumerate(lengths):
        held, rows = places(slots[n], dst_ref, src_ref, count_ref)
        tail = jnp.zeros((TAIL, TILE), jnp.int32)
        for t in range(length):
            tail = jnp.where(lane == t, jnp.where(line == 0, held[t], rows[t]), tail)
        outs[n][length * TILE : length * TILE + TAIL] = tail.astype(jnp.float32).astype(jnp.bfloat16)
    for copy in copies:
        copy.wait()


SMEM = pl.BlockSpec(memory_space=pltpu.SMEM)
VMEM = pl.BlockSpec(memory_space=pltpu.VMEM)
ANY = pl.BlockSpec(memory_space=pl.ANY)
HBM = pl.BlockSpec(memory_space=pltpu.HBM)


def in_space(space, *arrays):
    return [pltpu.with_memory_space_constraint(array, space) for array in arrays]


def pack_tiles(which, at, dst, src, count, tiles, name):
    shapes = [(LENGTHS[n] * TILE + TAIL, TILE) for n in which]
    return pl.pallas_call(
        functools.partial(pack_kernel, which),
        in_specs=[SMEM, SMEM, SMEM, SMEM, HBM],
        out_specs=[VMEM] * len(which),
        out_shape=[pltpu.VMEM(shape, jnp.bfloat16) for shape in shapes],
        scratch_shapes=[pltpu.SemaphoreType.DMA((len(which),))],
        compiler_params=pltpu.CompilerParams(vmem_limit_bytes=VMEM_LIMIT),
        cost_estimate=pl.CostEstimate(
            flops=0, bytes_accessed=sum(2 * rows * cols for rows, cols in shapes), transcendentals=0
        ),
        name=name,
    )(at, *in_space(pltpu.HBM, dst, src, count, tiles))


def products(held, rows, tiles, sources):
    total = None
    for t in range(0, PAIR, 2):
        sides, chosen = [], []
        for n in (t, t + 1):
            tile = tiles(n)
            empty = jnp.zeros_like(tile)
            sides.append(
                jnp.concatenate(
                    [jnp.where(rows[n] == 0, tile, empty), jnp.where(rows[n] == 1, tile, empty)], axis=0
                )
            )
            chosen.append(sources[pl.ds(pl.multiple_of(held[n] * TILE, TILE), TILE)])
        product = jnp.dot(
            jnp.concatenate(sides, axis=1),
            jnp.concatenate(chosen, axis=0),
            preferred_element_type=jnp.float32,
        )
        total = product if total is None else total + product
    return total


def read_places(messages, tail, tail_s, sem):
    lengths = [message.shape[0] // TILE for message in messages]
    for n, message in enumerate(messages):
        end = message[lengths[n] * TILE : lengths[n] * TILE + TAIL]
        tail[n] = end.astype(jnp.float32).astype(jnp.int32)
    copy = pltpu.make_async_copy(tail, tail_s, sem)
    copy.start()
    copy.wait()
    return [
        [
            (tail_s[n, 0, t], tail_s[n, 1, t], message.at[t * TILE : (t + 1) * TILE])
            for t in range(lengths[n])
        ]
        for n, message in enumerate(messages)
    ]


def write_products(out, tiles, sources):
    held, rows, refs = zip(*tiles)
    out[...] = products(held, rows, lambda n: refs[n][...], sources).astype(jnp.bfloat16)


def sum_side_kernel(core, at_ref, sources, near, far, odd, to_near, to_far, *scratch):
    near, far, odd = read_places((near, far, odd), *scratch)
    odd = [(held, jnp.where(at_ref[0] == core, row, 2), tile) for held, row, tile in odd]
    write_products(to_near, near, sources)
    write_products(to_far, far + odd, sources)


def sum_away(kernel, at, sources, messages, name):
    rows, channels = sources.shape
    return pl.pallas_call(
        kernel,
        in_specs=[SMEM] + [VMEM] * (1 + len(messages)),
        out_specs=[VMEM] * 2,
        out_shape=[pltpu.VMEM((2 * TILE, channels), jnp.bfloat16)] * 2,
        scratch_shapes=[
            pltpu.VMEM((len(messages), TAIL, TILE), jnp.int32),
            pltpu.SMEM((len(messages), TAIL, TILE), jnp.int32),
            pltpu.SemaphoreType.DMA,
        ],
        compiler_params=pltpu.CompilerParams(vmem_limit_bytes=VMEM_LIMIT),
        cost_estimate=pl.CostEstimate(
            flops=2 * 4 * TILE * TILE * PAIR * channels,
            bytes_accessed=2 * (rows * channels + 2 * PAIR * TILE * TILE),
            transcendentals=0,
        ),
        name=name,
    )(at, *in_space(pltpu.VMEM, sources, *messages))


def sum_own_kernel(at_ref, dst_ref, src_ref, count_ref, sources_ref, tiles_ref, out_ref, *rest):
    tiles, sem = rest
    slots = pair_slots(2, at_ref[0])
    held, placed = places(slots, dst_ref, src_ref, count_ref)
    begin = pl.multiple_of(slots[0][0] * (SLOTS * TILE), SLOTS * TILE)
    copy = pltpu.make_async_copy(tiles_ref.at[pl.ds(begin, PAIR * TILE)], tiles, sem)
    copy.start()
    copy.wait()
    out_ref[...] = products(held, placed, lambda n: tiles[n * TILE : (n + 1) * TILE], sources_ref)


def sum_own(at, dst, src, count, sources, tiles):
    rows, channels = sources.shape
    return pl.pallas_call(
        sum_own_kernel,
        in_specs=[SMEM] * 4 + [VMEM] + [HBM],
        out_specs=VMEM,
        out_shape=jax.ShapeDtypeStruct((2 * TILE, channels), jnp.float32),
        scratch_shapes=[
            pltpu.VMEM((PAIR * TILE, TILE), jnp.bfloat16),
            pltpu.SemaphoreType.DMA,
        ],
        compiler_params=pltpu.CompilerParams(vmem_limit_bytes=VMEM_LIMIT),
        cost_estimate=pl.CostEstimate(
            flops=4 * TILE * TILE * PAIR * channels,
            bytes_accessed=2 * (rows * channels + PAIR * TILE * TILE),
            transcendentals=0,
        ),
        name="sum_own",
    )(
        at,
        dst,
        src,
        count,
        *in_space(pltpu.VMEM, sources),
        tiles,
    )


def onehot(columns, channels):
    shape = (channels, columns.shape[1])
    channel = lax.broadcasted_iota(jnp.int32, shape, 0).astype(jnp.float32).astype(jnp.bfloat16)
    one, zero = jnp.ones(shape, jnp.bfloat16), jnp.zeros(shape, jnp.bfloat16)
    return jnp.where(channel == columns, one, zero)


def columns_kernel(left_ref, right_ref, left_out, right_out):
    for ref, out in ((left_ref, left_out), (right_ref, right_out)):
        out[...] = jnp.full(out.shape, -1, jnp.bfloat16)
        for j in range(SPLITS):
            row = ref[j : j + 1].astype(jnp.float32).astype(jnp.bfloat16)
            out[j, :, : ref.shape[1]] = row


def as_columns(left, right):
    return pl.pallas_call(
        columns_kernel,
        in_specs=[VMEM] * 2,
        out_specs=[VMEM] * 2,
        out_shape=[pltpu.VMEM((SPLITS, 1, OUTPAD), jnp.bfloat16)] * 2,
        compiler_params=pltpu.CompilerParams(vmem_limit_bytes=VMEM_LIMIT),
        cost_estimate=pl.CostEstimate(flops=10000000000, bytes_accessed=1, transcendentals=0),
        name="as_columns",
    )(left, right)


def pick_kernel(columns_ref, table_ref, out_ref):
    table = table_ref[...]
    for j in range(SPLITS):
        for begin in range(0, out_ref.shape[2], CHUNK):
            part = slice(begin, begin + CHUNK)
            picked = jnp.dot(
                table,
                onehot(columns_ref[j, :, part], table.shape[1]),
                preferred_element_type=jnp.float32,
            )
            out_ref[j, :, part] = picked.astype(jnp.bfloat16)


def pick_columns(table, columns):
    rows, channels = table.shape
    splits, _, width = columns.shape
    return pl.pallas_call(
        pick_kernel,
        in_specs=[VMEM] * 2,
        out_specs=VMEM,
        out_shape=pltpu.VMEM((splits, rows, width), jnp.bfloat16),
        compiler_params=pltpu.CompilerParams(vmem_limit_bytes=VMEM_LIMIT),
        cost_estimate=pl.CostEstimate(
            flops=2 * splits * rows * channels * width,
            bytes_accessed=2 * splits * rows * width,
            transcendentals=0,
        ),
        name="pick_active",
    )(columns, table)


def join_kernel(columns_ref, picked_ref, own_ref, n0, n1, n2, n3, out_ref):
    total = own_ref[...]
    for part in (n0, n1, n2, n3):
        total = total + part[...].astype(jnp.float32)
    neighbour = total.astype(jnp.bfloat16)
    rows, channels = neighbour.shape
    for begin in range(0, picked_ref.shape[2], CHUNK):
        part = slice(begin, begin + CHUNK)
        joined = jnp.zeros((rows, CHUNK), jnp.float32)
        for j in range(SPLITS):
            joined = joined + picked_ref[j, :, part].astype(jnp.float32) * jnp.dot(
                neighbour,
                onehot(columns_ref[j, :, part], channels),
                preferred_element_type=jnp.float32,
            )
        for piece in range(CHUNK // TILE):
            out_ref[begin // TILE + piece] = joined[:, piece * TILE : (piece + 1) * TILE].astype(
                out_ref.dtype
            )


def join(picked, own, parts, columns):
    splits, rows, width = picked.shape
    channels = own.shape[1]
    return pl.pallas_call(
        join_kernel,
        in_specs=[VMEM] * 7,
        out_specs=VMEM,
        out_shape=pltpu.VMEM((width // TILE, rows, TILE), jnp.bfloat16),
        compiler_params=pltpu.CompilerParams(vmem_limit_bytes=VMEM_LIMIT),
        cost_estimate=pl.CostEstimate(
            flops=2 * splits * rows * channels * width,
            bytes_accessed=2 * rows * width,
            transcendentals=0,
        ),
        name="join_sets",
    )(columns, *in_space(pltpu.VMEM, picked, own, *parts))


def local(
    active_table,
    passive_table,
    adjacency,
    tile_dst,
    tile_src,
    tile_count,
    split_active,
    split_passive,
):
    tiles_all = adjacency.reshape(-1, TILE)
    dst, src, count = tile_dst[0, 0].T, tile_src[0, 0].T, tile_count[0, 0]
    nc = lax.axis_size("cset")
    at = (lax.axis_index("blk") % 2).astype(jnp.int32)[None]

    up, down = pack_tiles((0, 1), at, dst, src, count, tiles_all, "pack_near")
    up, down, passive_table = lax.optimization_barrier((up, down, passive_table))
    left, right = as_columns(split_active, split_passive)
    left, later, down = lax.optimization_barrier((left, at, down))
    far = pack_tiles((2, 3, 4), later, dst, src, count, tiles_all, "pack_far")
    messages = [routed(message, hops) for message, hops in zip((up, down, *far), HOPS)]
    copies = jnp.broadcast_to(passive_table[None], (nc,) + passive_table.shape)
    own_rows = lax.all_to_all(copies, "cset", split_axis=0, concat_axis=0, tiled=True)
    own_rows = own_rows.reshape(-1, passive_table.shape[1])
    groups = [[b, b + 1] for b in range(0, lax.axis_size("blk"), 2)]
    twice = jnp.broadcast_to(own_rows[None], (2,) + own_rows.shape)
    sources = lax.all_to_all(
        twice, "blk", split_axis=0, concat_axis=0, tiled=True, axis_index_groups=groups
    ).reshape(-1, own_rows.shape[1])

    sources, left, right = lax.optimization_barrier((sources, left, right))
    near_up, near_down, far_up, far_down, odd = messages
    near_below, far_below = sum_away(
        functools.partial(sum_side_kernel, 1), at, sources, (near_up, far_up, odd), "sum_below"
    )
    near_below, far_below, sources = lax.optimization_barrier((near_below, far_below, sources))
    near_above, far_above = sum_away(
        functools.partial(sum_side_kernel, 0), at, sources, (near_down, far_down, odd), "sum_above"
    )
    near_above, far_above, left = lax.optimization_barrier((near_above, far_above, left))
    picked = pick_columns(active_table, left)
    own = sum_own(at, dst, src, count, sources, tiles_all)
    parts = [
        routed(near_above, lambda core: 1),
        routed(far_above, lambda core: 2),
        routed(near_below, lambda core: -1),
        routed(far_below, lambda core: -2),
    ]
    joined = join(picked, own, parts, right)
    spread = lax.all_to_all(joined, "cset", split_axis=0, concat_axis=0, tiled=True)
    return spread.reshape(-1, TILE)


def solution(mesh):
    in_specs = (
        P(("blk", "cset"), None),
        P(("blk", "cset"), None),
        P("blk", "cset", None, None, None, None),
        P("blk", "cset", None, None),
        P("blk", "cset", None, None),
        P("blk", "cset", None),
        P(),
        P(),
    )
    out_specs = P("blk", "cset")
    return jax.shard_map(local, mesh=mesh, in_specs=in_specs, out_specs=out_specs, check_vma=False)
```
